32 devices in a mesh: slab: 8 (over z, x), tile: 4 (over y, core).
Axes of the slice: x: 2, y: 2, z: 4, core: 2. Of those that a mesh axis runs over, the one named last changes fastest.
Arguments:
- particles: float32 [1024, 16, 128], P(('slab', 'tile')), may hold values from -6 to 6, as said below
- dest_slot: int32 [1024], P(('slab', 'tile')), may hold values from 0 to 31, as said below
- neighbours: int32 [1024, 4], P(('slab', 'tile')), may hold values from 0 to 95, as said below
- counts: int32 [1024], P(('slab', 'tile')), may hold values from 1 to 4, as said below
Outputs:
- updated: float32 [1024, 16, 128], P(('slab', 'tile'))
- derived: float32 [1024, 5, 128], P(('slab', 'tile'))
The draws below stay inside these ranges and needn't reach their ends.
Inputs may be any that keep to these rules, and one draw needn't show every extreme that they name: `dest_slot`: A bin on device (s, t) with value d goes to tile d // 8 of slab s. The values of one device are distinct, so at most 8 of its bins go to one owner; in every slab some owner receives 8 bins from every device of the slab. `neighbours`: entries index the 96 candidates of the slot's device: first the slab on the lower side (periodic), then the device's own slots, then the higher side. Entry 0 is the slot itself; the entries of a row are distinct. `counts`: every device has a slot that uses all 4 entries. `particles`: positions lie in 0 to 2, masses in 0.5 / 512 to 2 / 512, energies in 0.5 to 4, smoothing lengths in 0.6 to 1; velocities and carried quantities lie within -6 to 6.
All inputs are finite; a program needn't handle non-finite values.
Results may differ from the reference program's by a relative error of at most 0.0003.
Values sent between devices are 32-bit elements; how exact they have to be, the bound alone decides.
No kernel may reach another device: no remote copies, remote signals or barrier semaphores. Data moves between devices by JAX's collectives and lax.ppermute only.
A program may use at most 64 MiB of HBM per device.

```python
import math
import jax
import jax.numpy as jnp
from jax import lax

PARTICLE_FLOATS = 16
BIN_PARTICLES = 128
B_DEV = 32
NEIGHBOUR_COUNT = 4
OUTBOX_CELL_CAP = 8
PLACES_PER_CHIP = 32
NBINS = 1024
SLOT_COUNT = 1024
N_SLAB = 8
N_TILE = 4


def draw_particles(key, part):
    keys = jax.random.split(key, 6)
    place = jax.random.uniform(keys[0], (NBINS, 3, BIN_PARTICLES), minval=0.0, maxval=2.0)
    speed = jnp.clip(0.3 * jax.random.normal(keys[1], (NBINS, 3, BIN_PARTICLES)), -6.0, 6.0)
    masses = jnp.exp(jax.random.uniform(keys[2], (NBINS, BIN_PARTICLES), minval=math.log(0.5), maxval=math.log(2.0))) / (NEIGHBOUR_COUNT * BIN_PARTICLES)
    energy = jnp.exp(jax.random.uniform(keys[3], (NBINS, BIN_PARTICLES), minval=math.log(0.5), maxval=math.log(4.0)))
    smooth = jax.random.uniform(keys[4], (NBINS, BIN_PARTICLES), minval=0.6, maxval=1.0)
    carried = jnp.clip(jax.random.normal(keys[5], (NBINS, PARTICLE_FLOATS - 9, BIN_PARTICLES)), -6.0, 6.0)
    joined = jnp.concatenate([place, speed, masses[:, None], energy[:, None], smooth[:, None], carried], axis=1)
    return joined.astype(jnp.float32)


def draw_dest_slot(key, part):
    keys = jax.random.split(jax.random.fold_in(key, 11), 2)
    busiest_cells = jax.random.randint(keys[0], (N_SLAB,), 0, N_TILE)
    place_position = jnp.arange(PLACES_PER_CHIP, dtype=jnp.int32)
    cell_ranking = jax.random.randint(keys[1], (N_SLAB, N_TILE, PLACES_PER_CHIP), 0, 2 ** 20)
    added_reward = jnp.where(place_position[None, None, :] // OUTBOX_CELL_CAP == busiest_cells[:, None, None], 2 ** 21, 0)
    overall_number = (cell_ranking + added_reward) * PLACES_PER_CHIP + place_position[None, None, :]
    picked = lax.top_k(overall_number, B_DEV)[1].astype(jnp.int32)
    return picked.reshape((NBINS,))


def draw_neighbours(key, part):
    kernel_width = 3 * PLACES_PER_CHIP
    column_index = jnp.arange(kernel_width, dtype=jnp.int32)
    cell_ranking = jax.random.randint(jax.random.fold_in(key, 23), (SLOT_COUNT, kernel_width), 0, 2 ** 20) * kernel_width + column_index[None, :]
    self_term = PLACES_PER_CHIP + jnp.arange(SLOT_COUNT, dtype=jnp.int32) % PLACES_PER_CHIP
    cell_ranking = jnp.where(column_index[None, :] == self_term[:, None], -1, cell_ranking)
    others = lax.top_k(cell_ranking, NEIGHBOUR_COUNT - 1)[1].astype(jnp.int32)
    return jnp.concatenate([self_term[:, None], others], axis=1)


def draw_counts(key, part):
    sampled_rows = jax.random.randint(jax.random.fold_in(key, 37), (SLOT_COUNT,), 1, NEIGHBOUR_COUNT + 1)
    particle_rows = jnp.arange(SLOT_COUNT, dtype=jnp.int32)
    return jnp.where(particle_rows % PLACES_PER_CHIP == 0, NEIGHBOUR_COUNT, sampled_rows).astype(jnp.int32)


def setup_inputs(seed: int = 0) -> dict:
    seeds = jax.random.split(jax.random.key(seed), 5)
    particles = draw_particles(jax.random.fold_in(seeds[4], 71), 0)
    dest_slot = draw_dest_slot(jax.random.fold_in(seeds[4], 71), 0)
    neighbours = draw_neighbours(jax.random.fold_in(seeds[4], 71), 0)
    counts = draw_counts(jax.random.fold_in(seeds[4], 71), 0)
    return dict(particles=particles, dest_slot=dest_slot, neighbours=neighbours, counts=counts)


ADIABATIC = 5.0 / 3.0
TIMESTEP = 0.5
KERNEL_NORM = 21.0 / (16.0 * math.pi)

def pair_terms(near_place, near_width, far_place, far_width):
    offset = near_place[:, :, None] - far_place[:, None, :]
    spacing = jnp.sqrt(lax.optimization_barrier(jnp.sum(offset * offset, axis=0)))
    blended = 0.5 * (near_width[:, None] + far_width[None, :])
    ratio = spacing / blended
    remain = jnp.maximum(1.0 - 0.5 * ratio, 0.0)
    scaled = KERNEL_NORM / (blended * blended * blended)
    cubed = remain * remain * remain
    weight = scaled * cubed * remain * (1.0 + 2.0 * ratio)
    slope = -5.0 * scaled / (blended * blended) * cubed
    return (weight, slope, offset)

def slot_density(self_place, self_width, chosen, entries, pool_place, pool_mass, pool_width):
    active = (jnp.arange(chosen.shape[0]) < entries).astype(jnp.float32)
    weight, slope, offset = jax.vmap(pair_terms, in_axes=(None, None, 0, 0))(self_place, self_width, pool_place[chosen], pool_width[chosen])
    return lax.optimization_barrier(jnp.sum(weight * (pool_mass[chosen] * active[:, None])[:, None, :], axis=(0, 2)))

def slot_force(self_place, self_width, self_speed, self_ratio, chosen, entries, pool_place, pool_mass, pool_width, pool_speed, pool_ratio):
    active = (jnp.arange(chosen.shape[0]) < entries).astype(jnp.float32)
    weight, slope, offset = jax.vmap(pair_terms, in_axes=(None, None, 0, 0))(self_place, self_width, pool_place[chosen], pool_width[chosen])
    factor = (pool_mass[chosen] * active[:, None])[:, None, :] * slope
    pairing = factor * (self_ratio[None, :, None] + pool_ratio[chosen][:, None, :])
    accel = -lax.optimization_barrier(jnp.sum(pairing[:, None] * offset, axis=(0, 3)))
    relative = self_speed[None, :, :, None] - pool_speed[chosen][:, :, None, :]
    closing = lax.optimization_barrier(jnp.sum(relative * offset, axis=1))
    heating = self_ratio * lax.optimization_barrier(jnp.sum(factor * closing, axis=(0, 2)))
    return jnp.concatenate([accel, heating[None]], axis=0)

def over_slots(worker, per_slot, shared):
    overall_number = per_slot[0].shape[0]
    blocks = tuple((member.reshape((overall_number // 8, 8) + member.shape[1:]) for member in per_slot))

    def run(block):
        return jax.vmap(lambda *single: worker(*single, *shared))(*block)
    result = lax.map(run, blocks)
    return result.reshape((overall_number,) + result.shape[2:])

def density_pass(self_place, self_width, chosen, entries, pool_place, pool_mass, pool_width):
    return over_slots(slot_density, (self_place, self_width, chosen, entries), (pool_place, pool_mass, pool_width))

def force_pass(self_place, self_width, self_speed, self_ratio, chosen, entries, pool_place, pool_mass, pool_width, pool_speed, pool_ratio):
    return over_slots(slot_force, (self_place, self_width, self_speed, self_ratio, chosen, entries), (pool_place, pool_mass, pool_width, pool_speed, pool_ratio))

def pressure_of(local_density, energy):
    return (ADIABATIC - 1.0) * local_density * energy

def final_state(particle_states, local_density, change_rates):
    present = (particle_states[:, 6] > 0).astype(jnp.float32)
    speed = particle_states[:, 3:6] + TIMESTEP * change_rates[:, 0:3]
    place = particle_states[:, 0:3] + TIMESTEP * speed
    heat = particle_states[:, 7:8] + TIMESTEP * change_rates[:, 3:4]
    updated = jnp.concatenate([place, speed, particle_states[:, 6:7], heat, particle_states[:, 8:]], axis=1) * present[:, None, :]
    derived = jnp.concatenate([local_density[:, None], change_rates], axis=1) * present[:, None, :]
    return (updated, derived)

def surround(field):
    return jnp.concatenate([jnp.roll(field, 1, axis=0), field, jnp.roll(field, -1, axis=0)], axis=2)

def reference(particles, dest_slot, neighbours, counts):
    device_total = N_SLAB * N_TILE
    source = jnp.arange(NBINS, dtype=jnp.int32) // B_DEV
    source_slab = source // N_TILE
    source_tile = source % N_TILE
    target_owner = (source_slab * N_TILE + dest_slot // OUTBOX_CELL_CAP) * PLACES_PER_CHIP + source_tile * OUTBOX_CELL_CAP + dest_slot % OUTBOX_CELL_CAP
    particle_states = jnp.zeros((SLOT_COUNT, PARTICLE_FLOATS, BIN_PARTICLES), jnp.float32).at[target_owner].set(particles)
    layout = (N_SLAB, N_TILE, PLACES_PER_CHIP)
    grid = particle_states.reshape(layout + (PARTICLE_FLOATS, BIN_PARTICLES))
    masses = grid[:, :, :, 6]
    present = masses > 0
    smooth = jnp.where(present, grid[:, :, :, 8], 1.0)
    energy = grid[:, :, :, 7]
    pool_place = surround(grid[:, :, :, 0:3]).reshape((device_total, 3 * PLACES_PER_CHIP, 3, BIN_PARTICLES))
    pool_mass = surround(masses).reshape((device_total, 3 * PLACES_PER_CHIP, BIN_PARTICLES))
    pool_width = surround(smooth).reshape((device_total, 3 * PLACES_PER_CHIP, BIN_PARTICLES))
    pool_speed = surround(grid[:, :, :, 3:6]).reshape((device_total, 3 * PLACES_PER_CHIP, 3, BIN_PARTICLES))
    chosen = neighbours.reshape((device_total, PLACES_PER_CHIP, NEIGHBOUR_COUNT))
    entries = counts.reshape((device_total, PLACES_PER_CHIP))
    self_place = grid[:, :, :, 0:3].reshape((device_total, PLACES_PER_CHIP, 3, BIN_PARTICLES))
    self_width = smooth.reshape((device_total, PLACES_PER_CHIP, BIN_PARTICLES))
    self_speed = grid[:, :, :, 3:6].reshape((device_total, PLACES_PER_CHIP, 3, BIN_PARTICLES))
    local_density = lax.map(lambda pieces: density_pass(*pieces), (self_place, self_width, chosen, entries, pool_place, pool_mass, pool_width))
    local_density = local_density.reshape(layout + (BIN_PARTICLES,))
    pressure = pressure_of(local_density, energy)
    self_ratio = (pressure / jnp.square(jnp.where(present, local_density, 1.0))).reshape((device_total, PLACES_PER_CHIP, BIN_PARTICLES))
    pool_ratio = surround(pressure) / jnp.square(jnp.where(surround(present), surround(local_density), 1.0))
    pool_ratio = pool_ratio.reshape((device_total, 3 * PLACES_PER_CHIP, BIN_PARTICLES))
    change_rates = lax.map(lambda pieces: force_pass(*pieces), (self_place, self_width, self_speed, self_ratio, chosen, entries, pool_place, pool_mass, pool_width, pool_speed, pool_ratio))
    return final_state(particle_states, local_density.reshape((SLOT_COUNT, BIN_PARTICLES)), change_rates.reshape((SLOT_COUNT, 4, BIN_PARTICLES)))
```

```python
import math

import jax
import jax.numpy as jnp
from jax import lax
from jax.experimental import pallas as pl
from jax.experimental.pallas import tpu as pltpu
from jax.sharding import PartitionSpec as P

ADIABATIC = 5.0 / 3.0
TIMESTEP = 0.5
KERNEL_NORM = 21.0 / (16.0 * math.pi)
WEIGHT_FACTOR = 8.0 * KERNEL_NORM
SLOPE_FACTOR = -5.0 * 32.0 * KERNEL_NORM
CENTRE = 1.0
LANES = 128
UNROLL = 4

F32 = jnp.float32
BF16 = jnp.bfloat16


def vmem_spec():
    return pl.BlockSpec(memory_space=pltpu.VMEM)


def smem_spec():
    return pl.BlockSpec(memory_space=pltpu.SMEM)


def kernel_call(kernel, ins, outs, scratch, flops, name):
    specs = [smem_spec() if kind == "s" else vmem_spec() for kind, _ in ins]
    arrays = [array for _, array in ins]
    moved = sum(a.size * 4 for a in arrays) + sum(math.prod(o) * 4 for o in outs)
    return pl.pallas_call(
        kernel,
        out_shape=[jax.ShapeDtypeStruct(o, F32) for o in outs],
        in_specs=specs,
        out_specs=[vmem_spec() for _ in outs],
        scratch_shapes=scratch,
        compiler_params=pltpu.CompilerParams(vmem_limit_bytes=48 * 1024 * 1024),
        cost_estimate=pl.CostEstimate(flops=flops, bytes_accessed=moved, transcendentals=0),
        name=name,
    )(*arrays)


def partner_tile(index, step, count):
    if count & (count - 1) == 0:
        return index ^ step
    return (index + step) % count


def source_tile(index, step, count):
    if count & (count - 1) == 0:
        return index ^ step
    return (index + count - step) % count


def rounded(value):
    return value.astype(BF16).astype(F32)


def row_index():
    return lax.broadcasted_iota(jnp.int32, (8, LANES), 0)


def sum_rows(tile):
    tile = tile + pltpu.roll(tile, 4, 0)
    tile = tile + pltpu.roll(tile, 2, 0)
    return tile + pltpu.roll(tile, 1, 0)


def geometry_parts(tile, row):
    hi = rounded(tile)
    lo = rounded(tile - hi)
    point = jnp.where(row < 3, hi + lo, 0.0)
    norm = sum_rows(point * point)
    n1 = rounded(norm)
    n2 = rounded(norm - n1)
    n3 = rounded(norm - n1 - n2)
    return hi, lo, n1, n2, n3


def far_features(tile, row):
    hi, lo, n1, n2, n3 = geometry_parts(tile, row)
    ones = jnp.ones_like(tile)

    def block(part):
        return jnp.where(row < 3, part, jnp.where(row < 6, pltpu.roll(part, 3, 0), jnp.where(row == 6, ones, part)))

    b0, b1 = block(hi), block(lo)
    b2 = jnp.where(row == 0, n1, jnp.where(row == 1, n2, jnp.where(row == 2, n3, jnp.where(row < 6, ones, 0.0))))
    zero = jnp.zeros_like(tile)
    low = row < 6
    left = jnp.concatenate([jnp.where(low, -2.0 * b0, 0.0), jnp.where(low, -2.0 * b1, 0.0), b2, zero], axis=0)
    right = jnp.concatenate([jnp.where(low, 0.0, b0), jnp.where(low, 0.0, b1), zero, zero], axis=0)
    return left.astype(BF16), right.astype(BF16)


def near_features(tile, row):
    hi, lo, n1, n2, n3 = geometry_parts(tile, row)
    ones = jnp.ones_like(tile)
    shifted = pltpu.roll(lo, 3, 0)

    def block(part):
        return jnp.where(row < 3, hi, jnp.where(row < 6, shifted, jnp.where(row == 6, pltpu.roll(part, 7, 0), ones)))

    b2 = jnp.where(row < 3, ones, jnp.where(row == 3, n1, jnp.where(row == 4, n2, jnp.where(row == 5, n3, 0.0))))
    stacked = jnp.concatenate([block(hi), block(lo), b2, jnp.zeros_like(tile)], axis=0)
    return jnp.transpose(stacked).astype(BF16)


def store_far(far_ref, index, tile, row):
    left, right = far_features(tile, row)
    far_ref[index, :, 0:LANES] = left
    far_ref[index, :, LANES : 2 * LANES] = right


def dummy_tile(row):
    return jnp.where(row == 7, 1.0, jnp.zeros((8, LANES), F32))


def split3(value):
    hi = rounded(value)
    mid = rounded(value - hi)
    return hi, mid, rounded(value - hi - mid)


def closeness(near, far):
    both = jnp.dot(near, far, preferred_element_type=F32)
    squared = jnp.maximum(both[:, 0:LANES], 1e-24)
    inverse = pl.reciprocal(both[:, LANES : 2 * LANES], approx=True)
    remain = jnp.maximum(1.0 - squared * lax.rsqrt(squared) * inverse, 0.0)
    scaled = inverse * remain
    return inverse, remain, scaled * scaled * scaled


def build_list(neighbours_ref, counts_ref, near_list, far_list, slots, width):
    def fill(i, total):
        used = counts_ref[i]
        for k in range(width):
            near_list[total] = i
            far_list[total] = neighbours_ref[i, k]
            total = total + (k < used).astype(jnp.int32)
        return total

    total = lax.fori_loop(0, slots, fill, jnp.int32(0))
    for k in range(UNROLL):
        near_list[total + k] = slots
        far_list[total + k] = 3 * slots
    return total


def pack_kernel(tiles, cap, dest_ref, particles_ref, *refs):
    outs, packed = refs[:-1], refs[-1]
    packed[...] = jnp.zeros_like(packed)
    me = lax.axis_index("tile")

    def place(b, carry):
        dest = dest_ref[b]
        owner = lax.div(dest, cap)
        if tiles & (tiles - 1) == 0:
            step = owner ^ me
        else:
            step = lax.rem(owner + tiles - me, tiles)
        packed[step * cap + lax.rem(dest, cap)] = particles_ref[b]
        return carry

    lax.fori_loop(0, particles_ref.shape[0], place, 0, unroll=4)
    for k in range(tiles):
        outs[k][...] = packed[k * cap : (k + 1) * cap]


def state_kernel(tiles, cap, *refs):
    parts, (states_ref, halo_ref) = refs[:tiles], refs[tiles:]
    me = lax.axis_index("tile")
    row = row_index()
    for k in range(tiles):
        base = source_tile(me, k, tiles) * cap
        for j in range(cap):
            top = parts[k][j, 0:8, :]
            low = parts[k][j, 8:16, :]
            states_ref[base + j, 0:8, :] = top
            states_ref[base + j, 8:16, :] = low
            smooth = jnp.where(pltpu.roll(top, 1, 0) > 0, pltpu.roll(low, 7, 0), 1.0)
            halo_ref[base + j] = jnp.where(row < 3, top - CENTRE, jnp.where(row == 7, smooth, top))


def region_base(region, slots):
    upper = lax.rem(lax.axis_index("slab"), 2) == 0
    first = jnp.where(upper, 2 * slots, 0)
    return first if region == 0 else 2 * slots - first


def fill_far(far_ref, own_ref, side_refs, bases, slots):
    row = row_index()
    far_ref[3 * slots, :, :] = jnp.zeros_like(far_ref[3 * slots, :, :])
    store_far(far_ref, 3 * slots, dummy_tile(row), row)

    def fill(i, carry):
        store_far(far_ref, slots + i, own_ref[i], row)
        for side_ref, base in zip(side_refs, bases):
            store_far(far_ref, base + i, side_ref[i], row)
        return carry

    lax.fori_loop(0, slots, fill, 0, unroll=2)


def fill_near(near_ref, own_ref, slots):
    row = row_index()
    near_ref[slots] = near_features(dummy_tile(row), row)

    def fill(i, carry):
        near_ref[i] = near_features(own_ref[i], row)
        return carry

    lax.fori_loop(0, slots, fill, 0, unroll=2)


def density_kernel(slots, width, neighbours_ref, counts_ref, own_ref, first_ref, second_ref, states_ref,
                   density_ref, ratio_ref, near_ref, far_ref, sum_ref, mass_ref, near_list, far_list):
    total = build_list(neighbours_ref, counts_ref, near_list, far_list, slots, width)
    bases = [region_base(r, slots) for r in range(2)]
    fill_far(far_ref, own_ref, (first_ref, second_ref), bases, slots)
    fill_near(near_ref, own_ref, slots)
    mass_ref[3 * slots] = jnp.zeros((8, LANES), F32)

    def masses(i, carry):
        for ref, base in ((own_ref, slots), (first_ref, bases[0]), (second_ref, bases[1])):
            mass_ref[base + i] = jnp.broadcast_to(ref[i, 6:7, :], (8, LANES))
        return carry

    lax.fori_loop(0, slots, masses, 0, unroll=4)
    sum_ref[...] = jnp.zeros_like(sum_ref)

    def pairs(g, carry):
        for u in range(UNROLL):
            i = near_list[g * UNROLL + u]
            c = far_list[g * UNROLL + u]
            inverse, remain, cubed = closeness(near_ref[i], far_ref[c])
            weight = cubed * (remain * (5.0 - 4.0 * remain))
            mass = mass_ref[c]
            sum_ref[i] += (weight.reshape(LANES // 8, 8, LANES) * mass[None]).reshape(LANES, LANES)
        return carry

    lax.fori_loop(0, lax.div(total + UNROLL - 1, UNROLL), pairs, 0)
    ones = jnp.ones((8, LANES), BF16)

    def reduce(i, carry):
        part = sum_ref[i]
        hi = part.astype(BF16)
        lo = (part - hi.astype(F32)).astype(BF16)
        dims = (((1,), (1,)), ((), ()))
        summed = lax.dot_general(ones, hi, dims, preferred_element_type=F32) + lax.dot_general(
            ones, lo, dims, preferred_element_type=F32
        )
        density = WEIGHT_FACTOR * summed[0:1, :]
        density_ref[pl.ds(i, 1), :] = density
        energy = states_ref[i, 7:8, :]
        mass = states_ref[i, 6:7, :]
        safe = jnp.where(mass > 0, density, 1.0)
        ratio_ref[pl.ds(i, 1), :] = (ADIABATIC - 1.0) * density * energy / (safe * safe)
        return carry

    lax.fori_loop(0, slots, reduce, 0, unroll=4)


def force_features(tile, ratio, row):
    mass = jnp.broadcast_to(tile[6:7, :], (8, LANES))
    dotted = sum_rows(jnp.where(row < 3, tile * pltpu.roll(tile, 5, 0), 0.0))
    plain = jnp.where(row < 6, tile, jnp.where(row == 6, 1.0, dotted)) * mass
    heavy = jnp.where((row < 3) | (row == 6), plain * ratio, 0.0)
    p, h = split3(plain), split3(heavy)
    return jnp.concatenate([p[0], h[0], p[1], h[1], p[2], h[2]], axis=0).astype(BF16)


def force_kernel(slots, width, neighbours_ref, counts_ref, own_ref, first_ref, second_ref, states_ref,
                 density_ref, ratio_ref, first_ratio_ref, second_ratio_ref,
                 updated_ref, derived_ref, near_ref, far_ref, field_ref, sum_ref, near_list, far_list):
    total = build_list(neighbours_ref, counts_ref, near_list, far_list, slots, width)
    bases = [region_base(r, slots) for r in range(2)]
    row = row_index()
    fill_far(far_ref, own_ref, (first_ref, second_ref), bases, slots)
    fill_near(near_ref, own_ref, slots)
    field_ref[3 * slots] = jnp.zeros((48, LANES), BF16)

    def fields(i, carry):
        for ref, ratios, base in (
            (own_ref, ratio_ref, slots),
            (first_ref, first_ratio_ref, bases[0]),
            (second_ref, second_ratio_ref, bases[1]),
        ):
            field_ref[base + i] = force_features(ref[i], ratios[pl.ds(i, 1), :], row)
        return carry

    lax.fori_loop(0, slots, fields, 0, unroll=2)
    sum_ref[...] = jnp.zeros_like(sum_ref)

    def pairs(g, carry):
        for u in range(UNROLL):
            i = near_list[g * UNROLL + u]
            c = far_list[g * UNROLL + u]
            inverse, remain, cubed = closeness(near_ref[i], far_ref[c])
            slope = cubed * (inverse * inverse)
            hi = slope.astype(BF16)
            lo = (slope - hi.astype(F32)).astype(BF16)
            dims = (((1,), (1,)), ((), ()))
            field = field_ref[c]
            both = lax.dot_general(field, hi, dims, preferred_element_type=F32) + lax.dot_general(
                field, lo, dims, preferred_element_type=F32
            )
            sum_ref[i] += both[0:16] + (both[16:32] + both[32:48])
        return carry

    lax.fori_loop(0, lax.div(total + UNROLL - 1, UNROLL), pairs, 0)

    def finish(i, carry):
        tile = own_ref[i]
        ratio = ratio_ref[pl.ds(i, 1), :]
        density = density_ref[pl.ds(i, 1), :]
        plain = SLOPE_FACTOR * sum_ref[i, 0:8, :]
        heavy = SLOPE_FACTOR * sum_ref[i, 8:16, :]
        spread = tile * plain[6:7, :] - plain
        change = -(ratio * spread + (tile * heavy[6:7, :] - heavy))
        crossed = tile * pltpu.roll(spread, 5, 0) - pltpu.roll(tile, 5, 0) * plain
        heating = ratio * (sum_rows(jnp.where(row < 3, crossed, 0.0)) + plain[7:8, :])
        top = states_ref[i, 0:8, :]
        low = states_ref[i, 8:16, :]
        present = (top[6:7, :] > 0).astype(F32)
        moved = top + TIMESTEP * pltpu.roll(change, 3, 0)
        heated = top + TIMESTEP * heating
        placed = top + TIMESTEP * pltpu.roll(moved, 5, 0)
        fresh = jnp.where(row < 3, placed, jnp.where(row < 6, moved, jnp.where(row == 6, top, heated)))
        updated_ref[i, 0:8, :] = fresh * present
        updated_ref[i, 8:16, :] = low * present
        shown = jnp.where(row == 0, density, jnp.where(row < 4, pltpu.roll(change, 1, 0), heating)) * present
        derived_ref[i] = shown[0:5, :]
        return carry

    lax.fori_loop(0, slots, finish, 0, unroll=2)


def body(tiles, slabs, particles, dest_slot, neighbours, counts):
    bins, floats, lanes = particles.shape
    slots, width = neighbours.shape
    cap = slots // tiles
    chunk = (cap, floats, lanes)
    packed = kernel_call(
        lambda *refs: pack_kernel(tiles, cap, *refs),
        [("s", dest_slot), ("v", particles)],
        [chunk] * tiles,
        [pltpu.VMEM((slots, floats, lanes), F32)],
        0,
        "pack",
    )
    parts = [packed[0]] + [
        lax.ppermute(packed[k], "tile", [(t, partner_tile(t, k, tiles)) for t in range(tiles)])
        for k in range(1, tiles)
    ]
    states, halo = kernel_call(
        lambda *refs: state_kernel(tiles, cap, *refs),
        [("v", part) for part in parts],
        [(slots, floats, lanes), (slots, 8, lanes)],
        [],
        0,
        "states",
    )
    first_pairs = [(s, s ^ 1) for s in range(slabs)]
    second_pairs = [(s, (((s + 1) ^ 1) - 1) % slabs) for s in range(slabs)]

    def both_sides(array):
        second = lax.ppermute(array, "slab", second_pairs)
        first = lax.ppermute(array, "slab", first_pairs)
        return first, second

    first, second = both_sides(halo)
    pair_terms = slots * width * lanes * lanes
    tables = [
        pltpu.VMEM((slots + 1, lanes, 32), BF16),
        pltpu.VMEM((3 * slots + 1, 32, 2 * lanes), BF16),
    ]
    lists = [pltpu.SMEM((slots * width + UNROLL,), jnp.int32)] * 2
    density, ratio = kernel_call(
        lambda *refs: density_kernel(slots, width, *refs),
        [("s", neighbours), ("s", counts), ("v", halo), ("v", first), ("v", second), ("v", states)],
        [(slots, lanes)] * 2,
        tables
        + [pltpu.VMEM((slots + 1, lanes, lanes), F32), pltpu.VMEM((3 * slots + 1, 8, lanes), F32)]
        + lists,
        30 * pair_terms,
        "density",
    )
    first_ratio, second_ratio = both_sides(ratio)
    updated, derived = kernel_call(
        lambda *refs: force_kernel(slots, width, *refs),
        [("s", neighbours), ("s", counts), ("v", halo), ("v", first), ("v", second), ("v", states),
         ("v", density), ("v", ratio), ("v", first_ratio), ("v", second_ratio)],
        [(slots, floats, lanes), (slots, 5, lanes)],
        tables
        + [pltpu.VMEM((3 * slots + 1, 48, lanes), BF16), pltpu.VMEM((slots + 1, 16, lanes), F32)]
        + lists,
        30 * pair_terms,
        "force",
    )
    return updated, derived


def solution(mesh):
    tiles, slabs = mesh.shape["tile"], mesh.shape["slab"]
    in_specs = (
        P(("slab", "tile"), None, None),
        P(("slab", "tile")),
        P(("slab", "tile"), None),
        P(("slab", "tile")),
    )
    out_specs = (P(("slab", "tile"), None, None), P(("slab", "tile"), None, None))
    return jax.shard_map(
        lambda *args: body(tiles, slabs, *args), mesh=mesh, in_specs=in_specs, out_specs=out_specs, check_vma=False
    )
```

```python
import math

import jax
import jax.numpy as jnp
from jax import lax
from jax.experimental import pallas as pl
from jax.experimental.pallas import tpu as pltpu
from jax.sharding import PartitionSpec as P

ADIABATIC = 5.0 / 3.0
TIMESTEP = 0.5
KERNEL_NORM = 21.0 / (16.0 * math.pi)
MASS_UNIT = 512.0
WEIGHT_FACTOR = 8.0 * KERNEL_NORM / MASS_UNIT
SLOPE_FACTOR = -5.0 * 32.0 * KERNEL_NORM / MASS_UNIT
CENTRE = 1.0
AWAY = 1.0e4
LANES = 128
GROUP = 16
DEPTH = 32
FIELD_ROWS = 40

F32 = jnp.float32
BF16 = jnp.bfloat16
I32 = jnp.int32


def vmem_spec():
    return pl.BlockSpec(memory_space=pltpu.VMEM)


def smem_spec():
    return pl.BlockSpec(memory_space=pltpu.SMEM)


def hbm_spec():
    return pl.BlockSpec(memory_space=pltpu.HBM)


def any_spec():
    return pl.BlockSpec(memory_space=pl.ANY)


SPECS = {"s": smem_spec, "v": vmem_spec, "h": hbm_spec, "a": any_spec}


def in_hbm(array):
    return pltpu.with_memory_space_constraint(array, pltpu.HBM)


def kernel_call(kernel, ins, outs, scratch, nanoseconds, name, aliases=None):
    return pl.pallas_call(
        kernel,
        out_shape=[jax.ShapeDtypeStruct(shape, dtype) for _, shape, dtype in outs],
        in_specs=[SPECS[memory]() for memory, _ in ins],
        out_specs=[SPECS[memory]() for memory, _, _ in outs],
        scratch_shapes=scratch,
        input_output_aliases=aliases or {},
        compiler_params=pltpu.CompilerParams(vmem_limit_bytes=32 * 1024 * 1024),
        cost_estimate=pl.CostEstimate(flops=0, bytes_accessed=3000 * nanoseconds, transcendentals=0),
        name=name,
    )(*[array for _, array in ins])


def is_power(count):
    return count & (count - 1) == 0


def partner_tile(index, step, count):
    return index ^ step if is_power(count) else (index + step) % count


def source_tile(index, step, count):
    return index ^ step if is_power(count) else lax.rem(index + count - step, count)


def rounded(value):
    return value.astype(BF16).astype(F32)


def split2(value):
    hi = rounded(value)
    return hi, rounded(value - hi)


def split3(value):
    hi = rounded(value)
    mid = rounded(value - hi)
    return hi, mid, rounded(value - hi - mid)


class Plan:
    def __init__(self, slots, width):
        self.slots, self.width = slots, width
        self.entry_bits = (width - 1).bit_length()
        self.cand_bits = (2 * slots).bit_length()
        self.length = slots * width + 2 * GROUP
        self.codes = (slots + 1) << self.entry_bits
        self.local, self.remote = 0, self.length
        self.counts = 2 * self.length
        self.size = 2 * self.length + 8
        self.stored = slots * width + 2 * GROUP

    def word(self, slot, entry, cand):
        return (((slot << self.entry_bits) + entry) << self.cand_bits) + cand

    def code(self, word):
        return word >> self.cand_bits

    def slot(self, word):
        return word >> (self.cand_bits + self.entry_bits)

    def cand(self, word):
        return word & ((1 << self.cand_bits) - 1)

    def groups(self, ref, which):
        return lax.div(ref[self.counts + which] + GROUP - 1, GROUP)

    def stored_base(self, ref, which):
        return self.groups(ref, 0) * GROUP if which else 0


def plan_kernel(plan, neighbours_ref, counts_ref, after_ref, plan_ref):
    slots = plan.slots
    upper_first = lax.rem(lax.axis_index("slab"), 2) == 0
    low_base = jnp.where(upper_first, slots, 0)
    high_base = jnp.where(upper_first, -2 * slots, -slots)

    def fill(i, totals):
        near, far = totals
        used = counts_ref[i]
        for k in range(plan.width):
            n = neighbours_ref[k, i]
            local = (n >= slots) & (n < 2 * slots)
            cand = jnp.where(n < slots, n + low_base, jnp.where(local, n - slots, n + high_base))
            word = plan.word(i, k, cand)
            plan_ref[plan.local + near] = word
            plan_ref[plan.remote + far] = word
            active = k < used
            near = near + (active & local).astype(I32)
            far = far + (active & jnp.logical_not(local)).astype(I32)
        return near, far

    near, far = lax.fori_loop(0, slots, fill, (jnp.int32(0), jnp.int32(0)))
    for k in range(GROUP):
        plan_ref[plan.local + near + k] = plan.word(slots, 0, slots)
        plan_ref[plan.remote + far + k] = plan.word(slots, 0, 2 * slots)
    plan_ref[plan.counts] = near
    plan_ref[plan.counts + 1] = far


def pack_kernel(tiles, cap, floats, dest_ref, particles_ref, *refs):
    outs, (packed, staged, dest, sems) = refs[:tiles], refs[tiles:]
    bring = [pltpu.make_async_copy(dest_ref, dest, sems.at[0]), pltpu.make_async_copy(particles_ref, staged, sems.at[1])]
    for copy in bring:
        copy.start()
    packed[...] = jnp.zeros_like(packed)
    me = lax.axis_index("tile")
    for copy in bring:
        copy.wait()

    def place(b, carry):
        target = dest[b]
        owner = lax.div(target, cap)
        step = owner ^ me if is_power(tiles) else lax.rem(owner + tiles - me, tiles)
        packed[step * cap + lax.rem(target, cap)] = staged[b]
        return carry

    lax.fori_loop(0, staged.shape[0], place, 0, unroll=4)
    for k in range(tiles):
        outs[k][...] = packed[k * cap : (k + 1) * cap].reshape(cap * floats, LANES)


def states_kernel(tiles, cap, floats, *refs):
    parts, (after_ref, own_ref, moving_ref) = refs[:tiles], refs[tiles:]
    me = lax.axis_index("tile")
    for k in range(tiles):
        base = pl.multiple_of(source_tile(me, k, tiles) * cap, cap)
        rows = pl.ds(base, cap)

        def field(f):
            return parts[k][pl.ds(f, cap, stride=floats), :]

        for f in range(8):
            own_ref[f, rows, :] = field(f)
        mass = field(6)
        present = mass > 0
        for f in range(3):
            moving_ref[f, rows, :] = field(f) - CENTRE
        moving_ref[3, rows, :] = jnp.where(present, field(8), 1.0)
        scaled = jnp.where(present, mass * MASS_UNIT, 1.0)
        root = jnp.exp(jnp.log(scaled) * (-1.0 / 3.0))
        for _ in range(2):
            root = root * (4.0 - scaled * (root * root * root)) * (1.0 / 3.0)
        moving_ref[4, rows, :] = jnp.where(present, root, 0.0)
        for f in range(3):
            moving_ref[5 + f, rows, :] = field(3 + f)


def store_far(far_ref, base, moving_ref, slots):
    def put(row, value):
        far_ref[pl.ds(base * DEPTH + row, slots, stride=DEPTH), :] = value

    place = [moving_ref[f] for f in range(3)]
    smooth, stretch = moving_ref[3], moving_ref[4]
    present = stretch > 0
    stretch = jnp.where(present, stretch, 1.0)
    square = stretch * stretch
    norm = 0.0
    for f in range(3):
        hi, mid, lo = split3(-2.0 * square * place[f])
        norm = norm + place[f] * place[f]
        put(f, hi)
        put(3 + f, hi)
        put(6 + f, hi)
        put(9 + f, mid)
        put(12 + f, lo)
    for row, value in enumerate(split3(jnp.where(present, square * norm, AWAY))):
        put(15 + row, value)
    s1, s2, s3 = split3(square)
    for row, value in enumerate((s1, s1, s1, s2, s2, s3)):
        put(18 + row, value)
    for row, value in enumerate(split3(stretch * smooth)):
        put(24 + row, value)
    u1, u2 = split2(stretch)
    for row, value in enumerate((u1, u1, u2, u2)):
        put(27 + row, value)
    put(31, jnp.zeros_like(stretch))


def store_far_dummy(far_ref, index):
    row = lax.broadcasted_iota(I32, (DEPTH, LANES), 0)
    far_ref[index * DEPTH : (index + 1) * DEPTH, :] = jnp.where(row == 15, AWAY, jnp.where(row == 24, 1.0, 0.0))


def store_near(near_ref, moving_ref, slots):
    near_ref[...] = jnp.zeros_like(near_ref)
    row = lax.broadcasted_iota(I32, (DEPTH, LANES), 0)
    start = 2 * slots * DEPTH
    near_ref[start : start + DEPTH, :] = jnp.where((row >= 15) & (row < 18), 1.0, 0.0)
    near_ref[start + DEPTH : start + 2 * DEPTH, :] = jnp.where((row >= 24) & (row < 27), 1.0, 0.0)

    def put(row, value, half=0):
        near_ref[pl.ds(half * DEPTH + row, slots, stride=2 * DEPTH), :] = value

    place = [moving_ref[f] for f in range(3)]
    norm = 0.0
    for f in range(3):
        hi, mid, lo = split3(place[f])
        norm = norm + place[f] * place[f]
        put(f, hi)
        put(3 + f, mid)
        put(6 + f, lo)
        put(9 + f, hi)
        put(12 + f, hi)
    ones = jnp.ones_like(norm)
    for row in range(3):
        put(15 + row, ones)
        put(24 + row, ones, 1)
    n1, n2, n3 = split3(norm)
    for row, value in enumerate((n1, n2, n3, n1, n2, n1)):
        put(18 + row, value)
    h1, h2 = split2(moving_ref[3])
    for row, value in enumerate((h1, h2, h1, h2)):
        put(27 + row, value, 1)


def pair_loop(plan, plan_ref, which, near_ref, far_ref, weight_ref, slope_ref):
    base = plan.remote if which else plan.local
    stored = plan.stored_base(plan_ref, which)

    def group(g, carry):
        for u in range(GROUP):
            word = plan_ref[base + g * GROUP + u]
            far = far_ref[pl.ds(pl.multiple_of(plan.cand(word) * DEPTH, DEPTH), DEPTH), :]
            near = near_ref[pl.ds(pl.multiple_of(plan.slot(word) * (2 * DEPTH), DEPTH), 2 * DEPTH), :]
            near = jnp.concatenate([near[0:DEPTH], near[DEPTH : 2 * DEPTH]], axis=1)
            both = lax.dot_general(far, near, (((0,), (0,)), ((), ())), preferred_element_type=F32)
            squared = jnp.maximum(both[:, 0:LANES], 1e-20)
            inverse = pltpu.reciprocal(both[:, LANES : 2 * LANES], approx=True)
            remain = jnp.maximum(1.0 - squared * lax.rsqrt(squared) * inverse, 0.0)
            scaled = inverse * remain
            cubed = scaled * scaled * scaled
            weight = cubed * (remain * (5.0 - 4.0 * remain))
            weight_ref[plan.code(word)] = jnp.sum(weight.reshape(LANES // 8, 8, LANES), axis=0)
            slope_ref[stored + g * GROUP + u] = cubed * (inverse * inverse)
        return carry

    lax.fori_loop(0, plan.groups(plan_ref, which), group, 0)


def local_kernel(plan, plan_ref, moving_ref, near_ref, weight_ref, slope_ref, far_ref):
    slots = plan.slots
    store_near(near_ref, moving_ref, slots)
    store_far(far_ref, 0, moving_ref, slots)
    store_far_dummy(far_ref, slots)
    weight_ref[...] = jnp.zeros_like(weight_ref)
    pair_loop(plan, plan_ref, 0, near_ref, far_ref, weight_ref, slope_ref)


def remote_kernel(plan, plan_ref, own_ref, first_ref, second_ref, near_ref, weight_ref, slope_in_ref,
                  density_ref, ratio_ref, slope_ref, far_ref, added_ref):
    slots = plan.slots
    store_far(far_ref, 0, first_ref, slots)
    store_far(far_ref, slots, second_ref, slots)
    store_far_dummy(far_ref, 2 * slots)
    added_ref[...] = jnp.zeros_like(added_ref)
    pair_loop(plan, plan_ref, 1, near_ref, far_ref, added_ref, slope_ref)
    entries = 1 << plan.entry_bits
    weight_rows = weight_ref.reshape(plan.codes * 8, LANES)
    added_rows = added_ref.reshape(plan.codes * 8, LANES)
    total = 0.0
    for row in range(8 * plan.width):
        picked = pl.ds(row, slots, stride=8 * entries)
        total = total + (weight_rows[picked, :] + added_rows[picked, :])
    density = WEIGHT_FACTOR * total
    safe = jnp.where(own_ref[6] > 0, density, 1.0)
    density_ref[...] = density
    ratio_ref[...] = (ADIABATIC - 1.0) * density * own_ref[7] / (safe * safe)


def store_fields(field_ref, base, moving_ref, ratio_ref, slots):
    def put(row, value):
        field_ref[pl.ds(base * FIELD_ROWS + row, slots, stride=FIELD_ROWS), :] = value

    stretch = moving_ref[4]
    square = stretch * stretch
    place = [moving_ref[f] for f in range(3)]
    speed = [moving_ref[5 + f] for f in range(3)]
    dotted = place[0] * speed[0] + place[1] * speed[1] + place[2] * speed[2]
    plain = [square] + [square * value for value in place + speed + [dotted]]
    heavy = [ratio_ref[...] * value for value in plain[0:4]]
    for row, value in enumerate(plain):
        for part, piece in enumerate(split3(value)):
            put(8 * part + row, piece)
    for row, value in enumerate(heavy):
        for part, piece in enumerate(split3(value)):
            put(24 + 4 * part + row, piece)
        put(36 + row, jnp.zeros_like(value))


def store_field_dummy(field_ref, index):
    field_ref[index * FIELD_ROWS : (index + 1) * FIELD_ROWS, :] = jnp.zeros((FIELD_ROWS, LANES), F32)


def field_loop(plan, plan_ref, which, field_ref, slope_ref, sum_ref):
    base = plan.remote if which else plan.local
    stored = plan.stored_base(plan_ref, which)

    def group(g, carry):
        for u in range(GROUP):
            word = plan_ref[base + g * GROUP + u]
            start = pl.multiple_of(plan.cand(word) * FIELD_ROWS, 8)
            field = field_ref[pl.ds(start, FIELD_ROWS), :].astype(BF16)
            slope = slope_ref[stored + g * GROUP + u]
            hi = slope.astype(BF16)
            lo = (slope - hi.astype(F32)).astype(BF16)
            both = jnp.dot(
                jnp.concatenate([field, field], axis=1),
                jnp.concatenate([hi, lo], axis=0),
                preferred_element_type=F32,
            )
            code = plan.code(word)
            sum_ref[code, 0:8, :] = both[0:8] + both[8:16] + both[16:24]
            sum_ref[code, 8:16, :] = both[24:32] + both[32:40]
        return carry

    lax.fori_loop(0, plan.groups(plan_ref, which), group, 0)


def local_field_kernel(plan, plan_ref, moving_ref, ratio_ref, slope_ref, sum_ref, field_ref):
    store_fields(field_ref, 0, moving_ref, ratio_ref, plan.slots)
    store_field_dummy(field_ref, plan.slots)
    sum_ref[...] = jnp.zeros_like(sum_ref)
    field_loop(plan, plan_ref, 0, field_ref, slope_ref, sum_ref)


def final_kernel(plan, tiles, cap, floats, plan_ref, own_ref, moving_ref, first_ref, second_ref, density_ref, ratio_ref,
                 first_ratio_ref, second_ratio_ref, slope_ref, local_sum_ref, *refs):
    parts, (updated_ref, derived_ref, field_ref, sum_ref) = refs[:tiles], refs[tiles:]
    slots = plan.slots
    store_fields(field_ref, 0, first_ref, first_ratio_ref, slots)
    store_fields(field_ref, slots, second_ref, second_ratio_ref, slots)
    store_field_dummy(field_ref, 2 * slots)
    sum_ref[...] = jnp.zeros_like(sum_ref)
    me = lax.axis_index("tile")
    for k in range(tiles):
        base = source_tile(me, k, tiles) * cap
        for j in range(cap):
            present = (parts[k][j * floats + 6 : j * floats + 7, :] > 0).astype(F32)
            start = pl.multiple_of((base + j) * floats + 8, 8)
            updated_ref[pl.ds(start, floats - 8), :] = parts[k][j * floats + 8 : (j + 1) * floats, :] * present
    field_loop(plan, plan_ref, 1, field_ref, slope_ref, sum_ref)
    local_rows = local_sum_ref.reshape(plan.codes * 16, LANES)
    remote_rows = sum_ref.reshape(plan.codes * 16, LANES)
    entries = 1 << plan.entry_bits

    def summed(row):
        total = 0.0
        for k in range(plan.width):
            picked = pl.ds(16 * k + row, slots, stride=16 * entries)
            total = total + (local_rows[picked, :] + remote_rows[picked, :])
        return SLOPE_FACTOR * total

    plain = [summed(row) for row in range(8)]
    heavy = [summed(8 + row) + summed(12 + row) for row in range(4)]
    place = [moving_ref[f] for f in range(3)]
    speed = [own_ref[3 + f] for f in range(3)]
    ratio, density = ratio_ref[...], density_ref[...]
    accel, heating = [], plain[7]
    for f in range(3):
        spread = place[f] * plain[0] - plain[1 + f]
        accel.append(-(ratio * spread + (place[f] * heavy[0] - heavy[1 + f])))
        heating = heating + place[f] * (speed[f] * plain[0] - plain[4 + f]) - speed[f] * plain[1 + f]
    heating = ratio * heating
    present = (own_ref[6] > 0).astype(F32)
    fresh = {}
    for f in range(3):
        fresh[3 + f] = speed[f] + TIMESTEP * accel[f]
        fresh[f] = own_ref[f] + TIMESTEP * fresh[3 + f]
    fresh[6] = own_ref[6]
    fresh[7] = own_ref[7] + TIMESTEP * heating
    for f in range(8):
        updated_ref[pl.ds(f, slots, stride=floats), :] = fresh[f] * present
    for f, value in enumerate([density] + accel + [heating]):
        derived_ref[f] = value * present


def body(tiles, slabs, particles, dest_slot, neighbours, counts):
    bins, floats, lanes = particles.shape
    slots, width = neighbours.shape
    cap = slots // tiles
    plan = Plan(slots, width)
    packed = kernel_call(
        lambda *refs: pack_kernel(tiles, cap, floats, *refs),
        [("h", in_hbm(dest_slot)), ("h", in_hbm(particles))],
        [("v", (cap * floats, lanes), F32)] * tiles,
        [
            pltpu.VMEM((slots, floats, lanes), F32),
            pltpu.VMEM((bins, floats, lanes), F32),
            pltpu.SMEM((bins,), I32),
            pltpu.SemaphoreType.DMA((2,)),
        ],
        1500,
        "pack",
    )
    parts = [packed[0]] + [
        lax.ppermute(packed[k], "tile", [(t, partner_tile(t, k, tiles)) for t in range(tiles)])
        for k in range(1, tiles)
    ]
    (lists,) = kernel_call(
        lambda *refs: plan_kernel(plan, *refs),
        [("s", in_hbm(neighbours.T)), ("s", in_hbm(counts)), ("a", packed[0])],
        [("s", (plan.size,), I32)],
        [],
        2000,
        "plan",
    )
    own, moving = kernel_call(
        lambda *refs: states_kernel(tiles, cap, floats, *refs),
        [("v", part) for part in parts] + [("a", lists)],
        [("v", (8, slots, lanes), F32)] * 2,
        [],
        200,
        "states",
    )
    first_pairs = [(s, s ^ 1) for s in range(slabs)]
    second_pairs = [(s, (((s + 1) ^ 1) - 1) % slabs) for s in range(slabs)]

    def both_sides(array):
        second = lax.ppermute(array, "slab", second_pairs)
        first = lax.ppermute(array, "slab", first_pairs)
        return first, second

    first, second = both_sides(moving)
    near, weights, slopes = kernel_call(
        lambda *refs: local_kernel(plan, *refs),
        [("s", lists), ("v", moving)],
        [
            ("v", ((slots + 1) * 2 * DEPTH, lanes), F32),
            ("v", (plan.codes, 8, lanes), F32),
            ("v", (plan.stored, lanes, lanes), F32),
        ],
        [pltpu.VMEM(((slots + 1) * DEPTH, lanes), F32)],
        3500,
        "local",
    )
    density, ratio, slopes = kernel_call(
        lambda *refs: remote_kernel(plan, *refs),
        [("s", lists), ("v", own), ("v", first), ("v", second), ("v", near), ("v", weights), ("v", slopes)],
        [("v", (slots, lanes), F32)] * 2 + [("v", (plan.stored, lanes, lanes), F32)],
        [pltpu.VMEM(((2 * slots + 1) * DEPTH, lanes), F32), pltpu.VMEM((plan.codes, 8, lanes), F32)],
        3500,
        "remote",
        {6: 2},
    )
    first_ratio, second_ratio = both_sides(ratio)
    (local_sums,) = kernel_call(
        lambda *refs: local_field_kernel(plan, *refs),
        [("s", lists), ("v", moving), ("v", ratio), ("v", slopes)],
        [("v", (plan.codes, 16, lanes), F32)],
        [pltpu.VMEM(((slots + 1) * FIELD_ROWS, lanes), F32)],
        2500,
        "fields",
    )
    updated, derived = kernel_call(
        lambda *refs: final_kernel(plan, tiles, cap, floats, *refs),
        [("s", lists), ("v", own), ("v", moving), ("v", first), ("v", second), ("v", density), ("v", ratio),
         ("v", first_ratio), ("v", second_ratio), ("v", slopes), ("v", local_sums)]
        + [("v", part) for part in parts],
        [("v", (slots * floats, lanes), F32), ("v", (5, slots, lanes), F32)],
        [pltpu.VMEM(((2 * slots + 1) * FIELD_ROWS, lanes), F32), pltpu.VMEM((plan.codes, 16, lanes), F32)],
        3000,
        "final",
    )
    return updated.reshape(slots, floats, lanes), derived.transpose(1, 0, 2)


def solution(mesh):
    tiles, slabs = mesh.shape["tile"], mesh.shape["slab"]
    in_specs = (
        P(("slab", "tile"), None, None),
        P(("slab", "tile")),
        P(("slab", "tile"), None),
        P(("slab", "tile")),
    )
    out_specs = (P(("slab", "tile"), None, None), P(("slab", "tile"), None, None))
    return jax.shard_map(
        lambda *args: body(tiles, slabs, *args), mesh=mesh, in_specs=in_specs, out_specs=out_specs, check_vma=False
    )
```

```python
import math

import jax
import jax.numpy as jnp
from jax import lax
from jax.experimental import pallas as pl
from jax.experimental.pallas import tpu as pltpu
from jax.sharding import PartitionSpec as P

ADIABATIC = 5.0 / 3.0
TIMESTEP = 0.5
KERNEL_NORM = 21.0 / (16.0 * math.pi)
MASS_UNIT = 512.0
WEIGHT_FACTOR = 8.0 * KERNEL_NORM / MASS_UNIT / 4.0**7
SLOPE_FACTOR = -5.0 * 32.0 * KERNEL_NORM / MASS_UNIT / 4.0**8
CENTRE = 1.0
AWAY = 1.0e4
LANES = 128
GROUPS = (24, 16, 8)
DEPTH = 32
FIELD_ROWS = 40

F32 = jnp.float32
BF16 = jnp.bfloat16
I32 = jnp.int32


def vmem_spec():
    return pl.BlockSpec(memory_space=pltpu.VMEM)


def smem_spec():
    return pl.BlockSpec(memory_space=pltpu.SMEM)


def hbm_spec():
    return pl.BlockSpec(memory_space=pltpu.HBM)


def any_spec():
    return pl.BlockSpec(memory_space=pl.ANY)


SPECS = {"s": smem_spec, "v": vmem_spec, "h": hbm_spec, "a": any_spec}


def in_hbm(array):
    return pltpu.with_memory_space_constraint(array, pltpu.HBM)


def kernel_call(kernel, ins, outs, scratch, nanoseconds, name, aliases=None):
    return pl.pallas_call(
        kernel,
        out_shape=[jax.ShapeDtypeStruct(shape, dtype) for _, shape, dtype in outs],
        in_specs=[SPECS[memory]() for memory, _ in ins],
        out_specs=[SPECS[memory]() for memory, _, _ in outs],
        scratch_shapes=scratch,
        input_output_aliases=aliases or {},
        compiler_params=pltpu.CompilerParams(vmem_limit_bytes=32 * 1024 * 1024),
        cost_estimate=pl.CostEstimate(flops=0, bytes_accessed=3000 * nanoseconds, transcendentals=0),
        name=name,
    )(*[array for _, array in ins])


def is_power(count):
    return count & (count - 1) == 0


def partner_tile(index, step, count):
    return index ^ step if is_power(count) else (index + step) % count


def source_tile(index, step, count):
    return index ^ step if is_power(count) else lax.rem(index + count - step, count)


def rounded(value):
    return value.astype(BF16).astype(F32)


def split2(value):
    hi = rounded(value)
    return hi, rounded(value - hi)


def split3(value):
    hi = rounded(value)
    mid = rounded(value - hi)
    return hi, mid, rounded(value - hi - mid)


def sum_rows(tile):
    tile = tile + pltpu.roll(tile, 4, 0)
    tile = tile + pltpu.roll(tile, 2, 0)
    return tile + pltpu.roll(tile, 1, 0)


class Plan:
    def __init__(self, slots, width):
        self.slots, self.width = slots, width
        self.entry_bits = (width - 1).bit_length()
        self.cand_bits = slots.bit_length()
        self.length = slots * width + GROUPS[0]
        self.codes = (slots + 1) << self.entry_bits
        self.counts = 3 * self.length
        self.size = 3 * self.length + 8
        self.stored = slots * width + 3 * GROUPS[-1]
        self.dummy = self.word(slots, 0, slots)

    def word(self, slot, entry, cand):
        return (((slot << self.entry_bits) + entry) << self.cand_bits) + cand

    def code(self, word):
        return word >> self.cand_bits

    def slot(self, word):
        return word >> (self.cand_bits + self.entry_bits)

    def cand(self, word):
        return word & ((1 << self.cand_bits) - 1)

    def stored_base(self, ref, which):
        step = GROUPS[-1]
        base = 0
        for k in range(which):
            base = base + lax.div(ref[self.counts + k] + step - 1, step) * step
        return base


def in_groups(plan, plan_ref, which, work):
    count = plan_ref[plan.counts + which]
    large, medium, small = GROUPS
    full = lax.div(count + large - 1 - medium, large)

    def step(g, carry):
        work(g * large, large)
        return carry

    lax.fori_loop(0, full, step, 0)
    rest = count - full * large

    @pl.when(rest > small)
    def _():
        work(full * large, medium)

    @pl.when((rest > 0) & (rest <= small))
    def _():
        work(full * large, small)


def plan_kernel(plan, neighbours_ref, counts_ref, after_ref, plan_ref):
    slots = plan.slots
    upper_first = lax.rem(lax.axis_index("slab"), 2) == 0
    low = jnp.where(upper_first, 2, 1)
    high = 3 - low

    def fill(i, totals):
        used = counts_ref[i]
        for k in range(plan.width):
            n = neighbours_ref[k, i]
            region = lax.div(n, slots)
            which = jnp.where(region == 1, 0, jnp.where(region == 0, low, high))
            word = plan.word(i, k, n - region * slots)
            kept = []
            for w in range(3):
                plan_ref[w * plan.length + totals[w]] = word
                kept.append(totals[w] + ((k < used) & (which == w)).astype(I32))
            totals = tuple(kept)
        return totals

    totals = lax.fori_loop(0, slots, fill, (jnp.int32(0),) * 3)
    for w in range(3):
        for k in range(GROUPS[0]):
            plan_ref[w * plan.length + totals[w] + k] = plan.dummy
        plan_ref[plan.counts + w] = totals[w]


def pack_kernel(tiles, cap, floats, dest_ref, particles_ref, *refs):
    outs, (packed, staged, dest, sems) = refs[:tiles], refs[tiles:]
    bring = [pltpu.make_async_copy(dest_ref, dest, sems.at[0]), pltpu.make_async_copy(particles_ref, staged, sems.at[1])]
    for copy in bring:
        copy.start()
    packed[...] = jnp.zeros_like(packed)
    me = lax.axis_index("tile")
    for copy in bring:
        copy.wait()

    def place(b, carry):
        target = dest[b]
        owner = lax.div(target, cap)
        step = owner ^ me if is_power(tiles) else lax.rem(owner + tiles - me, tiles)
        packed[step * cap + lax.rem(target, cap)] = staged[b]
        return carry

    lax.fori_loop(0, staged.shape[0], place, 0, unroll=4)
    for k in range(tiles):
        outs[k][...] = packed[k * cap : (k + 1) * cap].reshape(cap * floats, LANES)


def states_kernel(tiles, cap, floats, *refs):
    parts, (after_ref, own_ref, moving_ref) = refs[:tiles], refs[tiles:]
    me = lax.axis_index("tile")
    for k in range(tiles):
        base = pl.multiple_of(source_tile(me, k, tiles) * cap, cap)
        rows = pl.ds(base, cap)

        def field(f):
            return parts[k][pl.ds(f, cap, stride=floats), :]

        for f in range(8):
            own_ref[f, rows, :] = field(f)
        mass = field(6)
        present = mass > 0
        for f in range(3):
            moving_ref[f, rows, :] = field(f) - CENTRE
        moving_ref[3, rows, :] = jnp.where(present, field(8), 1.0)
        scaled = jnp.where(present, mass * MASS_UNIT, 1.0)
        root = jnp.exp(jnp.log(scaled) * (-1.0 / 3.0))
        for _ in range(2):
            root = root * (4.0 - scaled * (root * root * root)) * (1.0 / 3.0)
        moving_ref[4, rows, :] = jnp.where(present, root, 0.0)


def store_far(far_ref, base, moving_ref, slots):
    def put(row, value):
        far_ref[pl.ds(base * DEPTH + row, slots, stride=DEPTH), :] = value

    place = [moving_ref[f] for f in range(3)]
    smooth, stretch = moving_ref[3], moving_ref[4]
    present = stretch > 0
    stretch = jnp.where(present, stretch, 1.0)
    square = stretch * stretch
    norm = 0.0
    for f in range(3):
        hi, mid, lo = split3(-2.0 * square * place[f])
        norm = norm + place[f] * place[f]
        put(f, hi)
        put(3 + f, hi)
        put(6 + f, hi)
        put(9 + f, mid)
        put(12 + f, lo)
    for row, value in enumerate(split3(jnp.where(present, square * norm, AWAY))):
        put(15 + row, value)
    s1, s2, s3 = split3(square)
    for row, value in enumerate((s1, s1, s1, s2, s2, s3)):
        put(18 + row, value)
    for row, value in enumerate(split3(0.25 * stretch * smooth)):
        put(24 + row, value)
    u1, u2 = split2(0.25 * stretch)
    for row, value in enumerate((u1, u1, u2, u2)):
        put(27 + row, value)
    put(31, jnp.zeros_like(stretch))


def store_far_dummy(far_ref, index):
    row = lax.broadcasted_iota(I32, (DEPTH, LANES), 0)
    far_ref[index * DEPTH : (index + 1) * DEPTH, :] = jnp.where(row == 15, AWAY, jnp.where(row == 24, 1.0, 0.0))


def store_near(near_ref, moving_ref, slots):
    near_ref[...] = jnp.zeros_like(near_ref)
    row = lax.broadcasted_iota(I32, (DEPTH, LANES), 0)
    start = 2 * slots * DEPTH
    near_ref[start : start + DEPTH, :] = jnp.where((row >= 15) & (row < 18), 1.0, 0.0)
    near_ref[start + DEPTH : start + 2 * DEPTH, :] = jnp.where((row >= 24) & (row < 27), 1.0, 0.0)

    def put(row, value, half=0):
        near_ref[pl.ds(half * DEPTH + row, slots, stride=2 * DEPTH), :] = value

    place = [moving_ref[f] for f in range(3)]
    norm = 0.0
    for f in range(3):
        hi, mid, lo = split3(place[f])
        norm = norm + place[f] * place[f]
        put(f, hi)
        put(3 + f, mid)
        put(6 + f, lo)
        put(9 + f, hi)
        put(12 + f, hi)
    ones = jnp.ones_like(norm)
    for row in range(3):
        put(15 + row, ones)
        put(24 + row, ones, 1)
    n1, n2, n3 = split3(norm)
    for row, value in enumerate((n1, n2, n3, n1, n2, n1)):
        put(18 + row, value)
    h1, h2 = split2(moving_ref[3])
    for row, value in enumerate((h1, h2, h1, h2)):
        put(27 + row, value, 1)


def pair_loop(plan, plan_ref, which, near_ref, far_ref, weight_ref, slope_ref):
    base = which * plan.length
    stored = plan.stored_base(plan_ref, which)

    def work(start, size):
        for u in range(size):
            word = plan_ref[base + start + u]
            far = far_ref[pl.ds(pl.multiple_of(plan.cand(word) * DEPTH, DEPTH), DEPTH), :]
            near = near_ref[pl.ds(pl.multiple_of(plan.slot(word) * (2 * DEPTH), DEPTH), 2 * DEPTH), :]
            near = jnp.concatenate([near[0:DEPTH], near[DEPTH : 2 * DEPTH]], axis=1)
            both = lax.dot_general(
                far.astype(BF16), near.astype(BF16), (((0,), (0,)), ((), ())), preferred_element_type=F32
            )
            squared = jnp.maximum(both[:, 0:LANES], 1e-20)
            inverse = pltpu.reciprocal(both[:, LANES : 2 * LANES], approx=True)
            remain = jnp.maximum(4.0 - squared * lax.rsqrt(squared) * inverse, 0.0)
            scaled = inverse * remain
            cubed = scaled * scaled * scaled
            weight = cubed * (remain * (5.0 - remain))
            weight_ref[plan.code(word)] = jnp.sum(weight.reshape(LANES // 8, 8, LANES), axis=0)
            slope_ref[stored + start + u] = cubed * (inverse * inverse)

    in_groups(plan, plan_ref, which, work)


def local_kernel(plan, plan_ref, moving_ref, near_ref, weight_ref, slope_ref, far_ref):
    slots = plan.slots
    store_near(near_ref, moving_ref, slots)
    store_far(far_ref, 0, moving_ref, slots)
    store_far_dummy(far_ref, slots)
    weight_ref[...] = jnp.zeros_like(weight_ref)
    pair_loop(plan, plan_ref, 0, near_ref, far_ref, weight_ref, slope_ref)


def first_kernel(plan, plan_ref, moving_ref, near_ref, weight_in_ref, slope_in_ref, weight_ref, slope_ref, far_ref):
    store_far(far_ref, 0, moving_ref, plan.slots)
    store_far_dummy(far_ref, plan.slots)
    pair_loop(plan, plan_ref, 1, near_ref, far_ref, weight_ref, slope_ref)


def second_kernel(plan, plan_ref, own_ref, moving_ref, near_ref, weight_in_ref, slope_in_ref,
                  density_ref, thermal_ref, weight_ref, slope_ref, far_ref):
    store_far(far_ref, 0, moving_ref, plan.slots)
    store_far_dummy(far_ref, plan.slots)
    pair_loop(plan, plan_ref, 2, near_ref, far_ref, weight_ref, slope_ref)
    for i in range(plan.slots):
        first = i << plan.entry_bits
        tile = weight_ref[first]
        for k in range(1, plan.width):
            tile = tile + weight_ref[first + k]
        density_ref[i : i + 1, :] = sum_rows(tile)[0:1, :]
    density = WEIGHT_FACTOR * density_ref[...]
    density_ref[...] = density
    safe = jnp.where(own_ref[6] > 0, density, 1.0)
    thermal_ref[0] = (ADIABATIC - 1.0) * density * own_ref[7] / (safe * safe)
    for f in range(3):
        thermal_ref[1 + f] = own_ref[3 + f]


def store_fields(field_ref, base, moving_ref, thermal_ref, slots):
    def put(row, value):
        field_ref[pl.ds(base * FIELD_ROWS + row, slots, stride=FIELD_ROWS), :] = value

    stretch = moving_ref[4]
    square = stretch * stretch
    place = [moving_ref[f] for f in range(3)]
    speed = [thermal_ref[1 + f] for f in range(3)]
    dotted = place[0] * speed[0] + place[1] * speed[1] + place[2] * speed[2]
    plain = [square] + [square * value for value in place + speed + [dotted]]
    heavy = [thermal_ref[0] * value for value in plain[0:4]]
    for row, value in enumerate(plain):
        for part, piece in enumerate(split3(value)):
            put(8 * part + row, piece)
    for row, value in enumerate(heavy):
        for part, piece in enumerate(split3(value)):
            put(24 + 4 * part + row, piece)
        put(36 + row, jnp.zeros_like(value))


def store_field_dummy(field_ref, index):
    field_ref[index * FIELD_ROWS : (index + 1) * FIELD_ROWS, :] = jnp.zeros((FIELD_ROWS, LANES), F32)


def field_loop(plan, plan_ref, which, field_ref, slope_ref, sum_ref):
    base = which * plan.length
    stored = plan.stored_base(plan_ref, which)

    def work(start, size):
        for u in range(size):
            word = plan_ref[base + start + u]
            field = field_ref[pl.ds(pl.multiple_of(plan.cand(word) * FIELD_ROWS, 8), FIELD_ROWS), :].astype(BF16)
            slope = slope_ref[stored + start + u]
            hi = slope.astype(BF16)
            lo = (slope - hi.astype(F32)).astype(BF16)
            both = jnp.dot(
                jnp.concatenate([field, field], axis=1),
                jnp.concatenate([hi, lo], axis=0),
                preferred_element_type=F32,
            )
            code = plan.code(word)
            sum_ref[code, 0:8, :] = both[0:8] + both[8:16] + both[16:24]
            sum_ref[code, 8:16, :] = both[24:32] + both[32:40]

    in_groups(plan, plan_ref, which, work)


def local_field_kernel(plan, plan_ref, moving_ref, thermal_ref, slope_ref, sum_ref, field_ref):
    store_fields(field_ref, 0, moving_ref, thermal_ref, plan.slots)
    store_field_dummy(field_ref, plan.slots)
    sum_ref[...] = jnp.zeros_like(sum_ref)
    field_loop(plan, plan_ref, 0, field_ref, slope_ref, sum_ref)


def first_field_kernel(plan, plan_ref, moving_ref, thermal_ref, slope_ref, sum_in_ref, sum_ref, field_ref):
    store_fields(field_ref, 0, moving_ref, thermal_ref, plan.slots)
    store_field_dummy(field_ref, plan.slots)
    field_loop(plan, plan_ref, 1, field_ref, slope_ref, sum_ref)


def final_kernel(plan, tiles, cap, floats, plan_ref, own_ref, moving_ref, second_ref, density_ref, thermal_ref,
                 second_thermal_ref, slope_ref, sum_in_ref, *refs):
    parts, (updated_ref, derived_ref, sum_ref, field_ref, total_ref) = refs[:tiles], refs[tiles:]
    slots = plan.slots
    store_fields(field_ref, 0, second_ref, second_thermal_ref, slots)
    store_field_dummy(field_ref, slots)
    me = lax.axis_index("tile")
    for k in range(tiles):
        base = source_tile(me, k, tiles) * cap
        for j in range(cap):
            present = (parts[k][j * floats + 6 : j * floats + 7, :] > 0).astype(F32)
            start = pl.multiple_of((base + j) * floats + 8, 8)
            updated_ref[pl.ds(start, floats - 8), :] = parts[k][j * floats + 8 : (j + 1) * floats, :] * present
    field_loop(plan, plan_ref, 2, field_ref, slope_ref, sum_ref)
    for i in range(slots):
        first = i << plan.entry_bits
        tile = sum_ref[first]
        for k in range(1, plan.width):
            tile = tile + sum_ref[first + k]
        total_ref[16 * i : 16 * (i + 1), :] = tile

    def summed(row):
        return SLOPE_FACTOR * total_ref[pl.ds(row, slots, stride=16), :]

    plain = [summed(row) for row in range(8)]
    heavy = [summed(8 + row) + summed(12 + row) for row in range(4)]
    place = [moving_ref[f] for f in range(3)]
    speed = [own_ref[3 + f] for f in range(3)]
    ratio, density = thermal_ref[0], density_ref[...]
    accel, heating = [], plain[7]
    for f in range(3):
        spread = place[f] * plain[0] - plain[1 + f]
        accel.append(-(ratio * spread + (place[f] * heavy[0] - heavy[1 + f])))
        heating = heating + place[f] * (speed[f] * plain[0] - plain[4 + f]) - speed[f] * plain[1 + f]
    heating = ratio * heating
    present = (own_ref[6] > 0).astype(F32)
    fresh = {}
    for f in range(3):
        fresh[3 + f] = speed[f] + TIMESTEP * accel[f]
        fresh[f] = own_ref[f] + TIMESTEP * fresh[3 + f]
    fresh[6] = own_ref[6]
    fresh[7] = own_ref[7] + TIMESTEP * heating
    for f in range(8):
        updated_ref[pl.ds(f, slots, stride=floats), :] = fresh[f] * present
    for f, value in enumerate([density] + accel + [heating]):
        derived_ref[f] = value * present


def body(tiles, slabs, particles, dest_slot, neighbours, counts):
    bins, floats, lanes = particles.shape
    slots, width = neighbours.shape
    cap = slots // tiles
    plan = Plan(slots, width)
    packed = kernel_call(
        lambda *refs: pack_kernel(tiles, cap, floats, *refs),
        [("h", in_hbm(dest_slot)), ("h", in_hbm(particles))],
        [("v", (cap * floats, lanes), F32)] * tiles,
        [
            pltpu.VMEM((slots, floats, lanes), F32),
            pltpu.VMEM((bins, floats, lanes), F32),
            pltpu.SMEM((bins,), I32),
            pltpu.SemaphoreType.DMA((2,)),
        ],
        1500,
        "pack",
    )
    parts = [packed[0]] + [
        lax.ppermute(packed[k], "tile", [(t, partner_tile(t, k, tiles)) for t in range(tiles)])
        for k in range(1, tiles)
    ]
    (lists,) = kernel_call(
        lambda *refs: plan_kernel(plan, *refs),
        [("s", in_hbm(neighbours.T)), ("s", in_hbm(counts)), ("a", packed[0])],
        [("s", (plan.size,), I32)],
        [],
        2000,
        "plan",
    )
    own, moving = kernel_call(
        lambda *refs: states_kernel(tiles, cap, floats, *refs),
        [("v", part) for part in parts] + [("a", lists)],
        [("v", (8, slots, lanes), F32), ("v", (5, slots, lanes), F32)],
        [],
        200,
        "states",
    )
    first_pairs = [(s, s ^ 1) for s in range(slabs)]
    second_pairs = [(s, (((s + 1) ^ 1) - 1) % slabs) for s in range(slabs)]

    def both_sides(array):
        second = lax.ppermute(array, "slab", second_pairs)
        first = lax.ppermute(array, "slab", first_pairs)
        return first, second

    first, second = both_sides(moving)
    weight_out = ("v", (plan.codes, 8, lanes), F32)
    slope_out = ("v", (plan.stored, lanes, lanes), F32)
    sum_out = ("v", (plan.codes, 16, lanes), F32)
    far_table = [pltpu.VMEM(((slots + 1) * DEPTH, lanes), F32)]
    field_table = [pltpu.VMEM(((slots + 1) * FIELD_ROWS, lanes), F32)]
    near, weights, slopes = kernel_call(
        lambda *refs: local_kernel(plan, *refs),
        [("s", lists), ("v", moving)],
        [("v", ((slots + 1) * 2 * DEPTH, lanes), F32), weight_out, slope_out],
        far_table,
        3500,
        "local",
    )
    weights, slopes = kernel_call(
        lambda *refs: first_kernel(plan, *refs),
        [("s", lists), ("v", first), ("v", near), ("v", weights), ("v", slopes)],
        [weight_out, slope_out],
        far_table,
        1500,
        "first",
        {3: 0, 4: 1},
    )
    density, thermal, weights, slopes = kernel_call(
        lambda *refs: second_kernel(plan, *refs),
        [("s", lists), ("v", own), ("v", second), ("v", near), ("v", weights), ("v", slopes)],
        [("v", (slots, lanes), F32), ("v", (4, slots, lanes), F32), weight_out, slope_out],
        far_table,
        2000,
        "second",
        {4: 2, 5: 3},
    )
    first_thermal, second_thermal = both_sides(thermal)
    (sums,) = kernel_call(
        lambda *refs: local_field_kernel(plan, *refs),
        [("s", lists), ("v", moving), ("v", thermal), ("v", slopes)],
        [sum_out],
        field_table,
        1700,
        "local_fields",
    )
    (sums,) = kernel_call(
        lambda *refs: first_field_kernel(plan, *refs),
        [("s", lists), ("v", first), ("v", first_thermal), ("v", slopes), ("v", sums)],
        [sum_out],
        field_table,
        1000,
        "first_fields",
        {4: 0},
    )
    updated, derived, _ = kernel_call(
        lambda *refs: final_kernel(plan, tiles, cap, floats, *refs),
        [("s", lists), ("v", own), ("v", moving), ("v", second), ("v", density), ("v", thermal),
         ("v", second_thermal), ("v", slopes), ("v", sums)]
        + [("v", part) for part in parts],
        [("v", (slots * floats, lanes), F32), ("v", (5, slots, lanes), F32), sum_out],
        field_table + [pltpu.VMEM((slots * 16, lanes), F32)],
        2000,
        "final",
        {8: 2},
    )
    return updated.reshape(slots, floats, lanes), derived.transpose(1, 0, 2)


def solution(mesh):
    tiles, slabs = mesh.shape["tile"], mesh.shape["slab"]
    in_specs = (
        P(("slab", "tile"), None, None),
        P(("slab", "tile")),
        P(("slab", "tile"), None),
        P(("slab", "tile")),
    )
    out_specs = (P(("slab", "tile"), None, None), P(("slab", "tile"), None, None))
    return jax.shard_map(
        lambda *args: body(tiles, slabs, *args), mesh=mesh, in_specs=in_specs, out_specs=out_specs, check_vma=False
    )
```

```python
import math

import jax
import jax.numpy as jnp
from jax import lax
from jax.experimental import pallas as pl
from jax.experimental.pallas import tpu as pltpu
from jax.sharding import PartitionSpec as P

ADIABATIC = 5.0 / 3.0
TIMESTEP = 0.5
KERNEL_NORM = 21.0 / (16.0 * math.pi)
MASS_UNIT = 512.0
WEIGHT_FACTOR = 8.0 * KERNEL_NORM / MASS_UNIT / 4.0**7
SLOPE_FACTOR = -5.0 * 32.0 * KERNEL_NORM / MASS_UNIT / 4.0**8
CENTRE = 1.0
AWAY = 1.0e4
LANES = 128
GROUPS = (24, 16, 8)
EARLY = 1
CORE = 9
DEPTH = 32
FIELD_ROWS = 40

F32 = jnp.float32
BF16 = jnp.bfloat16
I32 = jnp.int32


def vmem_spec():
    return pl.BlockSpec(memory_space=pltpu.VMEM)


def smem_spec():
    return pl.BlockSpec(memory_space=pltpu.SMEM)


def hbm_spec():
    return pl.BlockSpec(memory_space=pltpu.HBM)


def any_spec():
    return pl.BlockSpec(memory_space=pl.ANY)


SPECS = {"s": smem_spec, "v": vmem_spec, "h": hbm_spec, "a": any_spec}


def in_hbm(array):
    return pltpu.with_memory_space_constraint(array, pltpu.HBM)


def kernel_call(kernel, ins, outs, scratch, nanoseconds, name, aliases=None):
    return pl.pallas_call(
        kernel,
        out_shape=[
            pltpu.SMEM(shape, dtype) if memory == "s" else jax.ShapeDtypeStruct(shape, dtype)
            for memory, shape, dtype in outs
        ],
        in_specs=[SPECS[memory]() for memory, _ in ins],
        out_specs=[SPECS[memory]() for memory, _, _ in outs],
        scratch_shapes=scratch,
        input_output_aliases=aliases or {},
        compiler_params=pltpu.CompilerParams(vmem_limit_bytes=32 * 1024 * 1024),
        cost_estimate=pl.CostEstimate(flops=0, bytes_accessed=3000 * nanoseconds, transcendentals=0),
        name=name,
    )(*[array for _, array in ins])


def is_power(count):
    return count & (count - 1) == 0


def partner_tile(index, step, count):
    return index ^ step if is_power(count) else (index + step) % count


def source_tile(index, step, count):
    return index ^ step if is_power(count) else lax.rem(index + count - step, count)


def rounded(value):
    return value.astype(BF16).astype(F32)


def split2(value):
    hi = rounded(value)
    return hi, rounded(value - hi)


def split3(value):
    hi = rounded(value)
    mid = rounded(value - hi)
    return hi, mid, rounded(value - hi - mid)


def sum_rows(tile):
    tile = tile + pltpu.roll(tile, 4, 0)
    tile = tile + pltpu.roll(tile, 2, 0)
    return tile + pltpu.roll(tile, 1, 0)


class Plan:
    def __init__(self, slots, width):
        self.slots, self.width = slots, width
        self.entry_bits = (width - 1).bit_length()
        self.cand_bits = slots.bit_length()
        self.length = slots * width + GROUPS[0]
        self.codes = (slots + 1) << self.entry_bits
        self.counts = 3 * self.length
        self.size = 3 * self.length + 8
        self.stored = slots * width + 3 * GROUPS[-1]
        self.dummy = self.word(slots, 0, slots)

    def word(self, slot, entry, cand):
        return (((slot << self.entry_bits) + entry) << self.cand_bits) + cand

    def code(self, word):
        return word >> self.cand_bits

    def slot(self, word):
        return word >> (self.cand_bits + self.entry_bits)

    def cand(self, word):
        return word & ((1 << self.cand_bits) - 1)

    def stored_base(self, ref, which):
        step = GROUPS[-1]
        base = 0
        for k in range(which):
            base = base + lax.div(ref[self.counts + k] + step - 1, step) * step
        return base


def in_groups(plan, plan_ref, which, work):
    count = plan_ref[plan.counts + which]
    large, medium, small = GROUPS
    full = lax.div(count + large - 1 - medium, large)

    def step(g, carry):
        work(g * large, large)
        return carry

    lax.fori_loop(0, full, step, 0)
    rest = count - full * large

    @pl.when(rest > small)
    def _():
        work(full * large, medium)

    @pl.when((rest > 0) & (rest <= small))
    def _():
        work(full * large, small)


def plan_kernel(plan, neighbours_ref, counts_ref, after_ref, plan_ref):
    slots = plan.slots
    upper_first = lax.rem(lax.axis_index("slab"), 2) == 0
    low = jnp.where(upper_first, 2, 1)
    high = 3 - low

    def fill(i, totals):
        used = counts_ref[i]
        for k in range(plan.width):
            n = neighbours_ref[k, i]
            region = lax.div(n, slots)
            which = jnp.where(region == 1, 0, jnp.where(region == 0, low, high))
            word = plan.word(i, k, n - region * slots)
            kept = []
            for w in range(3):
                plan_ref[w * plan.length + totals[w]] = word
                kept.append(totals[w] + ((k < used) & (which == w)).astype(I32))
            totals = tuple(kept)
        return totals

    totals = lax.fori_loop(0, slots, fill, (jnp.int32(0),) * 3, unroll=4)
    for w in range(3):
        for k in range(GROUPS[0]):
            plan_ref[w * plan.length + totals[w] + k] = plan.dummy
        plan_ref[plan.counts + w] = totals[w]


def pack_kernel(tiles, cap, floats, dest_ref, particles_ref, *refs):
    cores, rests, (packed, staged, dest, sems) = refs[:tiles], refs[tiles : 2 * tiles], refs[2 * tiles :]
    bring = [pltpu.make_async_copy(dest_ref, dest, sems.at[0]), pltpu.make_async_copy(particles_ref, staged, sems.at[1])]
    for copy in bring:
        copy.start()
    packed[...] = jnp.zeros_like(packed)
    me = lax.axis_index("tile")
    for copy in bring:
        copy.wait()

    def place(b, carry):
        target = dest[b]
        owner = lax.div(target, cap)
        step = owner ^ me if is_power(tiles) else lax.rem(owner + tiles - me, tiles)
        start = pl.multiple_of((step * cap + lax.rem(target, cap)) * floats, 8)
        packed[pl.ds(start, floats), :] = staged[b]
        return carry

    lax.fori_loop(0, staged.shape[0], place, 0, unroll=4)
    for k in range(tiles):
        for f in range(floats):
            value = packed[pl.ds(k * cap * floats + f, cap, stride=floats), :]
            if f < CORE:
                cores[k][f] = value
            else:
                rests[k][f - CORE] = value


def states_kernel(tiles, cap, steps, *refs):
    parts, (own_ref, moving_ref) = dict(zip(steps, refs)), refs[-2:]
    me = lax.axis_index("tile")
    for k in steps:
        rows = pl.ds(pl.multiple_of(source_tile(me, k, tiles) * cap, cap), cap)
        field = parts[k]
        for f in range(CORE):
            own_ref[f, rows, :] = field[f]
        mass = field[6]
        present = mass > 0
        for f in range(3):
            moving_ref[f, rows, :] = field[f] - CENTRE
        moving_ref[3, rows, :] = jnp.where(present, field[8], 1.0)
        scaled = jnp.where(present, mass * MASS_UNIT, 1.0)
        root = jnp.exp(jnp.log(scaled) * (-1.0 / 3.0))
        for _ in range(2):
            root = root * (4.0 - scaled * (root * root * root)) * (1.0 / 3.0)
        moving_ref[4, rows, :] = jnp.where(present, root, 0.0)
        for f in range(EARLY):
            moving_ref[5 + f, rows, :] = field[3 + f]


def store_far(far_ref, base, moving_ref, slots):
    def put(row, value):
        far_ref[pl.ds(base * DEPTH + row, slots, stride=DEPTH), :] = value

    place = [moving_ref[f] for f in range(3)]
    smooth, stretch = moving_ref[3], moving_ref[4]
    present = stretch > 0
    stretch = jnp.where(present, stretch, 1.0)
    square = stretch * stretch
    norm = 0.0
    for f in range(3):
        hi, mid, lo = split3(-2.0 * square * place[f])
        norm = norm + place[f] * place[f]
        put(f, hi)
        put(3 + f, hi)
        put(6 + f, hi)
        put(9 + f, mid)
        put(12 + f, lo)
    for row, value in enumerate(split3(jnp.where(present, square * norm, AWAY))):
        put(15 + row, value)
    s1, s2, s3 = split3(square)
    for row, value in enumerate((s1, s1, s1, s2, s2, s3)):
        put(18 + row, value)
    for row, value in enumerate(split3(0.25 * stretch * smooth)):
        put(24 + row, value)
    u1, u2 = split2(0.25 * stretch)
    for row, value in enumerate((u1, u1, u2, u2)):
        put(27 + row, value)
    put(31, jnp.zeros_like(stretch))


def store_far_dummy(far_ref, index):
    row = lax.broadcasted_iota(I32, (DEPTH, LANES), 0)
    far_ref[index * DEPTH : (index + 1) * DEPTH, :] = jnp.where(row == 15, AWAY, jnp.where(row == 24, 1.0, 0.0))


def store_near(near_ref, moving_ref, slots):
    near_ref[...] = jnp.zeros_like(near_ref)
    row = lax.broadcasted_iota(I32, (DEPTH, LANES), 0)
    start = 2 * slots * DEPTH
    near_ref[start : start + DEPTH, :] = jnp.where((row >= 15) & (row < 18), 1.0, 0.0)
    near_ref[start + DEPTH : start + 2 * DEPTH, :] = jnp.where((row >= 24) & (row < 27), 1.0, 0.0)

    def put(row, value, half=0):
        near_ref[pl.ds(half * DEPTH + row, slots, stride=2 * DEPTH), :] = value

    place = [moving_ref[f] for f in range(3)]
    norm = 0.0
    for f in range(3):
        hi, mid, lo = split3(place[f])
        norm = norm + place[f] * place[f]
        put(f, hi)
        put(3 + f, mid)
        put(6 + f, lo)
        put(9 + f, hi)
        put(12 + f, hi)
    ones = jnp.ones_like(norm)
    for row in range(3):
        put(15 + row, ones)
        put(24 + row, ones, 1)
    n1, n2, n3 = split3(norm)
    for row, value in enumerate((n1, n2, n3, n1, n2, n1)):
        put(18 + row, value)
    h1, h2 = split2(moving_ref[3])
    for row, value in enumerate((h1, h2, h1, h2)):
        put(27 + row, value, 1)


def pair_loop(plan, plan_ref, which, near_ref, far_ref, weight_ref, slope_ref):
    base = which * plan.length
    stored = plan.stored_base(plan_ref, which)

    def work(start, size):
        for u in range(size):
            word = plan_ref[base + start + u]
            far = far_ref[pl.ds(pl.multiple_of(plan.cand(word) * DEPTH, DEPTH), DEPTH), :]
            near = near_ref[pl.ds(pl.multiple_of(plan.slot(word) * (2 * DEPTH), DEPTH), 2 * DEPTH), :]
            near = jnp.concatenate([near[0:DEPTH], near[DEPTH : 2 * DEPTH]], axis=1)
            both = lax.dot_general(
                far.astype(BF16), near.astype(BF16), (((0,), (0,)), ((), ())), preferred_element_type=F32
            )
            squared = jnp.maximum(both[:, 0:LANES], 1e-20)
            inverse = pltpu.reciprocal(both[:, LANES : 2 * LANES], approx=True)
            remain = jnp.maximum(4.0 - squared * lax.rsqrt(squared) * inverse, 0.0)
            scaled = inverse * remain
            cubed = scaled * scaled * scaled
            weight = cubed * (remain * (5.0 - remain))
            weight_ref[plan.code(word)] = jnp.sum(weight.reshape(LANES // 8, 8, LANES), axis=0)
            slope_ref[stored + start + u] = cubed * (inverse * inverse)

    in_groups(plan, plan_ref, which, work)


def local_kernel(plan, plan_ref, moving_ref, near_ref, weight_ref, slope_ref, far_ref):
    slots = plan.slots
    store_near(near_ref, moving_ref, slots)
    store_far(far_ref, 0, moving_ref, slots)
    store_far_dummy(far_ref, slots)
    weight_ref[...] = jnp.zeros_like(weight_ref)
    pair_loop(plan, plan_ref, 0, near_ref, far_ref, weight_ref, slope_ref)


def first_kernel(plan, plan_ref, moving_ref, near_ref, weight_in_ref, slope_in_ref, weight_ref, slope_ref, far_ref):
    store_far(far_ref, 0, moving_ref, plan.slots)
    store_far_dummy(far_ref, plan.slots)
    pair_loop(plan, plan_ref, 1, near_ref, far_ref, weight_ref, slope_ref)


def second_kernel(plan, plan_ref, own_ref, moving_ref, near_ref, weight_in_ref, slope_in_ref,
                  density_ref, thermal_ref, weight_ref, slope_ref, far_ref):
    store_far(far_ref, 0, moving_ref, plan.slots)
    store_far_dummy(far_ref, plan.slots)
    pair_loop(plan, plan_ref, 2, near_ref, far_ref, weight_ref, slope_ref)
    for i in range(plan.slots):
        first = i << plan.entry_bits
        tile = weight_ref[first]
        for k in range(1, plan.width):
            tile = tile + weight_ref[first + k]
        density_ref[i : i + 1, :] = sum_rows(tile)[0:1, :]
    density = WEIGHT_FACTOR * density_ref[...]
    density_ref[...] = density
    safe = jnp.where(own_ref[6] > 0, density, 1.0)
    thermal_ref[0] = (ADIABATIC - 1.0) * density * own_ref[7] / (safe * safe)
    for f in range(EARLY, 3):
        thermal_ref[1 + f - EARLY] = own_ref[3 + f]


def store_fields(field_ref, base, moving_ref, thermal_ref, slots):
    def put(row, value):
        field_ref[pl.ds(base * FIELD_ROWS + row, slots, stride=FIELD_ROWS), :] = value

    stretch = moving_ref[4]
    square = stretch * stretch
    place = [moving_ref[f] for f in range(3)]
    speed = [moving_ref[5 + f] if f < EARLY else thermal_ref[1 + f - EARLY] for f in range(3)]
    dotted = place[0] * speed[0] + place[1] * speed[1] + place[2] * speed[2]
    plain = [square] + [square * value for value in place + speed + [dotted]]
    heavy = [thermal_ref[0] * value for value in plain[0:4]]
    for row, value in enumerate(plain):
        for part, piece in enumerate(split3(value)):
            put(8 * part + row, piece)
    for row, value in enumerate(heavy):
        for part, piece in enumerate(split3(value)):
            put(24 + 4 * part + row, piece)
        put(36 + row, jnp.zeros_like(value))


def store_field_dummy(field_ref, index):
    field_ref[index * FIELD_ROWS : (index + 1) * FIELD_ROWS, :] = jnp.zeros((FIELD_ROWS, LANES), F32)


def field_loop(plan, plan_ref, which, field_ref, slope_ref, sum_ref):
    base = which * plan.length
    stored = plan.stored_base(plan_ref, which)

    def work(start, size):
        for u in range(size):
            word = plan_ref[base + start + u]
            field = field_ref[pl.ds(pl.multiple_of(plan.cand(word) * FIELD_ROWS, 8), FIELD_ROWS), :].astype(BF16)
            slope = slope_ref[stored + start + u]
            hi = slope.astype(BF16)
            lo = (slope - hi.astype(F32)).astype(BF16)
            both = jnp.dot(
                jnp.concatenate([field, field], axis=1),
                jnp.concatenate([hi, lo], axis=0),
                preferred_element_type=F32,
            )
            code = plan.code(word)
            sum_ref[code, 0:8, :] = both[0:8] + both[8:16] + both[16:24]
            sum_ref[code, 8:16, :] = both[24:32] + both[32:40]

    in_groups(plan, plan_ref, which, work)


def hold_kernel(*refs):
    pass


def local_field_kernel(plan, plan_ref, moving_ref, thermal_ref, slope_ref, sum_ref, field_ref):
    store_fields(field_ref, 0, moving_ref, thermal_ref, plan.slots)
    store_field_dummy(field_ref, plan.slots)
    sum_ref[...] = jnp.zeros_like(sum_ref)
    field_loop(plan, plan_ref, 0, field_ref, slope_ref, sum_ref)


def first_field_kernel(plan, plan_ref, moving_ref, thermal_ref, slope_ref, sum_in_ref, sum_ref, field_ref):
    store_fields(field_ref, 0, moving_ref, thermal_ref, plan.slots)
    store_field_dummy(field_ref, plan.slots)
    field_loop(plan, plan_ref, 1, field_ref, slope_ref, sum_ref)


def final_kernel(plan, tiles, cap, floats, plan_ref, own_ref, moving_ref, second_ref, density_ref, thermal_ref,
                 second_thermal_ref, slope_ref, sum_in_ref, *refs):
    rests, (updated_ref, derived_ref, sum_ref, field_ref, total_ref) = refs[:tiles], refs[tiles:]
    slots = plan.slots
    store_fields(field_ref, 0, second_ref, second_thermal_ref, slots)
    store_field_dummy(field_ref, slots)
    me = lax.axis_index("tile")
    for k in range(tiles):
        base = pl.multiple_of(source_tile(me, k, tiles) * cap, cap)
        held = (own_ref[6, pl.ds(base, cap), :] > 0).astype(F32)
        for f in range(floats - CORE):
            updated_ref[pl.ds(base * floats + CORE + f, cap, stride=floats), :] = rests[k][f] * held
    field_loop(plan, plan_ref, 2, field_ref, slope_ref, sum_ref)
    for i in range(slots):
        first = i << plan.entry_bits
        tile = sum_ref[first]
        for k in range(1, plan.width):
            tile = tile + sum_ref[first + k]
        total_ref[16 * i : 16 * (i + 1), :] = tile

    def summed(row):
        return SLOPE_FACTOR * total_ref[pl.ds(row, slots, stride=16), :]

    plain = [summed(row) for row in range(8)]
    heavy = [summed(8 + row) + summed(12 + row) for row in range(4)]
    place = [moving_ref[f] for f in range(3)]
    speed = [own_ref[3 + f] for f in range(3)]
    ratio, density = thermal_ref[0], density_ref[...]
    accel, heating = [], plain[7]
    for f in range(3):
        spread = place[f] * plain[0] - plain[1 + f]
        accel.append(-(ratio * spread + (place[f] * heavy[0] - heavy[1 + f])))
        heating = heating + place[f] * (speed[f] * plain[0] - plain[4 + f]) - speed[f] * plain[1 + f]
    heating = ratio * heating
    present = (own_ref[6] > 0).astype(F32)
    fresh = {}
    for f in range(3):
        fresh[3 + f] = speed[f] + TIMESTEP * accel[f]
        fresh[f] = own_ref[f] + TIMESTEP * fresh[3 + f]
    fresh[6] = own_ref[6]
    fresh[7] = own_ref[7] + TIMESTEP * heating
    fresh[8] = own_ref[8]
    for f in range(CORE):
        updated_ref[pl.ds(f, slots, stride=floats), :] = fresh[f] * present
    for f, value in enumerate([density] + accel + [heating]):
        derived_ref[f] = value * present


def body(tiles, slabs, particles, dest_slot, neighbours, counts):
    bins, floats, lanes = particles.shape
    slots, width = neighbours.shape
    cap = slots // tiles
    plan = Plan(slots, width)
    packed = kernel_call(
        lambda *refs: pack_kernel(tiles, cap, floats, *refs),
        [("h", in_hbm(dest_slot)), ("h", in_hbm(particles))],
        [("v", (CORE, cap, lanes), F32)] * tiles + [("v", (floats - CORE, cap, lanes), F32)] * tiles,
        [
            pltpu.VMEM((slots * floats, lanes), F32),
            pltpu.VMEM((bins, floats, lanes), F32),
            pltpu.SMEM((bins,), I32),
            pltpu.SemaphoreType.DMA((2,)),
        ],
        1500,
        "pack",
    )
    packed, rests = packed[:tiles], packed[tiles:]

    def to_partner(array, step):
        return lax.ppermute(array, "tile", [(t, partner_tile(t, step, tiles)) for t in range(tiles)])

    (lists,) = kernel_call(
        lambda *refs: plan_kernel(plan, *refs),
        [("s", in_hbm(neighbours.T)), ("s", in_hbm(counts)), ("a", packed[0])],
        [("s", (plan.size,), I32)],
        [],
        2000,
        "plan",
    )
    parts = [packed[0]] + [to_partner(packed[k], k) for k in range(1, tiles)]
    state_outs = [("v", (CORE, slots, lanes), F32), ("v", (5 + EARLY, slots, lanes), F32)]
    far_steps = [k for k in range(tiles) if k != 1]
    own, moving = kernel_call(
        lambda *refs: states_kernel(tiles, cap, far_steps, *refs),
        [("v", parts[k]) for k in far_steps],
        state_outs,
        [],
        200,
        "far_states",
    )
    if tiles > 1:
        own, moving = kernel_call(
            lambda *refs: states_kernel(tiles, cap, [1], *refs),
            [("v", parts[1]), ("v", own), ("v", moving), ("a", lists)],
            state_outs,
            [],
            100,
            "near_states",
            {1: 0, 2: 1},
        )
    first_pairs = [(s, s ^ 1) for s in range(slabs)]
    second_pairs = [(s, (((s + 1) ^ 1) - 1) % slabs) for s in range(slabs)]

    def both_sides(array):
        second = lax.ppermute(array, "slab", second_pairs)
        first = lax.ppermute(array, "slab", first_pairs)
        return first, second

    first, second = both_sides(moving)
    weight_out = ("v", (plan.codes, 8, lanes), F32)
    slope_out = ("v", (plan.stored, lanes, lanes), F32)
    sum_out = ("v", (plan.codes, 16, lanes), F32)
    far_table = [pltpu.VMEM(((slots + 1) * DEPTH, lanes), F32)]
    field_table = [pltpu.VMEM(((slots + 1) * FIELD_ROWS, lanes), F32)]
    near, weights, slopes = kernel_call(
        lambda *refs: local_kernel(plan, *refs),
        [("s", lists), ("v", moving)],
        [("v", ((slots + 1) * 2 * DEPTH, lanes), F32), weight_out, slope_out],
        far_table,
        3500,
        "local",
    )
    weights, slopes = kernel_call(
        lambda *refs: first_kernel(plan, *refs),
        [("s", lists), ("v", first), ("v", near), ("v", weights), ("v", slopes)],
        [weight_out, slope_out],
        far_table,
        1500,
        "first",
        {3: 0, 4: 1},
    )
    density, thermal, weights, slopes = kernel_call(
        lambda *refs: second_kernel(plan, *refs),
        [("s", lists), ("v", own), ("v", second), ("v", near), ("v", weights), ("v", slopes)],
        [("v", (slots, lanes), F32), ("v", (4 - EARLY, slots, lanes), F32), weight_out, slope_out],
        far_table,
        2000,
        "second",
        {4: 2, 5: 3},
    )
    first_thermal, second_thermal = both_sides(thermal)
    later = kernel_call(
        hold_kernel,
        [("a", rest) for rest in rests[1:]] + [("a", thermal)],
        [("a", (floats - CORE, cap, lanes), F32)] * (tiles - 1),
        [],
        10,
        "hold",
        {k: k for k in range(tiles - 1)},
    )
    (sums,) = kernel_call(
        lambda *refs: local_field_kernel(plan, *refs),
        [("s", lists), ("v", moving), ("v", thermal), ("v", slopes)],
        [sum_out],
        field_table,
        1700,
        "local_fields",
    )
    rests = [rests[0]] + [to_partner(later[k - 1], k) for k in range(1, tiles)]
    (sums,) = kernel_call(
        lambda *refs: first_field_kernel(plan, *refs),
        [("s", lists), ("v", first), ("v", first_thermal), ("v", slopes), ("v", sums)],
        [sum_out],
        field_table,
        1000,
        "first_fields",
        {4: 0},
    )
    updated, derived, _ = kernel_call(
        lambda *refs: final_kernel(plan, tiles, cap, floats, *refs),
        [("s", lists), ("v", own), ("v", moving), ("v", second), ("v", density), ("v", thermal),
         ("v", second_thermal), ("v", slopes), ("v", sums)]
        + [("v", rest) for rest in rests],
        [("v", (slots * floats, lanes), F32), ("v", (5, slots, lanes), F32), sum_out],
        field_table + [pltpu.VMEM((slots * 16, lanes), F32)],
        2000,
        "final",
        {8: 2},
    )
    return updated.reshape(slots, floats, lanes), derived.transpose(1, 0, 2)


def solution(mesh):
    tiles, slabs = mesh.shape["tile"], mesh.shape["slab"]
    in_specs = (
        P(("slab", "tile"), None, None),
        P(("slab", "tile")),
        P(("slab", "tile"), None),
        P(("slab", "tile")),
    )
    out_specs = (P(("slab", "tile"), None, None), P(("slab", "tile"), None, None))
    return jax.shard_map(
        lambda *args: body(tiles, slabs, *args), mesh=mesh, in_specs=in_specs, out_specs=out_specs, check_vma=False
    )
```

```python
import math

import jax
import jax.numpy as jnp
from jax import lax
from jax.experimental import pallas as pl
from jax.experimental.pallas import tpu as pltpu
from jax.sharding import PartitionSpec as P

ADIABATIC = 5.0 / 3.0
TIMESTEP = 0.5
KERNEL_NORM = 21.0 / (16.0 * math.pi)
MASS_UNIT = 512.0
WEIGHT_FACTOR = 8.0 * KERNEL_NORM / MASS_UNIT / 4.0**7
SLOPE_FACTOR = -5.0 * 32.0 * KERNEL_NORM / MASS_UNIT / 4.0**8
CENTRE = 1.0
AWAY = 1.0e4
LANES = 128
LARGE_GROUPS = (((48, 40), (24, 16)), 16, 8)
GROUPS = (((24, 16),), 16, 8)
STEP = 8
EARLY = 1
CORE = 9
DEPTH = 32
FIELD_ROWS = 40

F32 = jnp.float32
BF16 = jnp.bfloat16
I32 = jnp.int32


def vmem_spec():
    return pl.BlockSpec(memory_space=pltpu.VMEM)


def smem_spec():
    return pl.BlockSpec(memory_space=pltpu.SMEM)


def hbm_spec():
    return pl.BlockSpec(memory_space=pltpu.HBM)


def any_spec():
    return pl.BlockSpec(memory_space=pl.ANY)


SPECS = {"s": smem_spec, "v": vmem_spec, "h": hbm_spec, "a": any_spec}


def in_hbm(array):
    return pltpu.with_memory_space_constraint(array, pltpu.HBM)


def kernel_call(kernel, ins, outs, scratch, nanoseconds, name, aliases=None):
    return pl.pallas_call(
        kernel,
        out_shape=[
            pltpu.SMEM(shape, dtype) if memory == "s" else jax.ShapeDtypeStruct(shape, dtype)
            for memory, shape, dtype in outs
        ],
        in_specs=[SPECS[memory]() for memory, _ in ins],
        out_specs=[SPECS[memory]() for memory, _, _ in outs],
        scratch_shapes=scratch,
        input_output_aliases=aliases or {},
        compiler_params=pltpu.CompilerParams(vmem_limit_bytes=32 * 1024 * 1024),
        cost_estimate=pl.CostEstimate(flops=0, bytes_accessed=3000 * nanoseconds, transcendentals=0),
        name=name,
    )(*[array for _, array in ins])


def is_power(count):
    return count & (count - 1) == 0


def partner_tile(index, step, count):
    return index ^ step if is_power(count) else (index + step) % count


def source_tile(index, step, count):
    return index ^ step if is_power(count) else lax.rem(index + count - step, count)


def rounded(value):
    return value.astype(BF16).astype(F32)


def split2(value):
    hi = rounded(value)
    return hi, rounded(value - hi)


def split3(value):
    hi = rounded(value)
    mid = rounded(value - hi)
    return hi, mid, rounded(value - hi - mid)


def sum_rows(tile):
    tile = tile + pltpu.roll(tile, 4, 0)
    tile = tile + pltpu.roll(tile, 2, 0)
    return tile + pltpu.roll(tile, 1, 0)


class Plan:
    def __init__(self, slots, width):
        self.slots, self.width = slots, width
        self.entry_bits = (width - 1).bit_length()
        self.cand_bits = slots.bit_length()
        self.length = slots * width + STEP
        self.codes = (slots + 1) << self.entry_bits
        self.counts = 3 * self.length
        self.size = 3 * self.length + 8
        self.stored = slots * width + 4 * STEP
        self.dummy = self.word(slots, 0, slots)

    def word(self, slot, entry, cand):
        return (((slot << self.entry_bits) + entry) << self.cand_bits) + cand

    def code(self, word):
        return word >> self.cand_bits

    def slot(self, word):
        return word >> (self.cand_bits + self.entry_bits)

    def cand(self, word):
        return word & ((1 << self.cand_bits) - 1)

    def stored_base(self, ref, which):
        base = 0
        for k in range(which):
            base = base + lax.div(ref[self.counts + k] + STEP - 1, STEP) * STEP
        return base


def in_groups(plan, plan_ref, which, groups, work):
    loops, medium, small = groups
    start, count = 0, plan_ref[plan.counts + which]
    for size, left in loops:

        def step(g, first, size=size):
            work(first, size)
            return first + size

        number = lax.div(jnp.maximum(count - start - left + size - 1, 0), size)
        start = lax.fori_loop(0, number, step, start)

    @pl.when(count - start > small)
    def _():
        work(start, medium)

    @pl.when((count > start) & (count - start <= small))
    def _():
        work(start, small)


def plan_kernel(plan, neighbours_ref, counts_ref, after_ref, plan_ref, near_ref, weight_ref):
    slots = plan.slots
    entries = 1 << plan.entry_bits
    upper_first = lax.rem(lax.axis_index("slab"), 2) == 0
    low = jnp.where(upper_first, 2, 1)
    high = 3 - low

    def fill(i, totals):
        used = counts_ref[i]
        for k in range(plan.width):
            n = neighbours_ref[k, i]
            region = lax.div(n, slots)
            which = jnp.where(region == 1, 0, jnp.where(region == 0, low, high))
            word = plan.word(i, k, n - region * slots)
            kept = []
            for w in range(3):
                plan_ref[w * plan.length + totals[w]] = word
                kept.append(totals[w] + ((k < used) & (which == w)).astype(I32))
            totals = tuple(kept)
        rows = pl.ds(pl.multiple_of(i * (2 * DEPTH), 2 * DEPTH), 2 * DEPTH)
        near_ref[rows, :] = jnp.zeros((2 * DEPTH, LANES), F32)
        weight_ref[pl.ds(i * entries, entries)] = jnp.zeros((entries, 8, LANES), F32)
        return totals

    totals = lax.fori_loop(0, slots, fill, (jnp.int32(0),) * 3, unroll=4)
    for w in range(3):
        for k in range(STEP):
            plan_ref[w * plan.length + totals[w] + k] = plan.dummy
        plan_ref[plan.counts + w] = totals[w]


def pack_kernel(tiles, cap, floats, dest_ref, particles_ref, *refs):
    cores, rests, (packed, staged, dest, sems) = refs[:tiles], refs[tiles : 2 * tiles], refs[2 * tiles :]
    pieces = sems.shape[0] - 1
    bins = staged.shape[0] // pieces
    bring = [pltpu.make_async_copy(dest_ref, dest, sems.at[pieces])]
    for p in range(pieces):
        part = pl.ds(p * bins, bins)
        bring.append(pltpu.make_async_copy(particles_ref.at[part], staged.at[part], sems.at[p]))
    for copy in bring:
        copy.start()
    packed[...] = jnp.zeros_like(packed)
    me = lax.axis_index("tile")
    for copy in bring:
        copy.wait()

    def place(b, carry):
        target = dest[b]
        owner = lax.div(target, cap)
        step = owner ^ me if is_power(tiles) else lax.rem(owner + tiles - me, tiles)
        start = pl.multiple_of((step * cap + lax.rem(target, cap)) * floats, 8)
        packed[pl.ds(start, floats), :] = staged[b]
        return carry

    lax.fori_loop(0, staged.shape[0], place, 0, unroll=4)
    for k in range(tiles):
        for f in range(floats):
            value = packed[pl.ds(k * cap * floats + f, cap, stride=floats), :]
            if f < CORE:
                cores[k][f] = value
            else:
                rests[k][f - CORE] = value


def states_kernel(tiles, cap, steps, *refs):
    parts, (own_ref, moving_ref) = dict(zip(steps, refs)), refs[-2:]
    me = lax.axis_index("tile")
    for k in steps:
        rows = pl.ds(pl.multiple_of(source_tile(me, k, tiles) * cap, cap), cap)
        field = parts[k]
        for f in range(CORE):
            own_ref[f, rows, :] = field[f]
        mass = field[6]
        present = mass > 0
        for f in range(3):
            moving_ref[f, rows, :] = field[f] - CENTRE
        moving_ref[3, rows, :] = jnp.where(present, field[8], 1.0)
        scaled = jnp.where(present, mass * MASS_UNIT, 1.0)
        root = jnp.exp(jnp.log(scaled) * (-1.0 / 3.0))
        for _ in range(2):
            root = root * (4.0 - scaled * (root * root * root)) * (1.0 / 3.0)
        moving_ref[4, rows, :] = jnp.where(present, root, 0.0)
        for f in range(EARLY):
            moving_ref[5 + f, rows, :] = field[3 + f]


def store_far(far_ref, base, moving_ref, slots):
    def put(row, value):
        far_ref[pl.ds(base * DEPTH + row, slots, stride=DEPTH), :] = value

    place = [moving_ref[f] for f in range(3)]
    smooth, stretch = moving_ref[3], moving_ref[4]
    present = stretch > 0
    stretch = jnp.where(present, stretch, 1.0)
    square = stretch * stretch
    norm = 0.0
    for f in range(3):
        hi, mid, lo = split3(-2.0 * square * place[f])
        norm = norm + place[f] * place[f]
        put(f, hi)
        put(3 + f, hi)
        put(6 + f, hi)
        put(9 + f, mid)
        put(12 + f, lo)
    for row, value in enumerate(split3(jnp.where(present, square * norm, AWAY))):
        put(15 + row, value)
    s1, s2, s3 = split3(square)
    for row, value in enumerate((s1, s1, s1, s2, s2, s3)):
        put(18 + row, value)
    for row, value in enumerate(split3(0.25 * stretch * smooth)):
        put(24 + row, value)
    u1, u2 = split2(0.25 * stretch)
    for row, value in enumerate((u1, u1, u2, u2)):
        put(27 + row, value)
    put(31, jnp.zeros_like(stretch))


def store_far_dummy(far_ref, index):
    row = lax.broadcasted_iota(I32, (DEPTH, LANES), 0)
    far_ref[index * DEPTH : (index + 1) * DEPTH, :] = jnp.where(row == 15, AWAY, jnp.where(row == 24, 1.0, 0.0))


def store_near(near_ref, moving_ref, slots):
    row = lax.broadcasted_iota(I32, (DEPTH, LANES), 0)
    start = 2 * slots * DEPTH
    near_ref[start : start + DEPTH, :] = jnp.where((row >= 15) & (row < 18), 1.0, 0.0)
    near_ref[start + DEPTH : start + 2 * DEPTH, :] = jnp.where((row >= 24) & (row < 27), 1.0, 0.0)

    def put(row, value, half=0):
        near_ref[pl.ds(half * DEPTH + row, slots, stride=2 * DEPTH), :] = value

    place = [moving_ref[f] for f in range(3)]
    norm = 0.0
    for f in range(3):
        hi, mid, lo = split3(place[f])
        norm = norm + place[f] * place[f]
        put(f, hi)
        put(3 + f, mid)
        put(6 + f, lo)
        put(9 + f, hi)
        put(12 + f, hi)
    ones = jnp.ones_like(norm)
    for row in range(3):
        put(15 + row, ones)
        put(24 + row, ones, 1)
    n1, n2, n3 = split3(norm)
    for row, value in enumerate((n1, n2, n3, n1, n2, n1)):
        put(18 + row, value)
    h1, h2 = split2(moving_ref[3])
    for row, value in enumerate((h1, h2, h1, h2)):
        put(27 + row, value, 1)


def pair_loop(plan, plan_ref, which, groups, near_ref, far_ref, weight_ref, slope_ref):
    base = which * plan.length
    stored = plan.stored_base(plan_ref, which)

    def work(start, size):
        for u in range(size):
            word = plan_ref[base + start + u]
            far = far_ref[pl.ds(pl.multiple_of(plan.cand(word) * DEPTH, DEPTH), DEPTH), :]
            near = near_ref[pl.ds(pl.multiple_of(plan.slot(word) * (2 * DEPTH), DEPTH), 2 * DEPTH), :]
            near = jnp.concatenate([near[0:DEPTH], near[DEPTH : 2 * DEPTH]], axis=1)
            both = lax.dot_general(
                far.astype(BF16), near.astype(BF16), (((0,), (0,)), ((), ())), preferred_element_type=F32
            )
            squared = jnp.maximum(both[:, 0:LANES], 1e-20)
            inverse = pltpu.reciprocal(both[:, LANES : 2 * LANES], approx=True)
            remain = jnp.maximum(4.0 - squared * lax.rsqrt(squared) * inverse, 0.0)
            scaled = inverse * remain
            cubed = scaled * scaled * scaled
            weight = cubed * (remain * (5.0 - remain))
            weight_ref[plan.code(word)] = jnp.sum(weight.reshape(LANES // 8, 8, LANES), axis=0)
            slope_ref[stored + start + u] = cubed * (inverse * inverse)

    in_groups(plan, plan_ref, which, groups, work)


def local_kernel(plan, plan_ref, moving_ref, near_in_ref, weight_in_ref, near_ref, weight_ref, slope_ref, far_ref):
    slots = plan.slots
    store_near(near_ref, moving_ref, slots)
    store_far(far_ref, 0, moving_ref, slots)
    store_far_dummy(far_ref, slots)
    pair_loop(plan, plan_ref, 0, LARGE_GROUPS, near_ref, far_ref, weight_ref, slope_ref)


def first_kernel(plan, plan_ref, moving_ref, near_ref, weight_in_ref, slope_in_ref, weight_ref, slope_ref, far_ref):
    store_far(far_ref, 0, moving_ref, plan.slots)
    store_far_dummy(far_ref, plan.slots)
    pair_loop(plan, plan_ref, 1, GROUPS, near_ref, far_ref, weight_ref, slope_ref)


def second_kernel(plan, plan_ref, own_ref, moving_ref, near_ref, weight_in_ref, slope_in_ref,
                  density_ref, thermal_ref, weight_ref, slope_ref, far_ref):
    store_far(far_ref, 0, moving_ref, plan.slots)
    store_far_dummy(far_ref, plan.slots)
    pair_loop(plan, plan_ref, 2, GROUPS, near_ref, far_ref, weight_ref, slope_ref)
    for i in range(plan.slots):
        first = i << plan.entry_bits
        tile = weight_ref[first]
        for k in range(1, plan.width):
            tile = tile + weight_ref[first + k]
        density_ref[i : i + 1, :] = sum_rows(tile)[0:1, :]
    density = WEIGHT_FACTOR * density_ref[...]
    density_ref[...] = density
    safe = jnp.where(own_ref[6] > 0, density, 1.0)
    thermal_ref[0] = (ADIABATIC - 1.0) * density * own_ref[7] / (safe * safe)
    for f in range(EARLY, 3):
        thermal_ref[1 + f - EARLY] = own_ref[3 + f]


def store_fields(field_ref, base, moving_ref, thermal_ref, slots):
    def put(row, value):
        field_ref[pl.ds(base * FIELD_ROWS + row, slots, stride=FIELD_ROWS), :] = value

    stretch = moving_ref[4]
    square = stretch * stretch
    place = [moving_ref[f] for f in range(3)]
    speed = [moving_ref[5 + f] if f < EARLY else thermal_ref[1 + f - EARLY] for f in range(3)]
    dotted = place[0] * speed[0] + place[1] * speed[1] + place[2] * speed[2]
    plain = [square] + [square * value for value in place + speed + [dotted]]
    heavy = [thermal_ref[0] * value for value in plain[0:4]]
    for row, value in enumerate(plain):
        for part, piece in enumerate(split3(value)):
            put(8 * part + row, piece)
    for row, value in enumerate(heavy):
        for part, piece in enumerate(split3(value)):
            put(24 + 4 * part + row, piece)
        put(36 + row, jnp.zeros_like(value))


def store_field_dummy(field_ref, index):
    field_ref[index * FIELD_ROWS : (index + 1) * FIELD_ROWS, :] = jnp.zeros((FIELD_ROWS, LANES), F32)


def field_loop(plan, plan_ref, which, field_ref, slope_ref, sum_ref):
    base = which * plan.length
    stored = plan.stored_base(plan_ref, which)

    def work(start, size):
        for u in range(size):
            word = plan_ref[base + start + u]
            field = field_ref[pl.ds(pl.multiple_of(plan.cand(word) * FIELD_ROWS, 8), FIELD_ROWS), :].astype(BF16)
            slope = slope_ref[stored + start + u]
            hi = slope.astype(BF16)
            lo = (slope - hi.astype(F32)).astype(BF16)
            both = jnp.dot(
                jnp.concatenate([field, field], axis=1),
                jnp.concatenate([hi, lo], axis=0),
                preferred_element_type=F32,
            )
            code = plan.code(word)
            sum_ref[code, 0:8, :] = both[0:8] + both[8:16] + both[16:24]
            sum_ref[code, 8:16, :] = both[24:32] + both[32:40]

    in_groups(plan, plan_ref, which, GROUPS, work)


def hold_kernel(*refs):
    pass


def local_field_kernel(plan, plan_ref, moving_ref, thermal_ref, slope_ref, sum_ref, field_ref):
    store_fields(field_ref, 0, moving_ref, thermal_ref, plan.slots)
    store_field_dummy(field_ref, plan.slots)
    sum_ref[...] = jnp.zeros_like(sum_ref)
    field_loop(plan, plan_ref, 0, field_ref, slope_ref, sum_ref)


def first_field_kernel(plan, plan_ref, moving_ref, thermal_ref, slope_ref, sum_in_ref, sum_ref, field_ref):
    store_fields(field_ref, 0, moving_ref, thermal_ref, plan.slots)
    store_field_dummy(field_ref, plan.slots)
    field_loop(plan, plan_ref, 1, field_ref, slope_ref, sum_ref)


def final_kernel(plan, tiles, cap, floats, plan_ref, own_ref, moving_ref, second_ref, density_ref, thermal_ref,
                 second_thermal_ref, slope_ref, sum_in_ref, *refs):
    rests, (updated_ref, derived_ref, sum_ref, field_ref, total_ref) = refs[:tiles], refs[tiles:]
    slots = plan.slots
    store_fields(field_ref, 0, second_ref, second_thermal_ref, slots)
    store_field_dummy(field_ref, slots)
    me = lax.axis_index("tile")
    for k in range(tiles):
        base = pl.multiple_of(source_tile(me, k, tiles) * cap, cap)
        held = (own_ref[6, pl.ds(base, cap), :] > 0).astype(F32)
        for f in range(floats - CORE):
            updated_ref[pl.ds(base * floats + CORE + f, cap, stride=floats), :] = rests[k][f] * held
    field_loop(plan, plan_ref, 2, field_ref, slope_ref, sum_ref)
    for i in range(slots):
        first = i << plan.entry_bits
        tile = sum_ref[first]
        for k in range(1, plan.width):
            tile = tile + sum_ref[first + k]
        total_ref[16 * i : 16 * (i + 1), :] = tile

    def summed(row):
        return SLOPE_FACTOR * total_ref[pl.ds(row, slots, stride=16), :]

    plain = [summed(row) for row in range(8)]
    heavy = [summed(8 + row) + summed(12 + row) for row in range(4)]
    place = [moving_ref[f] for f in range(3)]
    speed = [own_ref[3 + f] for f in range(3)]
    ratio, density = thermal_ref[0], density_ref[...]
    accel, heating = [], plain[7]
    for f in range(3):
        spread = place[f] * plain[0] - plain[1 + f]
        accel.append(-(ratio * spread + (place[f] * heavy[0] - heavy[1 + f])))
        heating = heating + place[f] * (speed[f] * plain[0] - plain[4 + f]) - speed[f] * plain[1 + f]
    heating = ratio * heating
    present = (own_ref[6] > 0).astype(F32)
    fresh = {}
    for f in range(3):
        fresh[3 + f] = speed[f] + TIMESTEP * accel[f]
        fresh[f] = own_ref[f] + TIMESTEP * fresh[3 + f]
    fresh[6] = own_ref[6]
    fresh[7] = own_ref[7] + TIMESTEP * heating
    fresh[8] = own_ref[8]
    for f in range(CORE):
        updated_ref[pl.ds(f, slots, stride=floats), :] = fresh[f] * present
    for f, value in enumerate([density] + accel + [heating]):
        derived_ref[f] = value * present


def body(tiles, slabs, particles, dest_slot, neighbours, counts):
    bins, floats, lanes = particles.shape
    slots, width = neighbours.shape
    cap = slots // tiles
    plan = Plan(slots, width)
    packed = kernel_call(
        lambda *refs: pack_kernel(tiles, cap, floats, *refs),
        [("h", in_hbm(dest_slot)), ("h", in_hbm(particles))],
        [("v", (CORE, cap, lanes), F32)] * tiles + [("v", (floats - CORE, cap, lanes), F32)] * tiles,
        [
            pltpu.VMEM((slots * floats, lanes), F32),
            pltpu.VMEM((bins, floats, lanes), F32),
            pltpu.SMEM((bins,), I32),
            pltpu.SemaphoreType.DMA((9 if bins % 8 == 0 else 2,)),
        ],
        1500,
        "pack",
    )
    packed, rests = packed[:tiles], packed[tiles:]

    def to_partner(array, step):
        return lax.ppermute(array, "tile", [(t, partner_tile(t, step, tiles)) for t in range(tiles)])

    near_out = ("v", ((slots + 1) * 2 * DEPTH, lanes), F32)
    weight_out = ("v", (plan.codes, 8, lanes), F32)
    lists, near, weights = kernel_call(
        lambda *refs: plan_kernel(plan, *refs),
        [("s", in_hbm(neighbours.T)), ("s", in_hbm(counts)), ("a", packed[0])],
        [("s", (plan.size,), I32), near_out, weight_out],
        [],
        2000,
        "plan",
    )
    parts = [packed[0]] + [to_partner(packed[k], k) for k in range(1, tiles)]
    state_outs = [("v", (CORE, slots, lanes), F32), ("v", (5 + EARLY, slots, lanes), F32)]
    far_steps = [k for k in range(tiles) if k != 1]
    own, moving = kernel_call(
        lambda *refs: states_kernel(tiles, cap, far_steps, *refs),
        [("v", parts[k]) for k in far_steps],
        state_outs,
        [],
        200,
        "far_states",
    )
    if tiles > 1:
        own, moving = kernel_call(
            lambda *refs: states_kernel(tiles, cap, [1], *refs),
            [("v", parts[1]), ("v", own), ("v", moving), ("a", lists)],
            state_outs,
            [],
            100,
            "near_states",
            {1: 0, 2: 1},
        )
    first_pairs = [(s, s ^ 1) for s in range(slabs)]
    second_pairs = [(s, (((s + 1) ^ 1) - 1) % slabs) for s in range(slabs)]

    def both_sides(array):
        second = lax.ppermute(array, "slab", second_pairs)
        first = lax.ppermute(array, "slab", first_pairs)
        return first, second

    first, second = both_sides(moving)
    slope_out = ("v", (plan.stored, lanes, lanes), F32)
    sum_out = ("v", (plan.codes, 16, lanes), F32)
    far_table = [pltpu.VMEM(((slots + 1) * DEPTH, lanes), F32)]
    field_table = [pltpu.VMEM(((slots + 1) * FIELD_ROWS, lanes), F32)]
    near, weights, slopes = kernel_call(
        lambda *refs: local_kernel(plan, *refs),
        [("s", lists), ("v", moving), ("v", near), ("v", weights)],
        [near_out, weight_out, slope_out],
        far_table,
        3500,
        "local",
        {2: 0, 3: 1},
    )
    weights, slopes = kernel_call(
        lambda *refs: first_kernel(plan, *refs),
        [("s", lists), ("v", first), ("v", near), ("v", weights), ("v", slopes)],
        [weight_out, slope_out],
        far_table,
        1500,
        "first",
        {3: 0, 4: 1},
    )
    density, thermal, weights, slopes = kernel_call(
        lambda *refs: second_kernel(plan, *refs),
        [("s", lists), ("v", own), ("v", second), ("v", near), ("v", weights), ("v", slopes)],
        [("v", (slots, lanes), F32), ("v", (4 - EARLY, slots, lanes), F32), weight_out, slope_out],
        far_table,
        2000,
        "second",
        {4: 2, 5: 3},
    )
    first_thermal, second_thermal = both_sides(thermal)
    later = kernel_call(
        hold_kernel,
        [("a", rest) for rest in rests[1:]] + [("a", thermal)],
        [("a", (floats - CORE, cap, lanes), F32)] * (tiles - 1),
        [],
        10,
        "hold",
        {k: k for k in range(tiles - 1)},
    )
    (sums,) = kernel_call(
        lambda *refs: local_field_kernel(plan, *refs),
        [("s", lists), ("v", moving), ("v", thermal), ("v", slopes)],
        [sum_out],
        field_table,
        1700,
        "local_fields",
    )
    rests = [rests[0]] + [to_partner(later[k - 1], k) for k in range(1, tiles)]
    (sums,) = kernel_call(
        lambda *refs: first_field_kernel(plan, *refs),
        [("s", lists), ("v", first), ("v", first_thermal), ("v", slopes), ("v", sums)],
        [sum_out],
        field_table,
        1000,
        "first_fields",
        {4: 0},
    )
    updated, derived, _ = kernel_call(
        lambda *refs: final_kernel(plan, tiles, cap, floats, *refs),
        [("s", lists), ("v", own), ("v", moving), ("v", second), ("v", density), ("v", thermal),
         ("v", second_thermal), ("v", slopes), ("v", sums)]
        + [("v", rest) for rest in rests],
        [("v", (slots * floats, lanes), F32), ("v", (5, slots, lanes), F32), sum_out],
        field_table + [pltpu.VMEM((slots * 16, lanes), F32)],
        2000,
        "final",
        {8: 2},
    )
    return updated.reshape(slots, floats, lanes), derived.transpose(1, 0, 2)


def solution(mesh):
    tiles, slabs = mesh.shape["tile"], mesh.shape["slab"]
    in_specs = (
        P(("slab", "tile"), None, None),
        P(("slab", "tile")),
        P(("slab", "tile"), None),
        P(("slab", "tile")),
    )
    out_specs = (P(("slab", "tile"), None, None), P(("slab", "tile"), None, None))
    return jax.shard_map(
        lambda *args: body(tiles, slabs, *args), mesh=mesh, in_specs=in_specs, out_specs=out_specs, check_vma=False
    )
```

```python
import math

import jax
import jax.numpy as jnp
from jax import lax
from jax.experimental import pallas as pl
from jax.experimental.pallas import tpu as pltpu
from jax.sharding import PartitionSpec as P

ADIABATIC = 5.0 / 3.0
TIMESTEP = 0.5
KERNEL_NORM = 21.0 / (16.0 * math.pi)
MASS_UNIT = 512.0
WEIGHT_FACTOR = 8.0 * KERNEL_NORM / MASS_UNIT / 4.0**7
SLOPE_FACTOR = -5.0 * 32.0 * KERNEL_NORM / MASS_UNIT / 4.0**8
CENTRE = 1.0
AWAY = 1.0e4
LANES = 128
LARGE_GROUPS = (((48, 40), (24, 16)), (16, 8))
GROUPS = (((24, 16),), (16, 8))
STEP = 8
EARLY = 1
CORE = 9
DEPTH = 32
FIELD_ROWS = 40

F32 = jnp.float32
BF16 = jnp.bfloat16
I32 = jnp.int32


def vmem_spec():
    return pl.BlockSpec(memory_space=pltpu.VMEM)


def smem_spec():
    return pl.BlockSpec(memory_space=pltpu.SMEM)


def hbm_spec():
    return pl.BlockSpec(memory_space=pltpu.HBM)


def any_spec():
    return pl.BlockSpec(memory_space=pl.ANY)


SPECS = {"s": smem_spec, "v": vmem_spec, "h": hbm_spec, "a": any_spec}


def in_hbm(array):
    return pltpu.with_memory_space_constraint(array, pltpu.HBM)


def kernel_call(kernel, ins, outs, scratch, nanoseconds, name, aliases=None):
    return pl.pallas_call(
        kernel,
        out_shape=[
            pltpu.SMEM(shape, dtype) if memory == "s" else jax.ShapeDtypeStruct(shape, dtype)
            for memory, shape, dtype in outs
        ],
        in_specs=[SPECS[memory]() for memory, _ in ins],
        out_specs=[SPECS[memory]() for memory, _, _ in outs],
        scratch_shapes=scratch,
        input_output_aliases=aliases or {},
        compiler_params=pltpu.CompilerParams(vmem_limit_bytes=32 * 1024 * 1024),
        cost_estimate=pl.CostEstimate(flops=0, bytes_accessed=3000 * nanoseconds, transcendentals=0),
        name=name,
    )(*[array for _, array in ins])


def is_power(count):
    return count & (count - 1) == 0


def partner_tile(index, step, count):
    return index ^ step if is_power(count) else (index + step) % count


def source_tile(index, step, count):
    return index ^ step if is_power(count) else lax.rem(index + count - step, count)


def rounded(value):
    return value.astype(BF16).astype(F32)


def split2(value):
    hi = rounded(value)
    return hi, rounded(value - hi)


def split3(value):
    hi = rounded(value)
    mid = rounded(value - hi)
    return hi, mid, rounded(value - hi - mid)


def sum_rows(tile):
    tile = tile + pltpu.roll(tile, 4, 0)
    tile = tile + pltpu.roll(tile, 2, 0)
    return tile + pltpu.roll(tile, 1, 0)


class Plan:
    def __init__(self, slots, width):
        self.slots, self.width = slots, width
        self.entry_bits = (width - 1).bit_length()
        self.cand_bits = slots.bit_length()
        self.length = slots * width + STEP
        self.codes = (slots + 1) << self.entry_bits
        self.counts = 3 * self.length
        self.size = 3 * self.length + 8
        self.stored = slots * width + 4 * STEP
        self.dummy = self.word(slots, 0, slots)

    def word(self, slot, entry, cand):
        return (((slot << self.entry_bits) + entry) << self.cand_bits) + cand

    def code(self, word):
        return word >> self.cand_bits

    def slot(self, word):
        return word >> (self.cand_bits + self.entry_bits)

    def cand(self, word):
        return word & ((1 << self.cand_bits) - 1)

    def stored_base(self, ref, which):
        base = 0
        for k in range(which):
            base = base + lax.div(ref[self.counts + k] + STEP - 1, STEP) * STEP
        return base


def in_groups(plan, plan_ref, which, groups, work):
    loops, tails = groups
    start, count = 0, plan_ref[plan.counts + which]
    for size, left in loops:

        def step(g, first, size=size):
            work(first, size)
            return first + size

        number = lax.div(jnp.maximum(count - start - left + size - 1, 0), size)
        start = lax.fori_loop(0, number, step, start)
    rest = count - start
    for size, below in zip(tails, tails[1:] + (0,)):

        @pl.when((rest <= size) & (rest > below))
        def _(size=size):
            work(start, size)


def plan_kernel(plan, neighbours_ref, counts_ref, after_ref, plan_ref, weight_ref):
    slots = plan.slots
    entries = 1 << plan.entry_bits
    upper_first = lax.rem(lax.axis_index("slab"), 2) == 0
    low = jnp.where(upper_first, 2, 1)
    high = 3 - low

    def fill(i, totals):
        used = counts_ref[i]
        for k in range(plan.width):
            n = neighbours_ref[k, i]
            region = lax.div(n, slots)
            which = jnp.where(region == 1, 0, jnp.where(region == 0, low, high))
            word = plan.word(i, k, n - region * slots)
            kept = []
            for w in range(3):
                plan_ref[w * plan.length + totals[w]] = word
                kept.append(totals[w] + ((k < used) & (which == w)).astype(I32))
            totals = tuple(kept)
        weight_ref[pl.ds(i * entries, entries)] = jnp.zeros((entries, 8, LANES), F32)
        return totals

    totals = lax.fori_loop(0, slots, fill, (jnp.int32(0),) * 3, unroll=4)
    for w in range(3):
        for k in range(STEP):
            plan_ref[w * plan.length + totals[w] + k] = plan.dummy
        plan_ref[plan.counts + w] = totals[w]


def pack_kernel(tiles, cap, floats, dest_ref, particles_ref, *refs):
    cores, rests, (packed, staged, dest, sems) = refs[:tiles], refs[tiles : 2 * tiles], refs[2 * tiles :]
    pieces = sems.shape[0] - 1
    bins = staged.shape[0] // pieces
    bring = [pltpu.make_async_copy(dest_ref, dest, sems.at[pieces])]
    for p in range(pieces):
        part = pl.ds(p * bins, bins)
        bring.append(pltpu.make_async_copy(particles_ref.at[part], staged.at[part], sems.at[p]))
    for copy in bring:
        copy.start()
    packed[...] = jnp.zeros_like(packed)
    me = lax.axis_index("tile")
    for copy in bring:
        copy.wait()

    def place(b, carry):
        target = dest[b]
        owner = lax.div(target, cap)
        step = owner ^ me if is_power(tiles) else lax.rem(owner + tiles - me, tiles)
        start = pl.multiple_of((step * cap + lax.rem(target, cap)) * floats, 8)
        packed[pl.ds(start, floats), :] = staged[b]
        return carry

    lax.fori_loop(0, staged.shape[0], place, 0, unroll=4)
    for k in range(tiles):
        for f in range(floats):
            value = packed[pl.ds(k * cap * floats + f, cap, stride=floats), :]
            if f < CORE:
                cores[k][f] = value
            else:
                rests[k][f - CORE] = value


def states_kernel(tiles, cap, steps, *refs):
    parts, (own_ref, moving_ref) = dict(zip(steps, refs)), refs[-2:]
    me = lax.axis_index("tile")
    for k in steps:
        rows = pl.ds(pl.multiple_of(source_tile(me, k, tiles) * cap, cap), cap)
        field = parts[k]
        for f in range(CORE):
            own_ref[f, rows, :] = field[f]
        mass = field[6]
        present = mass > 0
        for f in range(3):
            moving_ref[f, rows, :] = field[f] - CENTRE
        moving_ref[3, rows, :] = jnp.where(present, field[8], 1.0)
        scaled = jnp.where(present, mass * MASS_UNIT, 1.0)
        root = jnp.exp(jnp.log(scaled) * (-1.0 / 3.0))
        for _ in range(2):
            root = root * (4.0 - scaled * (root * root * root)) * (1.0 / 3.0)
        moving_ref[4, rows, :] = jnp.where(present, root, 0.0)
        for f in range(EARLY):
            moving_ref[5 + f, rows, :] = field[3 + f]


def slot_major(rows):
    slots, lanes = rows[0].shape
    return jnp.swapaxes(jnp.stack(rows, axis=0), 0, 1).reshape(slots * len(rows), lanes)


def store_far(far_ref, moving_ref, slots):
    place = [moving_ref[f] for f in range(3)]
    smooth, stretch = moving_ref[3], moving_ref[4]
    present = stretch > 0
    stretch = jnp.where(present, stretch, 1.0)
    square = stretch * stretch
    norm = 0.0
    rows = [None] * DEPTH
    for f in range(3):
        hi, mid, lo = split3(-2.0 * square * place[f])
        norm = norm + place[f] * place[f]
        rows[f : 15 : 3] = [hi, hi, hi, mid, lo]
    rows[15:18] = split3(jnp.where(present, square * norm, AWAY))
    s1, s2, s3 = split3(square)
    rows[18:24] = [s1, s1, s1, s2, s2, s3]
    rows[24:27] = split3(0.25 * stretch * smooth)
    u1, u2 = split2(0.25 * stretch)
    rows[27:32] = [u1, u1, u2, u2, jnp.zeros_like(u1)]
    far_ref[0 : slots * DEPTH, :] = slot_major(rows)


def store_far_dummy(far_ref, index):
    row = lax.broadcasted_iota(I32, (DEPTH, LANES), 0)
    far_ref[index * DEPTH : (index + 1) * DEPTH, :] = jnp.where(row == 15, AWAY, jnp.where(row == 24, 1.0, 0.0))


def store_near(near_ref, moving_ref, slots):
    row = lax.broadcasted_iota(I32, (DEPTH, LANES), 0)
    start = 2 * slots * DEPTH
    near_ref[start : start + DEPTH, :] = jnp.where((row >= 15) & (row < 18), 1.0, 0.0)
    near_ref[start + DEPTH : start + 2 * DEPTH, :] = jnp.where((row >= 24) & (row < 27), 1.0, 0.0)
    place = [moving_ref[f] for f in range(3)]
    zeros, ones = jnp.zeros_like(place[0]), jnp.ones_like(place[0])
    norm = 0.0
    rows = [zeros] * (2 * DEPTH)
    for f in range(3):
        hi, mid, lo = split3(place[f])
        norm = norm + place[f] * place[f]
        rows[f : 15 : 3] = [hi, mid, lo, hi, hi]
    rows[15:18] = [ones] * 3
    n1, n2, n3 = split3(norm)
    rows[18:24] = [n1, n2, n3, n1, n2, n1]
    h1, h2 = split2(moving_ref[3])
    rows[DEPTH + 24 : DEPTH + 31] = [ones] * 3 + [h1, h2, h1, h2]
    near_ref[0:start, :] = slot_major(rows)


def pair_loop(plan, plan_ref, which, groups, near_ref, far_ref, weight_ref, slope_ref):
    base = which * plan.length
    stored = plan.stored_base(plan_ref, which)

    def work(start, size):
        for u in range(size):
            word = plan_ref[base + start + u]
            far = far_ref[pl.ds(pl.multiple_of(plan.cand(word) * DEPTH, DEPTH), DEPTH), :]
            near = near_ref[pl.ds(pl.multiple_of(plan.slot(word) * (2 * DEPTH), DEPTH), 2 * DEPTH), :]
            near = jnp.concatenate([near[0:DEPTH], near[DEPTH : 2 * DEPTH]], axis=1)
            both = lax.dot_general(
                far.astype(BF16), near.astype(BF16), (((0,), (0,)), ((), ())), preferred_element_type=F32
            )
            squared = jnp.maximum(both[:, 0:LANES], 1e-20)
            inverse = pltpu.reciprocal(both[:, LANES : 2 * LANES], approx=True)
            remain = jnp.maximum(4.0 - squared * lax.rsqrt(squared) * inverse, 0.0)
            scaled = inverse * remain
            cubed = scaled * scaled * scaled
            weight = cubed * (remain * (5.0 - remain))
            weight_ref[plan.code(word)] = jnp.sum(weight.reshape(LANES // 8, 8, LANES), axis=0)
            slope_ref[stored + start + u] = cubed * (inverse * inverse)

    in_groups(plan, plan_ref, which, groups, work)


def local_kernel(plan, plan_ref, moving_ref, weight_in_ref, near_ref, weight_ref, slope_ref, far_ref):
    slots = plan.slots
    store_near(near_ref, moving_ref, slots)
    store_far(far_ref, moving_ref, slots)
    store_far_dummy(far_ref, slots)
    pair_loop(plan, plan_ref, 0, LARGE_GROUPS, near_ref, far_ref, weight_ref, slope_ref)


def first_kernel(plan, plan_ref, moving_ref, near_ref, weight_in_ref, slope_in_ref, weight_ref, slope_ref, far_ref):
    store_far(far_ref, moving_ref, plan.slots)
    store_far_dummy(far_ref, plan.slots)
    pair_loop(plan, plan_ref, 1, GROUPS, near_ref, far_ref, weight_ref, slope_ref)


def second_kernel(plan, plan_ref, own_ref, moving_ref, near_ref, weight_in_ref, slope_in_ref,
                  density_ref, thermal_ref, weight_ref, slope_ref, far_ref):
    store_far(far_ref, moving_ref, plan.slots)
    store_far_dummy(far_ref, plan.slots)
    pair_loop(plan, plan_ref, 2, GROUPS, near_ref, far_ref, weight_ref, slope_ref)
    for i in range(plan.slots):
        first = i << plan.entry_bits
        tile = weight_ref[first]
        for k in range(1, plan.width):
            tile = tile + weight_ref[first + k]
        density_ref[i : i + 1, :] = sum_rows(tile)[0:1, :]
    density = WEIGHT_FACTOR * density_ref[...]
    density_ref[...] = density
    safe = jnp.where(own_ref[6] > 0, density, 1.0)
    thermal_ref[0] = (ADIABATIC - 1.0) * density * own_ref[7] / (safe * safe)
    for f in range(EARLY, 3):
        thermal_ref[1 + f - EARLY] = own_ref[3 + f]


def store_fields(field_ref, moving_ref, thermal_ref, slots):
    def put(row, value):
        field_ref[pl.ds(row, slots, stride=FIELD_ROWS), :] = value

    stretch = moving_ref[4]
    square = stretch * stretch
    place = [moving_ref[f] for f in range(3)]
    speed = [moving_ref[5 + f] if f < EARLY else thermal_ref[1 + f - EARLY] for f in range(3)]
    dotted = place[0] * speed[0] + place[1] * speed[1] + place[2] * speed[2]
    plain = [square] + [square * value for value in place + speed + [dotted]]
    heavy = [thermal_ref[0] * value for value in plain[0:4]]
    for row, value in enumerate(plain):
        for part, piece in enumerate(split3(value)):
            put(8 * part + row, piece)
    for row, value in enumerate(heavy):
        for part, piece in enumerate(split3(value)):
            put(24 + 4 * part + row, piece)
        put(36 + row, jnp.zeros_like(value))


def store_field_dummy(field_ref, index):
    field_ref[index * FIELD_ROWS : (index + 1) * FIELD_ROWS, :] = jnp.zeros((FIELD_ROWS, LANES), F32)


def field_loop(plan, plan_ref, which, field_ref, slope_ref, sum_ref):
    base = which * plan.length
    stored = plan.stored_base(plan_ref, which)

    def work(start, size):
        for u in range(size):
            word = plan_ref[base + start + u]
            field = field_ref[pl.ds(pl.multiple_of(plan.cand(word) * FIELD_ROWS, 8), FIELD_ROWS), :].astype(BF16)
            slope = slope_ref[stored + start + u]
            hi = slope.astype(BF16)
            lo = (slope - hi.astype(F32)).astype(BF16)
            both = jnp.dot(
                jnp.concatenate([field, field], axis=1),
                jnp.concatenate([hi, lo], axis=0),
                preferred_element_type=F32,
            )
            code = plan.code(word)
            sum_ref[code, 0:8, :] = both[0:8] + both[8:16] + both[16:24]
            sum_ref[code, 8:16, :] = both[24:32] + both[32:40]

    in_groups(plan, plan_ref, which, GROUPS, work)


def local_field_kernel(plan, plan_ref, moving_ref, thermal_ref, slope_ref, sum_ref, field_ref):
    store_fields(field_ref, moving_ref, thermal_ref, plan.slots)
    store_field_dummy(field_ref, plan.slots)
    sum_ref[...] = jnp.zeros_like(sum_ref)
    field_loop(plan, plan_ref, 0, field_ref, slope_ref, sum_ref)


def first_field_kernel(plan, plan_ref, moving_ref, thermal_ref, slope_ref, sum_in_ref, sum_ref, field_ref):
    store_fields(field_ref, moving_ref, thermal_ref, plan.slots)
    store_field_dummy(field_ref, plan.slots)
    field_loop(plan, plan_ref, 1, field_ref, slope_ref, sum_ref)


def final_kernel(plan, tiles, cap, floats, plan_ref, own_ref, moving_ref, second_ref, density_ref, thermal_ref,
                 second_thermal_ref, slope_ref, sum_in_ref, *refs):
    rests, (updated_ref, derived_ref, sum_ref, field_ref, total_ref) = refs[:tiles], refs[tiles:]
    slots = plan.slots
    store_fields(field_ref, second_ref, second_thermal_ref, slots)
    store_field_dummy(field_ref, slots)
    me = lax.axis_index("tile")
    for k in range(tiles):
        base = pl.multiple_of(source_tile(me, k, tiles) * cap, cap)
        held = (own_ref[6, pl.ds(base, cap), :] > 0).astype(F32)
        for f in range(floats - CORE):
            updated_ref[pl.ds(base * floats + CORE + f, cap, stride=floats), :] = rests[k][f] * held
    field_loop(plan, plan_ref, 2, field_ref, slope_ref, sum_ref)
    for i in range(slots):
        first = i << plan.entry_bits
        tile = sum_ref[first]
        for k in range(1, plan.width):
            tile = tile + sum_ref[first + k]
        total_ref[16 * i : 16 * (i + 1), :] = tile

    def summed(row):
        return SLOPE_FACTOR * total_ref[pl.ds(row, slots, stride=16), :]

    plain = [summed(row) for row in range(8)]
    heavy = [summed(8 + row) + summed(12 + row) for row in range(4)]
    place = [moving_ref[f] for f in range(3)]
    speed = [own_ref[3 + f] for f in range(3)]
    ratio, density = thermal_ref[0], density_ref[...]
    accel, heating = [], plain[7]
    for f in range(3):
        spread = place[f] * plain[0] - plain[1 + f]
        accel.append(-(ratio * spread + (place[f] * heavy[0] - heavy[1 + f])))
        heating = heating + place[f] * (speed[f] * plain[0] - plain[4 + f]) - speed[f] * plain[1 + f]
    heating = ratio * heating
    present = (own_ref[6] > 0).astype(F32)
    fresh = {}
    for f in range(3):
        fresh[3 + f] = speed[f] + TIMESTEP * accel[f]
        fresh[f] = own_ref[f] + TIMESTEP * fresh[3 + f]
    fresh[6] = own_ref[6]
    fresh[7] = own_ref[7] + TIMESTEP * heating
    fresh[8] = own_ref[8]
    for f in range(CORE):
        updated_ref[pl.ds(f, slots, stride=floats), :] = fresh[f] * present
    for f, value in enumerate([density] + accel + [heating]):
        derived_ref[f] = value * present


def body(tiles, slabs, particles, dest_slot, neighbours, counts):
    bins, floats, lanes = particles.shape
    slots, width = neighbours.shape
    cap = slots // tiles
    plan = Plan(slots, width)
    packed = kernel_call(
        lambda *refs: pack_kernel(tiles, cap, floats, *refs),
        [("h", in_hbm(dest_slot)), ("h", in_hbm(particles))],
        [("v", (CORE, cap, lanes), F32)] * tiles + [("v", (floats - CORE, cap, lanes), F32)] * tiles,
        [
            pltpu.VMEM((slots * floats, lanes), F32),
            pltpu.VMEM((bins, floats, lanes), F32),
            pltpu.SMEM((bins,), I32),
            pltpu.SemaphoreType.DMA((9 if bins % 8 == 0 else 2,)),
        ],
        1500,
        "pack",
    )
    packed, rests = packed[:tiles], packed[tiles:]

    def to_partner(array, step):
        return lax.ppermute(array, "tile", [(t, partner_tile(t, step, tiles)) for t in range(tiles)])

    near_out = ("v", ((slots + 1) * 2 * DEPTH, lanes), F32)
    weight_out = ("v", (plan.codes, 8, lanes), F32)
    lists, weights = kernel_call(
        lambda *refs: plan_kernel(plan, *refs),
        [("s", in_hbm(neighbours.T)), ("s", in_hbm(counts)), ("a", packed[0])],
        [("s", (plan.size,), I32), weight_out],
        [],
        2000,
        "plan",
    )
    parts = [packed[0]] + [to_partner(packed[k], k) for k in range(1, tiles)]
    state_outs = [("v", (CORE, slots, lanes), F32), ("v", (5 + EARLY, slots, lanes), F32)]
    far_steps = [k for k in range(tiles) if k != 1]
    own, moving = kernel_call(
        lambda *refs: states_kernel(tiles, cap, far_steps, *refs),
        [("v", parts[k]) for k in far_steps],
        state_outs,
        [],
        200,
        "far_states",
    )
    if tiles > 1:
        own, moving = kernel_call(
            lambda *refs: states_kernel(tiles, cap, [1], *refs),
            [("v", parts[1]), ("v", own), ("v", moving), ("a", lists)],
            state_outs,
            [],
            100,
            "near_states",
            {1: 0, 2: 1},
        )
    first_pairs = [(s, s ^ 1) for s in range(slabs)]
    second_pairs = [(s, (((s + 1) ^ 1) - 1) % slabs) for s in range(slabs)]

    def both_sides(array):
        second = lax.ppermute(array, "slab", second_pairs)
        first = lax.ppermute(array, "slab", first_pairs)
        return first, second

    first, second = both_sides(moving)
    slope_out = ("v", (plan.stored, lanes, lanes), F32)
    sum_out = ("v", (plan.codes, 16, lanes), F32)
    far_table = [pltpu.VMEM(((slots + 1) * DEPTH, lanes), F32)]
    field_table = [pltpu.VMEM(((slots + 1) * FIELD_ROWS, lanes), F32)]
    near, weights, slopes = kernel_call(
        lambda *refs: local_kernel(plan, *refs),
        [("s", lists), ("v", moving), ("v", weights)],
        [near_out, weight_out, slope_out],
        far_table,
        3500,
        "local",
        {2: 1},
    )
    weights, slopes = kernel_call(
        lambda *refs: first_kernel(plan, *refs),
        [("s", lists), ("v", first), ("v", near), ("v", weights), ("v", slopes)],
        [weight_out, slope_out],
        far_table,
        1500,
        "first",
        {3: 0, 4: 1},
    )
    density, thermal, weights, slopes = kernel_call(
        lambda *refs: second_kernel(plan, *refs),
        [("s", lists), ("v", own), ("v", second), ("v", near), ("v", weights), ("v", slopes)],
        [("v", (slots, lanes), F32), ("v", (4 - EARLY, slots, lanes), F32), weight_out, slope_out],
        far_table,
        2000,
        "second",
        {4: 2, 5: 3},
    )
    first_thermal, second_thermal = both_sides(thermal)
    later = rests[1:]
    (sums,) = kernel_call(
        lambda *refs: local_field_kernel(plan, *refs),
        [("s", lists), ("v", moving), ("v", thermal), ("v", slopes)],
        [sum_out],
        field_table,
        1700,
        "local_fields",
    )
    rests = [rests[0]] + [to_partner(later[k - 1], k) for k in range(1, tiles)]
    (sums,) = kernel_call(
        lambda *refs: first_field_kernel(plan, *refs),
        [("s", lists), ("v", first), ("v", first_thermal), ("v", slopes), ("v", sums)],
        [sum_out],
        field_table,
        1000,
        "first_fields",
        {4: 0},
    )
    updated, derived, _ = kernel_call(
        lambda *refs: final_kernel(plan, tiles, cap, floats, *refs),
        [("s", lists), ("v", own), ("v", moving), ("v", second), ("v", density), ("v", thermal),
         ("v", second_thermal), ("v", slopes), ("v", sums)]
        + [("v", rest) for rest in rests],
        [("v", (slots * floats, lanes), F32), ("v", (5, slots, lanes), F32), sum_out],
        field_table + [pltpu.VMEM((slots * 16, lanes), F32)],
        2000,
        "final",
        {8: 2},
    )
    return updated.reshape(slots, floats, lanes), derived.transpose(1, 0, 2)


def solution(mesh):
    tiles, slabs = mesh.shape["tile"], mesh.shape["slab"]
    in_specs = (
        P(("slab", "tile"), None, None),
        P(("slab", "tile")),
        P(("slab", "tile"), None),
        P(("slab", "tile")),
    )
    out_specs = (P(("slab", "tile"), None, None), P(("slab", "tile"), None, None))
    return jax.shard_map(
        lambda *args: body(tiles, slabs, *args), mesh=mesh, in_specs=in_specs, out_specs=out_specs, check_vma=False
    )
```

```python
import math

import jax
import jax.numpy as jnp
from jax import lax
from jax.experimental import pallas as pl
from jax.experimental.pallas import tpu as pltpu
from jax.sharding import PartitionSpec as P

ADIABATIC = 5.0 / 3.0
TIMESTEP = 0.5
KERNEL_NORM = 21.0 / (16.0 * math.pi)
MASS_UNIT = 512.0
WEIGHT_FACTOR = 8.0 * KERNEL_NORM / MASS_UNIT / 4.0**7
SLOPE_FACTOR = -5.0 * 32.0 * KERNEL_NORM / MASS_UNIT / 4.0**8
CENTRE = 1.0
AWAY = 1.0e4
LANES = 128
LARGE_GROUPS = (((48, 40), (24, 16)), (16, 8))
GROUPS = (((24, 16),), (16, 8))
STEP = 8
EARLY = 0
CORE = 9
DEPTH = 32
FIELD_ROWS = 40

F32 = jnp.float32
BF16 = jnp.bfloat16
I32 = jnp.int32


def vmem_spec():
    return pl.BlockSpec(memory_space=pltpu.VMEM)


def smem_spec():
    return pl.BlockSpec(memory_space=pltpu.SMEM)


def hbm_spec():
    return pl.BlockSpec(memory_space=pltpu.HBM)


def any_spec():
    return pl.BlockSpec(memory_space=pl.ANY)


SPECS = {"s": smem_spec, "v": vmem_spec, "h": hbm_spec, "a": any_spec}


def in_hbm(array):
    return pltpu.with_memory_space_constraint(array, pltpu.HBM)


def kernel_call(kernel, ins, outs, scratch, nanoseconds, name, aliases=None):
    return pl.pallas_call(
        kernel,
        out_shape=[
            pltpu.SMEM(shape, dtype) if memory == "s" else jax.ShapeDtypeStruct(shape, dtype)
            for memory, shape, dtype in outs
        ],
        in_specs=[SPECS[memory]() for memory, _ in ins],
        out_specs=[SPECS[memory]() for memory, _, _ in outs],
        scratch_shapes=scratch,
        input_output_aliases=aliases or {},
        compiler_params=pltpu.CompilerParams(vmem_limit_bytes=32 * 1024 * 1024),
        cost_estimate=pl.CostEstimate(flops=0, bytes_accessed=3000 * nanoseconds, transcendentals=0),
        name=name,
    )(*[array for _, array in ins])


def is_power(count):
    return count & (count - 1) == 0


def partner_tile(index, step, count):
    return index ^ step if is_power(count) else (index + step) % count


def source_tile(index, step, count):
    return index ^ step if is_power(count) else lax.rem(index + count - step, count)


def rounded(value):
    return value.astype(BF16).astype(F32)


def split2(value):
    hi = rounded(value)
    return hi, rounded(value - hi)


def split3(value):
    hi = rounded(value)
    mid = rounded(value - hi)
    return hi, mid, rounded(value - hi - mid)


def sum_rows(tile):
    tile = tile + pltpu.roll(tile, 4, 0)
    tile = tile + pltpu.roll(tile, 2, 0)
    return tile + pltpu.roll(tile, 1, 0)


class Plan:
    def __init__(self, slots, width):
        self.slots, self.width = slots, width
        self.entry_bits = (width - 1).bit_length()
        self.cand_bits = slots.bit_length()
        self.length = slots * width + STEP
        self.codes = (slots + 1) << self.entry_bits
        self.counts = 3 * self.length
        self.size = 3 * self.length + 8
        self.stored = slots * width + 4 * STEP
        self.dummy = self.word(slots, 0, slots)

    def word(self, slot, entry, cand):
        return (((slot << self.entry_bits) + entry) << self.cand_bits) + cand

    def code(self, word):
        return word >> self.cand_bits

    def slot(self, word):
        return word >> (self.cand_bits + self.entry_bits)

    def cand(self, word):
        return word & ((1 << self.cand_bits) - 1)

    def stored_base(self, ref, which):
        base = 0
        for k in range(which):
            base = base + lax.div(ref[self.counts + k] + STEP - 1, STEP) * STEP
        return base


def in_groups(plan, plan_ref, which, groups, work):
    loops, tails = groups
    start, count = 0, plan_ref[plan.counts + which]
    for size, left in loops:

        def step(g, first, size=size):
            work(first, size)
            return first + size

        number = lax.div(jnp.maximum(count - start - left + size - 1, 0), size)
        start = lax.fori_loop(0, number, step, start)
    rest = count - start
    for size, below in zip(tails, tails[1:] + (0,)):

        @pl.when((rest <= size) & (rest > below))
        def _(size=size):
            work(start, size)


def plan_kernel(plan, neighbours_ref, counts_ref, after_ref, plan_ref, weight_ref):
    slots = plan.slots
    entries = 1 << plan.entry_bits
    upper_first = lax.rem(lax.axis_index("slab"), 2) == 0
    low = jnp.where(upper_first, 2, 1)
    high = 3 - low

    def fill(i, totals):
        used = counts_ref[i]
        for k in range(plan.width):
            n = neighbours_ref[k, i]
            region = lax.div(n, slots)
            which = jnp.where(region == 1, 0, jnp.where(region == 0, low, high))
            word = plan.word(i, k, n - region * slots)
            kept = []
            for w in range(3):
                plan_ref[w * plan.length + totals[w]] = word
                kept.append(totals[w] + ((k < used) & (which == w)).astype(I32))
            totals = tuple(kept)
        weight_ref[pl.ds(i * entries, entries)] = jnp.zeros((entries, 8, LANES), F32)
        return totals

    totals = lax.fori_loop(0, slots, fill, (jnp.int32(0),) * 3, unroll=4)
    for w in range(3):
        for k in range(STEP):
            plan_ref[w * plan.length + totals[w] + k] = plan.dummy
        plan_ref[plan.counts + w] = totals[w]


def pack_kernel(tiles, cap, floats, dest_ref, particles_ref, *refs):
    cores, rests, (packed, staged, dest, sems) = refs[:tiles], refs[tiles:-4], refs[-4:]
    pieces = sems.shape[0] - 1
    bins = staged.shape[0] // pieces
    bring = [pltpu.make_async_copy(dest_ref, dest, sems.at[pieces])]
    for p in range(pieces):
        part = pl.ds(p * bins, bins)
        bring.append(pltpu.make_async_copy(particles_ref.at[part], staged.at[part], sems.at[p]))
    for copy in bring:
        copy.start()
    packed[...] = jnp.zeros_like(packed)
    me = lax.axis_index("tile")
    for copy in bring:
        copy.wait()

    def place(b, carry):
        target = dest[b]
        owner = lax.div(target, cap)
        step = owner ^ me if is_power(tiles) else lax.rem(owner + tiles - me, tiles)
        start = pl.multiple_of((step * cap + lax.rem(target, cap)) * floats, 8)
        packed[pl.ds(start, floats), :] = staged[b]
        return carry

    lax.fori_loop(0, staged.shape[0], place, 0, unroll=4)
    for k in range(tiles):
        for f in range(floats):
            value = packed[pl.ds(k * cap * floats + f, cap, stride=floats), :]
            if f < CORE:
                cores[k][f] = value
            else:
                if k % 2 == 0:
                    rests[k // 2][f - CORE] = value
                else:
                    cores[1][f + (k // 2) * (floats - CORE)] = value


def states_kernel(tiles, cap, steps, *refs):
    parts, (own_ref, moving_ref) = dict(zip(steps, refs)), refs[-2:]
    me = lax.axis_index("tile")
    for k in steps:
        rows = pl.ds(pl.multiple_of(source_tile(me, k, tiles) * cap, cap), cap)
        field = parts[k]
        for f in range(CORE):
            own_ref[f, rows, :] = field[f]
        mass = field[6]
        present = mass > 0
        for f in range(3):
            moving_ref[f, rows, :] = field[f] - CENTRE
        moving_ref[3, rows, :] = jnp.where(present, field[8], 1.0)
        scaled = jnp.where(present, mass * MASS_UNIT, 1.0)
        root = jnp.exp(jnp.log(scaled) * (-1.0 / 3.0))
        for _ in range(2):
            root = root * (4.0 - scaled * (root * root * root)) * (1.0 / 3.0)
        moving_ref[4, rows, :] = jnp.where(present, root, 0.0)
        for f in range(EARLY):
            moving_ref[5 + f, rows, :] = field[3 + f]


def near_states_kernel(tiles, cap, floats, *refs):
    nearest, rests, refs = refs[0], refs[1 : 1 + tiles // 2], refs[1 + tiles // 2 :]
    bundles, (own_ref, moving_ref) = refs[-2 - tiles // 2 : -2], refs[-2:]
    states_kernel(tiles, cap, [1], nearest, own_ref, moving_ref)
    extra = floats - CORE
    for q in range(tiles // 2):
        bundles[q][0:extra] = rests[q][...]
        bundles[q][extra : 2 * extra] = nearest[CORE + q * extra : CORE + (q + 1) * extra]


def slot_major(rows):
    slots, lanes = rows[0].shape
    return jnp.swapaxes(jnp.stack(rows, axis=0), 0, 1).reshape(slots * len(rows), lanes)


def store_far(far_ref, moving_ref, slots):
    place = [moving_ref[f] for f in range(3)]
    smooth, stretch = moving_ref[3], moving_ref[4]
    present = stretch > 0
    stretch = jnp.where(present, stretch, 1.0)
    square = stretch * stretch
    norm = 0.0
    rows = [None] * DEPTH
    for f in range(3):
        hi, mid, lo = split3(-2.0 * square * place[f])
        norm = norm + place[f] * place[f]
        rows[f : 15 : 3] = [hi, hi, hi, mid, lo]
    rows[15:18] = split3(jnp.where(present, square * norm, AWAY))
    s1, s2, s3 = split3(square)
    rows[18:24] = [s1, s1, s1, s2, s2, s3]
    rows[24:27] = split3(0.25 * stretch * smooth)
    u1, u2 = split2(0.25 * stretch)
    rows[27:32] = [u1, u1, u2, u2, jnp.zeros_like(u1)]
    far_ref[0 : slots * DEPTH, :] = slot_major(rows)


def store_far_dummy(far_ref, index):
    row = lax.broadcasted_iota(I32, (DEPTH, LANES), 0)
    far_ref[index * DEPTH : (index + 1) * DEPTH, :] = jnp.where(row == 15, AWAY, jnp.where(row == 24, 1.0, 0.0))


def store_near(near_ref, moving_ref, slots):
    row = lax.broadcasted_iota(I32, (DEPTH, LANES), 0)
    start = 2 * slots * DEPTH
    near_ref[start : start + DEPTH, :] = jnp.where((row >= 15) & (row < 18), 1.0, 0.0)
    near_ref[start + DEPTH : start + 2 * DEPTH, :] = jnp.where((row >= 24) & (row < 27), 1.0, 0.0)
    place = [moving_ref[f] for f in range(3)]
    zeros, ones = jnp.zeros_like(place[0]), jnp.ones_like(place[0])
    norm = 0.0
    rows = [zeros] * (2 * DEPTH)
    for f in range(3):
        hi, mid, lo = split3(place[f])
        norm = norm + place[f] * place[f]
        rows[f : 15 : 3] = [hi, mid, lo, hi, hi]
    rows[15:18] = [ones] * 3
    n1, n2, n3 = split3(norm)
    rows[18:24] = [n1, n2, n3, n1, n2, n1]
    h1, h2 = split2(moving_ref[3])
    rows[DEPTH + 24 : DEPTH + 31] = [ones] * 3 + [h1, h2, h1, h2]
    near_ref[0:start, :] = slot_major(rows)


def pair_loop(plan, plan_ref, which, groups, near_ref, far_ref, weight_ref, slope_ref):
    base = which * plan.length
    stored = plan.stored_base(plan_ref, which)

    def work(start, size):
        for u in range(size):
            word = plan_ref[base + start + u]
            far = far_ref[pl.ds(pl.multiple_of(plan.cand(word) * DEPTH, DEPTH), DEPTH), :]
            near = near_ref[pl.ds(pl.multiple_of(plan.slot(word) * (2 * DEPTH), DEPTH), 2 * DEPTH), :]
            near = jnp.concatenate([near[0:DEPTH], near[DEPTH : 2 * DEPTH]], axis=1)
            both = lax.dot_general(
                far.astype(BF16), near.astype(BF16), (((0,), (0,)), ((), ())), preferred_element_type=F32
            )
            squared = jnp.maximum(both[:, 0:LANES], 1e-20)
            inverse = pltpu.reciprocal(both[:, LANES : 2 * LANES], approx=True)
            remain = jnp.maximum(4.0 - squared * lax.rsqrt(squared) * inverse, 0.0)
            scaled = inverse * remain
            cubed = scaled * scaled * scaled
            weight = cubed * (remain * (5.0 - remain))
            weight_ref[plan.code(word)] = jnp.sum(weight.reshape(LANES // 8, 8, LANES), axis=0)
            slope_ref[stored + start + u] = cubed * (inverse * inverse)

    in_groups(plan, plan_ref, which, groups, work)


def local_kernel(plan, plan_ref, moving_ref, weight_in_ref, near_ref, weight_ref, slope_ref, far_ref):
    slots = plan.slots
    store_near(near_ref, moving_ref, slots)
    store_far(far_ref, moving_ref, slots)
    store_far_dummy(far_ref, slots)
    pair_loop(plan, plan_ref, 0, LARGE_GROUPS, near_ref, far_ref, weight_ref, slope_ref)


def first_kernel(plan, plan_ref, moving_ref, near_ref, weight_in_ref, slope_in_ref, weight_ref, slope_ref, far_ref):
    store_far(far_ref, moving_ref, plan.slots)
    store_far_dummy(far_ref, plan.slots)
    pair_loop(plan, plan_ref, 1, GROUPS, near_ref, far_ref, weight_ref, slope_ref)


def second_kernel(plan, plan_ref, own_ref, moving_ref, near_ref, weight_in_ref, slope_in_ref,
                  density_ref, thermal_ref, weight_ref, slope_ref, far_ref):
    store_far(far_ref, moving_ref, plan.slots)
    store_far_dummy(far_ref, plan.slots)
    pair_loop(plan, plan_ref, 2, GROUPS, near_ref, far_ref, weight_ref, slope_ref)
    for i in range(plan.slots):
        first = i << plan.entry_bits
        tile = weight_ref[first]
        for k in range(1, plan.width):
            tile = tile + weight_ref[first + k]
        density_ref[i : i + 1, :] = sum_rows(tile)[0:1, :]
    density = WEIGHT_FACTOR * density_ref[...]
    density_ref[...] = density
    safe = jnp.where(own_ref[6] > 0, density, 1.0)
    thermal_ref[0] = (ADIABATIC - 1.0) * density * own_ref[7] / (safe * safe)
    for f in range(EARLY, 3):
        thermal_ref[1 + f - EARLY] = own_ref[3 + f]


def store_fields(field_ref, moving_ref, thermal_ref, slots):
    def put(row, value):
        field_ref[pl.ds(row, slots, stride=FIELD_ROWS), :] = value

    stretch = moving_ref[4]
    square = stretch * stretch
    place = [moving_ref[f] for f in range(3)]
    speed = [moving_ref[5 + f] if f < EARLY else thermal_ref[1 + f - EARLY] for f in range(3)]
    dotted = place[0] * speed[0] + place[1] * speed[1] + place[2] * speed[2]
    plain = [square] + [square * value for value in place + speed + [dotted]]
    heavy = [thermal_ref[0] * value for value in plain[0:4]]
    for row, value in enumerate(plain):
        for part, piece in enumerate(split3(value)):
            put(8 * part + row, piece)
    for row, value in enumerate(heavy):
        for part, piece in enumerate(split3(value)):
            put(24 + 4 * part + row, piece)
        put(36 + row, jnp.zeros_like(value))


def store_field_dummy(field_ref, index):
    field_ref[index * FIELD_ROWS : (index + 1) * FIELD_ROWS, :] = jnp.zeros((FIELD_ROWS, LANES), F32)


def field_loop(plan, plan_ref, which, field_ref, slope_ref, sum_ref):
    base = which * plan.length
    stored = plan.stored_base(plan_ref, which)

    def work(start, size):
        for u in range(size):
            word = plan_ref[base + start + u]
            field = field_ref[pl.ds(pl.multiple_of(plan.cand(word) * FIELD_ROWS, 8), FIELD_ROWS), :].astype(BF16)
            slope = slope_ref[stored + start + u]
            hi = slope.astype(BF16)
            lo = (slope - hi.astype(F32)).astype(BF16)
            both = jnp.dot(
                jnp.concatenate([field, field], axis=1),
                jnp.concatenate([hi, lo], axis=0),
                preferred_element_type=F32,
            )
            code = plan.code(word)
            sum_ref[code, 0:8, :] = both[0:8] + both[8:16] + both[16:24]
            sum_ref[code, 8:16, :] = both[24:32] + both[32:40]

    in_groups(plan, plan_ref, which, GROUPS, work)


def local_field_kernel(plan, plan_ref, moving_ref, thermal_ref, slope_ref, sum_ref, field_ref):
    store_fields(field_ref, moving_ref, thermal_ref, plan.slots)
    store_field_dummy(field_ref, plan.slots)
    sum_ref[...] = jnp.zeros_like(sum_ref)
    field_loop(plan, plan_ref, 0, field_ref, slope_ref, sum_ref)


def first_field_kernel(plan, plan_ref, moving_ref, thermal_ref, slope_ref, sum_in_ref, sum_ref, field_ref):
    store_fields(field_ref, moving_ref, thermal_ref, plan.slots)
    store_field_dummy(field_ref, plan.slots)
    field_loop(plan, plan_ref, 1, field_ref, slope_ref, sum_ref)


def final_kernel(plan, tiles, cap, floats, plan_ref, own_ref, moving_ref, second_ref, density_ref, thermal_ref,
                 second_thermal_ref, slope_ref, sum_in_ref, *refs):
    bundles, (updated_ref, derived_ref, sum_ref, field_ref, total_ref) = refs[: tiles // 2], refs[tiles // 2 :]
    slots = plan.slots
    store_fields(field_ref, second_ref, second_thermal_ref, slots)
    store_field_dummy(field_ref, slots)
    me = lax.axis_index("tile")
    for k in range(tiles):
        base = pl.multiple_of(source_tile(me, k, tiles) * cap, cap)
        held = (own_ref[6, pl.ds(base, cap), :] > 0).astype(F32)
        for f in range(floats - CORE):
            value = bundles[k // 2][(k % 2) * (floats - CORE) + f]
            updated_ref[pl.ds(base * floats + CORE + f, cap, stride=floats), :] = value * held
    field_loop(plan, plan_ref, 2, field_ref, slope_ref, sum_ref)
    for i in range(slots):
        first = i << plan.entry_bits
        tile = sum_ref[first]
        for k in range(1, plan.width):
            tile = tile + sum_ref[first + k]
        total_ref[16 * i : 16 * (i + 1), :] = tile

    def summed(row):
        return SLOPE_FACTOR * total_ref[pl.ds(row, slots, stride=16), :]

    plain = [summed(row) for row in range(8)]
    heavy = [summed(8 + row) + summed(12 + row) for row in range(4)]
    place = [moving_ref[f] for f in range(3)]
    speed = [own_ref[3 + f] for f in range(3)]
    ratio, density = thermal_ref[0], density_ref[...]
    accel, heating = [], plain[7]
    for f in range(3):
        spread = place[f] * plain[0] - plain[1 + f]
        accel.append(-(ratio * spread + (place[f] * heavy[0] - heavy[1 + f])))
        heating = heating + place[f] * (speed[f] * plain[0] - plain[4 + f]) - speed[f] * plain[1 + f]
    heating = ratio * heating
    present = (own_ref[6] > 0).astype(F32)
    fresh = {}
    for f in range(3):
        fresh[3 + f] = speed[f] + TIMESTEP * accel[f]
        fresh[f] = own_ref[f] + TIMESTEP * fresh[3 + f]
    fresh[6] = own_ref[6]
    fresh[7] = own_ref[7] + TIMESTEP * heating
    fresh[8] = own_ref[8]
    for f in range(CORE):
        updated_ref[pl.ds(f, slots, stride=floats), :] = fresh[f] * present
    for f, value in enumerate([density] + accel + [heating]):
        derived_ref[f] = value * present


def body(tiles, slabs, particles, dest_slot, neighbours, counts):
    bins, floats, lanes = particles.shape
    slots, width = neighbours.shape
    cap = slots // tiles
    plan = Plan(slots, width)
    half, extra = tiles // 2, floats - CORE
    packed = kernel_call(
        lambda *refs: pack_kernel(tiles, cap, floats, *refs),
        [("h", in_hbm(dest_slot)), ("h", in_hbm(particles))],
        [("v", (CORE + (extra * half if k == 1 else 0), cap, lanes), F32) for k in range(tiles)]
        + [("v", (extra, cap, lanes), F32)] * half,
        [
            pltpu.VMEM((slots * floats, lanes), F32),
            pltpu.VMEM((bins, floats, lanes), F32),
            pltpu.SMEM((bins,), I32),
            pltpu.SemaphoreType.DMA((9 if bins % 8 == 0 else 2,)),
        ],
        1500,
        "pack",
    )
    packed, rests = packed[:tiles], packed[tiles:]

    def to_partner(array, step):
        return lax.ppermute(array, "tile", [(t, partner_tile(t, step, tiles)) for t in range(tiles)])

    near_out = ("v", ((slots + 1) * 2 * DEPTH, lanes), F32)
    weight_out = ("v", (plan.codes, 8, lanes), F32)
    lists, weights = kernel_call(
        lambda *refs: plan_kernel(plan, *refs),
        [("s", in_hbm(neighbours.T)), ("s", in_hbm(counts)), ("a", packed[0])],
        [("s", (plan.size,), I32), weight_out],
        [],
        2000,
        "plan",
    )
    parts = [packed[0]] + [to_partner(packed[k], k) for k in range(1, tiles)]
    state_outs = [("v", (CORE, slots, lanes), F32), ("v", (5 + EARLY, slots, lanes), F32)]
    far_steps = [k for k in range(tiles) if k != 1]
    own, moving = kernel_call(
        lambda *refs: states_kernel(tiles, cap, far_steps, *refs),
        [("v", parts[k]) for k in far_steps],
        state_outs,
        [],
        200,
        "far_states",
    )
    *bundles, own, moving = kernel_call(
        lambda *refs: near_states_kernel(tiles, cap, floats, *refs),
        [("v", parts[1])] + [("v", rest) for rest in rests] + [("v", own), ("v", moving), ("a", lists)],
        [("v", (2 * extra, cap, lanes), F32)] * half + state_outs,
        [],
        100,
        "near_states",
        {1 + half: half, 2 + half: half + 1},
    )
    first_pairs = [(s, s ^ 1) for s in range(slabs)]
    second_pairs = [(s, (((s + 1) ^ 1) - 1) % slabs) for s in range(slabs)]

    def both_sides(array):
        second = lax.ppermute(array, "slab", second_pairs)
        first = lax.ppermute(array, "slab", first_pairs)
        return first, second

    first, second = both_sides(moving)
    slope_out = ("v", (plan.stored, lanes, lanes), F32)
    sum_out = ("v", (plan.codes, 16, lanes), F32)
    far_table = [pltpu.VMEM(((slots + 1) * DEPTH, lanes), F32)]
    field_table = [pltpu.VMEM(((slots + 1) * FIELD_ROWS, lanes), F32)]
    near, weights, slopes = kernel_call(
        lambda *refs: local_kernel(plan, *refs),
        [("s", lists), ("v", moving), ("v", weights)],
        [near_out, weight_out, slope_out],
        far_table,
        3500,
        "local",
        {2: 1},
    )
    weights, slopes = kernel_call(
        lambda *refs: first_kernel(plan, *refs),
        [("s", lists), ("v", first), ("v", near), ("v", weights), ("v", slopes)],
        [weight_out, slope_out],
        far_table,
        1500,
        "first",
        {3: 0, 4: 1},
    )
    density, thermal, weights, slopes = kernel_call(
        lambda *refs: second_kernel(plan, *refs),
        [("s", lists), ("v", own), ("v", second), ("v", near), ("v", weights), ("v", slopes)],
        [("v", (slots, lanes), F32), ("v", (4 - EARLY, slots, lanes), F32), weight_out, slope_out],
        far_table,
        2000,
        "second",
        {4: 2, 5: 3},
    )
    first_thermal, second_thermal = both_sides(thermal)
    (sums,) = kernel_call(
        lambda *refs: local_field_kernel(plan, *refs),
        [("s", lists), ("v", moving), ("v", thermal), ("v", slopes)],
        [sum_out],
        field_table,
        1700,
        "local_fields",
    )
    bundles = [bundles[0]] + [to_partner(bundles[q], 2 * q) for q in range(1, half)]
    (sums,) = kernel_call(
        lambda *refs: first_field_kernel(plan, *refs),
        [("s", lists), ("v", first), ("v", first_thermal), ("v", slopes), ("v", sums)],
        [sum_out],
        field_table,
        1000,
        "first_fields",
        {4: 0},
    )
    updated, derived, _ = kernel_call(
        lambda *refs: final_kernel(plan, tiles, cap, floats, *refs),
        [("s", lists), ("v", own), ("v", moving), ("v", second), ("v", density), ("v", thermal),
         ("v", second_thermal), ("v", slopes), ("v", sums)]
        + [("v", bundle) for bundle in bundles],
        [("v", (slots * floats, lanes), F32), ("v", (5, slots, lanes), F32), sum_out],
        field_table + [pltpu.VMEM((slots * 16, lanes), F32)],
        2000,
        "final",
        {8: 2},
    )
    return updated.reshape(slots, floats, lanes), derived.transpose(1, 0, 2)


def solution(mesh):
    tiles, slabs = mesh.shape["tile"], mesh.shape["slab"]
    in_specs = (
        P(("slab", "tile"), None, None),
        P(("slab", "tile")),
        P(("slab", "tile"), None),
        P(("slab", "tile")),
    )
    out_specs = (P(("slab", "tile"), None, None), P(("slab", "tile"), None, None))
    return jax.shard_map(
        lambda *args: body(tiles, slabs, *args), mesh=mesh, in_specs=in_specs, out_specs=out_specs, check_vma=False
    )
```

```python
import math

import jax
import jax.numpy as jnp
from jax import lax
from jax.experimental import pallas as pl
from jax.experimental.pallas import tpu as pltpu
from jax.sharding import PartitionSpec as P

ADIABATIC = 5.0 / 3.0
TIMESTEP = 0.5
KERNEL_NORM = 21.0 / (16.0 * math.pi)
MASS_UNIT = 512.0
WEIGHT_FACTOR = 8.0 * KERNEL_NORM / MASS_UNIT / 4.0**7
SLOPE_FACTOR = -5.0 * 32.0 * KERNEL_NORM / MASS_UNIT / 4.0**8
CENTRE = 1.0
AWAY = 1.0e4
LANES = 128
LARGE_GROUPS = (((48, 40), (24, 16)), (16, 8))
GROUPS = (((24, 16),), (16, 8))
STEP = 8
EARLY = 0
CORE = 9
DEPTH = 32
FIELD_ROWS = 40

F32 = jnp.float32
BF16 = jnp.bfloat16
I32 = jnp.int32


def vmem_spec():
    return pl.BlockSpec(memory_space=pltpu.VMEM)


def smem_spec():
    return pl.BlockSpec(memory_space=pltpu.SMEM)


def hbm_spec():
    return pl.BlockSpec(memory_space=pltpu.HBM)


def any_spec():
    return pl.BlockSpec(memory_space=pl.ANY)


SPECS = {"s": smem_spec, "v": vmem_spec, "h": hbm_spec, "a": any_spec}


def in_hbm(array):
    return pltpu.with_memory_space_constraint(array, pltpu.HBM)


def kernel_call(kernel, ins, outs, scratch, nanoseconds, name, aliases=None):
    return pl.pallas_call(
        kernel,
        out_shape=[
            pltpu.SMEM(shape, dtype) if memory == "s" else jax.ShapeDtypeStruct(shape, dtype)
            for memory, shape, dtype in outs
        ],
        in_specs=[SPECS[memory]() for memory, _ in ins],
        out_specs=[SPECS[memory]() for memory, _, _ in outs],
        scratch_shapes=scratch,
        input_output_aliases=aliases or {},
        compiler_params=pltpu.CompilerParams(vmem_limit_bytes=32 * 1024 * 1024),
        cost_estimate=pl.CostEstimate(flops=0, bytes_accessed=3000 * nanoseconds, transcendentals=0),
        name=name,
    )(*[array for _, array in ins])


def is_power(count):
    return count & (count - 1) == 0


def partner_tile(index, step, count):
    return index ^ step if is_power(count) else (index + step) % count


def source_tile(index, step, count):
    return index ^ step if is_power(count) else lax.rem(index + count - step, count)


def rounded(value):
    return value.astype(BF16).astype(F32)


def split2(value):
    hi = rounded(value)
    return hi, rounded(value - hi)


def split3(value):
    hi = rounded(value)
    mid = rounded(value - hi)
    return hi, mid, rounded(value - hi - mid)


def sum_rows(tile):
    tile = tile + pltpu.roll(tile, 4, 0)
    tile = tile + pltpu.roll(tile, 2, 0)
    return tile + pltpu.roll(tile, 1, 0)


class Plan:
    def __init__(self, slots, width):
        self.slots, self.width = slots, width
        self.entry_bits = (width - 1).bit_length()
        self.cand_bits = slots.bit_length()
        self.length = slots * width + STEP
        self.codes = (slots + 1) << self.entry_bits
        self.counts = 3 * self.length
        self.size = 3 * self.length + 8
        self.stored = slots * width + 4 * STEP
        self.dummy = self.word(slots, 0, slots)

    def word(self, slot, entry, cand):
        return (((slot << self.entry_bits) + entry) << self.cand_bits) + cand

    def code(self, word):
        return word >> self.cand_bits

    def slot(self, word):
        return word >> (self.cand_bits + self.entry_bits)

    def cand(self, word):
        return word & ((1 << self.cand_bits) - 1)

    def stored_base(self, ref, which):
        base = 0
        for k in range(which):
            base = base + lax.div(ref[self.counts + k] + STEP - 1, STEP) * STEP
        return base


def in_groups(plan, plan_ref, which, groups, work):
    loops, tails = groups
    start, count = 0, plan_ref[plan.counts + which]
    for size, left in loops:

        def step(g, first, size=size):
            work(first, size)
            return first + size

        number = lax.div(jnp.maximum(count - start - left + size - 1, 0), size)
        start = lax.fori_loop(0, number, step, start)
    rest = count - start
    for size, below in zip(tails, tails[1:] + (0,)):

        @pl.when((rest <= size) & (rest > below))
        def _(size=size):
            work(start, size)


def plan_kernel(plan, neighbours_ref, counts_ref, after_ref, plan_ref, weight_ref):
    slots = plan.slots
    entries = 1 << plan.entry_bits
    upper_first = lax.rem(lax.axis_index("slab"), 2) == 0
    low = jnp.where(upper_first, 2, 1)
    high = 3 - low

    def fill(i, totals):
        used = counts_ref[i]
        for k in range(plan.width):
            n = neighbours_ref[k, i]
            region = lax.div(n, slots)
            which = jnp.where(region == 1, 0, jnp.where(region == 0, low, high))
            word = plan.word(i, k, n - region * slots)
            kept = []
            for w in range(3):
                plan_ref[w * plan.length + totals[w]] = word
                kept.append(totals[w] + ((k < used) & (which == w)).astype(I32))
            totals = tuple(kept)
        weight_ref[pl.ds(i * entries, entries)] = jnp.zeros((entries, 8, LANES), F32)
        return totals

    totals = lax.fori_loop(0, slots, fill, (jnp.int32(0),) * 3, unroll=4)
    for w in range(3):
        for k in range(STEP):
            plan_ref[w * plan.length + totals[w] + k] = plan.dummy
        plan_ref[plan.counts + w] = totals[w]


def pack_kernel(tiles, cap, floats, dest_ref, particles_ref, *refs):
    cores, rests, (packed, staged, dest, sems) = refs[:tiles], refs[tiles:-4], refs[-4:]
    pieces = sems.shape[0] - 1
    bins = staged.shape[0] // pieces
    bring = [pltpu.make_async_copy(dest_ref, dest, sems.at[pieces])]
    for p in range(pieces):
        part = pl.ds(p * bins, bins)
        bring.append(pltpu.make_async_copy(particles_ref.at[part], staged.at[part], sems.at[p]))
    for copy in bring:
        copy.start()
    packed[...] = jnp.zeros_like(packed)
    me = lax.axis_index("tile")
    for copy in bring:
        copy.wait()

    def place(b, carry):
        target = dest[b]
        owner = lax.div(target, cap)
        step = owner ^ me if is_power(tiles) else lax.rem(owner + tiles - me, tiles)
        start = pl.multiple_of((step * cap + lax.rem(target, cap)) * floats, 8)
        packed[pl.ds(start, floats), :] = staged[b]
        return carry

    lax.fori_loop(0, staged.shape[0], place, 0, unroll=4)
    for k in range(tiles):
        for f in range(floats):
            value = packed[pl.ds(k * cap * floats + f, cap, stride=floats), :]
            if f < CORE:
                cores[k][f] = value
            else:
                if k % 2 == 0:
                    rests[k // 2][f - CORE] = value
                else:
                    cores[1][f + (k // 2) * (floats - CORE)] = value


def states_kernel(tiles, cap, steps, *refs):
    parts, (own_ref, moving_ref) = dict(zip(steps, refs)), refs[-2:]
    me = lax.axis_index("tile")
    for k in steps:
        rows = pl.ds(pl.multiple_of(source_tile(me, k, tiles) * cap, cap), cap)
        field = parts[k]
        for f in range(CORE):
            own_ref[f, rows, :] = field[f]
        mass = field[6]
        present = mass > 0
        for f in range(3):
            moving_ref[f, rows, :] = field[f] - CENTRE
        moving_ref[3, rows, :] = jnp.where(present, field[8], 1.0)
        scaled = jnp.where(present, mass * MASS_UNIT, 1.0)
        root = jnp.exp(jnp.log(scaled) * (-1.0 / 3.0))
        for _ in range(2):
            root = root * (4.0 - scaled * (root * root * root)) * (1.0 / 3.0)
        moving_ref[4, rows, :] = jnp.where(present, root, 0.0)
        for f in range(EARLY):
            moving_ref[5 + f, rows, :] = field[3 + f]


def near_states_kernel(tiles, cap, floats, *refs):
    nearest, rests, refs = refs[0], refs[1 : 1 + tiles // 2], refs[1 + tiles // 2 :]
    bundles, (own_ref, moving_ref) = refs[-2 - tiles // 2 : -2], refs[-2:]
    states_kernel(tiles, cap, [1], nearest, own_ref, moving_ref)
    extra = floats - CORE
    for q in range(tiles // 2):
        bundles[q][0:extra] = rests[q][...]
        bundles[q][extra : 2 * extra] = nearest[CORE + q * extra : CORE + (q + 1) * extra]


def slot_major(rows):
    slots, lanes = rows[0].shape
    return jnp.swapaxes(jnp.stack(rows, axis=0), 0, 1).reshape(slots * len(rows), lanes)


def store_far(far_ref, moving_ref, slots):
    place = [moving_ref[f] for f in range(3)]
    smooth, stretch = moving_ref[3], moving_ref[4]
    present = stretch > 0
    stretch = jnp.where(present, stretch, 1.0)
    square = stretch * stretch
    norm = 0.0
    rows = [None] * DEPTH
    for f in range(3):
        hi, mid, lo = split3(-2.0 * square * place[f])
        norm = norm + place[f] * place[f]
        rows[f : 15 : 3] = [hi, hi, hi, mid, lo]
    rows[15:18] = split3(jnp.where(present, square * norm, AWAY))
    s1, s2, s3 = split3(square)
    rows[18:24] = [s1, s1, s1, s2, s2, s3]
    rows[24:27] = split3(0.25 * stretch * smooth)
    u1, u2 = split2(0.25 * stretch)
    rows[27:32] = [u1, u1, u2, u2, jnp.zeros_like(u1)]
    far_ref[0 : slots * DEPTH, :] = slot_major(rows)


def store_far_dummy(far_ref, index):
    row = lax.broadcasted_iota(I32, (DEPTH, LANES), 0)
    far_ref[index * DEPTH : (index + 1) * DEPTH, :] = jnp.where(row == 15, AWAY, jnp.where(row == 24, 1.0, 0.0))


def store_near(near_ref, moving_ref, slots):
    row = lax.broadcasted_iota(I32, (DEPTH, LANES), 0)
    start = 2 * slots * DEPTH
    near_ref[start : start + DEPTH, :] = jnp.where((row >= 15) & (row < 18), 1.0, 0.0)
    near_ref[start + DEPTH : start + 2 * DEPTH, :] = jnp.where((row >= 24) & (row < 27), 1.0, 0.0)
    place = [moving_ref[f] for f in range(3)]
    zeros, ones = jnp.zeros_like(place[0]), jnp.ones_like(place[0])
    norm = 0.0
    rows = [zeros] * (2 * DEPTH)
    for f in range(3):
        hi, mid, lo = split3(place[f])
        norm = norm + place[f] * place[f]
        rows[f : 15 : 3] = [hi, mid, lo, hi, hi]
    rows[15:18] = [ones] * 3
    n1, n2, n3 = split3(norm)
    rows[18:24] = [n1, n2, n3, n1, n2, n1]
    h1, h2 = split2(moving_ref[3])
    rows[DEPTH + 24 : DEPTH + 31] = [ones] * 3 + [h1, h2, h1, h2]
    near_ref[0:start, :] = slot_major(rows)


def pair_loop(plan, plan_ref, which, groups, near_ref, far_ref, weight_ref, slope_ref):
    base = which * plan.length
    stored = plan.stored_base(plan_ref, which)

    def work(start, size):
        for u in range(size):
            word = plan_ref[base + start + u]
            far = far_ref[pl.ds(pl.multiple_of(plan.cand(word) * DEPTH, DEPTH), DEPTH), :]
            near = near_ref[pl.ds(pl.multiple_of(plan.slot(word) * (2 * DEPTH), DEPTH), 2 * DEPTH), :]
            near = jnp.concatenate([near[0:DEPTH], near[DEPTH : 2 * DEPTH]], axis=1)
            both = lax.dot_general(
                far.astype(BF16), near.astype(BF16), (((0,), (0,)), ((), ())), preferred_element_type=F32
            )
            squared = jnp.maximum(both[:, 0:LANES], 1e-20)
            inverse = pltpu.reciprocal(both[:, LANES : 2 * LANES], approx=True)
            remain = jnp.maximum(4.0 - squared * lax.rsqrt(squared) * inverse, 0.0)
            scaled = inverse * remain
            cubed = scaled * scaled * scaled
            if weight_ref is not None:
                weight = cubed * (remain * (5.0 - remain))
                weight_ref[plan.code(word)] = jnp.sum(weight.reshape(LANES // 8, 8, LANES), axis=0)
            if slope_ref is not None:
                slope_ref[stored + start + u] = cubed * (inverse * inverse)

    in_groups(plan, plan_ref, which, groups, work)


def local_kernel(plan, plan_ref, moving_ref, weight_in_ref, near_ref, weight_ref, slope_ref, far_ref):
    slots = plan.slots
    store_near(near_ref, moving_ref, slots)
    store_far(far_ref, moving_ref, slots)
    store_far_dummy(far_ref, slots)
    pair_loop(plan, plan_ref, 0, LARGE_GROUPS, near_ref, far_ref, weight_ref, slope_ref)


def first_kernel(plan, plan_ref, moving_ref, near_ref, weight_in_ref, slope_in_ref, weight_ref, slope_ref, far_ref):
    store_far(far_ref, moving_ref, plan.slots)
    store_far_dummy(far_ref, plan.slots)
    pair_loop(plan, plan_ref, 1, GROUPS, near_ref, far_ref, weight_ref, slope_ref)


def second_kernel(plan, plan_ref, own_ref, moving_ref, near_ref, weight_in_ref,
                  density_ref, thermal_ref, weight_ref, far_ref):
    store_far(far_ref, moving_ref, plan.slots)
    store_far_dummy(far_ref, plan.slots)
    pair_loop(plan, plan_ref, 2, GROUPS, near_ref, far_ref, weight_ref, None)
    for i in range(plan.slots):
        first = i << plan.entry_bits
        tile = weight_ref[first]
        for k in range(1, plan.width):
            tile = tile + weight_ref[first + k]
        density_ref[i : i + 1, :] = sum_rows(tile)[0:1, :]
    density = WEIGHT_FACTOR * density_ref[...]
    density_ref[...] = density
    safe = jnp.where(own_ref[6] > 0, density, 1.0)
    thermal_ref[0] = (ADIABATIC - 1.0) * density * own_ref[7] / (safe * safe)
    for f in range(EARLY, 3):
        thermal_ref[1 + f - EARLY] = own_ref[3 + f]


def slope_kernel(plan, plan_ref, moving_ref, near_ref, thermal_ref, slope_in_ref, slope_ref, far_ref):
    store_far(far_ref, moving_ref, plan.slots)
    store_far_dummy(far_ref, plan.slots)
    pair_loop(plan, plan_ref, 2, GROUPS, near_ref, far_ref, None, slope_ref)


def store_fields(field_ref, moving_ref, thermal_ref, slots):
    def put(row, value):
        field_ref[pl.ds(row, slots, stride=FIELD_ROWS), :] = value

    stretch = moving_ref[4]
    square = stretch * stretch
    place = [moving_ref[f] for f in range(3)]
    speed = [moving_ref[5 + f] if f < EARLY else thermal_ref[1 + f - EARLY] for f in range(3)]
    dotted = place[0] * speed[0] + place[1] * speed[1] + place[2] * speed[2]
    plain = [square] + [square * value for value in place + speed + [dotted]]
    heavy = [thermal_ref[0] * value for value in plain[0:4]]
    for row, value in enumerate(plain):
        for part, piece in enumerate(split3(value)):
            put(8 * part + row, piece)
    for row, value in enumerate(heavy):
        for part, piece in enumerate(split3(value)):
            put(24 + 4 * part + row, piece)
        put(36 + row, jnp.zeros_like(value))


def store_field_dummy(field_ref, index):
    field_ref[index * FIELD_ROWS : (index + 1) * FIELD_ROWS, :] = jnp.zeros((FIELD_ROWS, LANES), F32)


def field_loop(plan, plan_ref, which, field_ref, slope_ref, sum_ref):
    base = which * plan.length
    stored = plan.stored_base(plan_ref, which)

    def work(start, size):
        for u in range(size):
            word = plan_ref[base + start + u]
            field = field_ref[pl.ds(pl.multiple_of(plan.cand(word) * FIELD_ROWS, 8), FIELD_ROWS), :].astype(BF16)
            slope = slope_ref[stored + start + u]
            hi = slope.astype(BF16)
            lo = (slope - hi.astype(F32)).astype(BF16)
            both = jnp.dot(
                jnp.concatenate([field, field], axis=1),
                jnp.concatenate([hi, lo], axis=0),
                preferred_element_type=F32,
            )
            code = plan.code(word)
            sum_ref[code, 0:8, :] = both[0:8] + both[8:16] + both[16:24]
            sum_ref[code, 8:16, :] = both[24:32] + both[32:40]

    in_groups(plan, plan_ref, which, GROUPS, work)


def local_field_kernel(plan, plan_ref, moving_ref, thermal_ref, slope_ref, sum_ref, field_ref):
    store_fields(field_ref, moving_ref, thermal_ref, plan.slots)
    store_field_dummy(field_ref, plan.slots)
    sum_ref[...] = jnp.zeros_like(sum_ref)
    field_loop(plan, plan_ref, 0, field_ref, slope_ref, sum_ref)


def first_field_kernel(plan, plan_ref, moving_ref, thermal_ref, slope_ref, sum_in_ref, sum_ref, field_ref):
    store_fields(field_ref, moving_ref, thermal_ref, plan.slots)
    store_field_dummy(field_ref, plan.slots)
    field_loop(plan, plan_ref, 1, field_ref, slope_ref, sum_ref)


def final_kernel(plan, tiles, cap, floats, plan_ref, own_ref, moving_ref, second_ref, density_ref, thermal_ref,
                 second_thermal_ref, slope_ref, sum_in_ref, *refs):
    bundles, (updated_ref, derived_ref, sum_ref, field_ref, total_ref) = refs[: tiles // 2], refs[tiles // 2 :]
    slots = plan.slots
    store_fields(field_ref, second_ref, second_thermal_ref, slots)
    store_field_dummy(field_ref, slots)
    me = lax.axis_index("tile")
    for k in range(tiles):
        base = pl.multiple_of(source_tile(me, k, tiles) * cap, cap)
        held = (own_ref[6, pl.ds(base, cap), :] > 0).astype(F32)
        for f in range(floats - CORE):
            value = bundles[k // 2][(k % 2) * (floats - CORE) + f]
            updated_ref[pl.ds(base * floats + CORE + f, cap, stride=floats), :] = value * held
    field_loop(plan, plan_ref, 2, field_ref, slope_ref, sum_ref)
    for i in range(slots):
        first = i << plan.entry_bits
        tile = sum_ref[first]
        for k in range(1, plan.width):
            tile = tile + sum_ref[first + k]
        total_ref[16 * i : 16 * (i + 1), :] = tile

    def summed(row):
        return SLOPE_FACTOR * total_ref[pl.ds(row, slots, stride=16), :]

    plain = [summed(row) for row in range(8)]
    heavy = [summed(8 + row) + summed(12 + row) for row in range(4)]
    place = [moving_ref[f] for f in range(3)]
    speed = [own_ref[3 + f] for f in range(3)]
    ratio, density = thermal_ref[0], density_ref[...]
    accel, heating = [], plain[7]
    for f in range(3):
        spread = place[f] * plain[0] - plain[1 + f]
        accel.append(-(ratio * spread + (place[f] * heavy[0] - heavy[1 + f])))
        heating = heating + place[f] * (speed[f] * plain[0] - plain[4 + f]) - speed[f] * plain[1 + f]
    heating = ratio * heating
    present = (own_ref[6] > 0).astype(F32)
    fresh = {}
    for f in range(3):
        fresh[3 + f] = speed[f] + TIMESTEP * accel[f]
        fresh[f] = own_ref[f] + TIMESTEP * fresh[3 + f]
    fresh[6] = own_ref[6]
    fresh[7] = own_ref[7] + TIMESTEP * heating
    fresh[8] = own_ref[8]
    for f in range(CORE):
        updated_ref[pl.ds(f, slots, stride=floats), :] = fresh[f] * present
    for f, value in enumerate([density] + accel + [heating]):
        derived_ref[f] = value * present


def body(tiles, slabs, particles, dest_slot, neighbours, counts):
    bins, floats, lanes = particles.shape
    slots, width = neighbours.shape
    cap = slots // tiles
    plan = Plan(slots, width)
    half, extra = tiles // 2, floats - CORE
    packed = kernel_call(
        lambda *refs: pack_kernel(tiles, cap, floats, *refs),
        [("h", in_hbm(dest_slot)), ("h", in_hbm(particles))],
        [("v", (CORE + (extra * half if k == 1 else 0), cap, lanes), F32) for k in range(tiles)]
        + [("v", (extra, cap, lanes), F32)] * half,
        [
            pltpu.VMEM((slots * floats, lanes), F32),
            pltpu.VMEM((bins, floats, lanes), F32),
            pltpu.SMEM((bins,), I32),
            pltpu.SemaphoreType.DMA((9 if bins % 8 == 0 else 2,)),
        ],
        1500,
        "pack",
    )
    packed, rests = packed[:tiles], packed[tiles:]

    def to_partner(array, step):
        return lax.ppermute(array, "tile", [(t, partner_tile(t, step, tiles)) for t in range(tiles)])

    near_out = ("v", ((slots + 1) * 2 * DEPTH, lanes), F32)
    weight_out = ("v", (plan.codes, 8, lanes), F32)
    lists, weights = kernel_call(
        lambda *refs: plan_kernel(plan, *refs),
        [("s", in_hbm(neighbours.T)), ("s", in_hbm(counts)), ("a", packed[0])],
        [("s", (plan.size,), I32), weight_out],
        [],
        2000,
        "plan",
    )
    parts = [packed[0]] + [to_partner(packed[k], k) for k in range(1, tiles)]
    state_outs = [("v", (CORE, slots, lanes), F32), ("v", (5 + EARLY, slots, lanes), F32)]
    far_steps = [k for k in range(tiles) if k != 1]
    own, moving = kernel_call(
        lambda *refs: states_kernel(tiles, cap, far_steps, *refs),
        [("v", parts[k]) for k in far_steps],
        state_outs,
        [],
        200,
        "far_states",
    )
    *bundles, own, moving = kernel_call(
        lambda *refs: near_states_kernel(tiles, cap, floats, *refs),
        [("v", parts[1])] + [("v", rest) for rest in rests] + [("v", own), ("v", moving), ("a", lists)],
        [("v", (2 * extra, cap, lanes), F32)] * half + state_outs,
        [],
        100,
        "near_states",
        {1 + half: half, 2 + half: half + 1},
    )
    first_pairs = [(s, s ^ 1) for s in range(slabs)]
    second_pairs = [(s, (((s + 1) ^ 1) - 1) % slabs) for s in range(slabs)]

    def both_sides(array):
        second = lax.ppermute(array, "slab", second_pairs)
        first = lax.ppermute(array, "slab", first_pairs)
        return first, second

    first, second = both_sides(moving)
    slope_out = ("v", (plan.stored, lanes, lanes), F32)
    sum_out = ("v", (plan.codes, 16, lanes), F32)
    far_table = [pltpu.VMEM(((slots + 1) * DEPTH, lanes), F32)]
    field_table = [pltpu.VMEM(((slots + 1) * FIELD_ROWS, lanes), F32)]
    near, weights, slopes = kernel_call(
        lambda *refs: local_kernel(plan, *refs),
        [("s", lists), ("v", moving), ("v", weights)],
        [near_out, weight_out, slope_out],
        far_table,
        3500,
        "local",
        {2: 1},
    )
    weights, slopes = kernel_call(
        lambda *refs: first_kernel(plan, *refs),
        [("s", lists), ("v", first), ("v", near), ("v", weights), ("v", slopes)],
        [weight_out, slope_out],
        far_table,
        1500,
        "first",
        {3: 0, 4: 1},
    )
    density, thermal, weights = kernel_call(
        lambda *refs: second_kernel(plan, *refs),
        [("s", lists), ("v", own), ("v", second), ("v", near), ("v", weights)],
        [("v", (slots, lanes), F32), ("v", (4 - EARLY, slots, lanes), F32), weight_out],
        far_table,
        2000,
        "second",
        {4: 2},
    )
    first_thermal, second_thermal = both_sides(thermal)
    (sums,) = kernel_call(
        lambda *refs: local_field_kernel(plan, *refs),
        [("s", lists), ("v", moving), ("v", thermal), ("v", slopes)],
        [sum_out],
        field_table,
        1700,
        "local_fields",
    )
    bundles = [bundles[0]] + [to_partner(bundles[q], 2 * q) for q in range(1, half)]
    (slopes,) = kernel_call(
        lambda *refs: slope_kernel(plan, *refs),
        [("s", lists), ("v", second), ("v", near), ("a", thermal), ("v", slopes)],
        [slope_out],
        far_table,
        1300,
        "slopes",
        {4: 0},
    )
    (sums,) = kernel_call(
        lambda *refs: first_field_kernel(plan, *refs),
        [("s", lists), ("v", first), ("v", first_thermal), ("v", slopes), ("v", sums)],
        [sum_out],
        field_table,
        1000,
        "first_fields",
        {4: 0},
    )
    updated, derived, _ = kernel_call(
        lambda *refs: final_kernel(plan, tiles, cap, floats, *refs),
        [("s", lists), ("v", own), ("v", moving), ("v", second), ("v", density), ("v", thermal),
         ("v", second_thermal), ("v", slopes), ("v", sums)]
        + [("v", bundle) for bundle in bundles],
        [("v", (slots * floats, lanes), F32), ("v", (5, slots, lanes), F32), sum_out],
        field_table + [pltpu.VMEM((slots * 16, lanes), F32)],
        2000,
        "final",
        {8: 2},
    )
    return updated.reshape(slots, floats, lanes), derived.transpose(1, 0, 2)


def solution(mesh):
    tiles, slabs = mesh.shape["tile"], mesh.shape["slab"]
    in_specs = (
        P(("slab", "tile"), None, None),
        P(("slab", "tile")),
        P(("slab", "tile"), None),
        P(("slab", "tile")),
    )
    out_specs = (P(("slab", "tile"), None, None), P(("slab", "tile"), None, None))
    return jax.shard_map(
        lambda *args: body(tiles, slabs, *args), mesh=mesh, in_specs=in_specs, out_specs=out_specs, check_vma=False
    )
```

```python
import math

import jax
import jax.numpy as jnp
from jax import lax
from jax.experimental import pallas as pl
from jax.experimental.pallas import tpu as pltpu
from jax.sharding import PartitionSpec as P

ADIABATIC = 5.0 / 3.0
TIMESTEP = 0.5
KERNEL_NORM = 21.0 / (16.0 * math.pi)
MASS_UNIT = 512.0
WEIGHT_FACTOR = 8.0 * KERNEL_NORM / MASS_UNIT / 4.0**7
SLOPE_FACTOR = -5.0 * 32.0 * KERNEL_NORM / MASS_UNIT / 4.0**8
CENTRE = 1.0
AWAY = 1.0e4
LANES = 128
LARGE_GROUPS = (((48, 40), (24, 16)), (16, 8))
GROUPS = (((24, 16),), (16, 8))
WEIGHT_GROUPS = (((28, 24), (24, 16)), (16, 8))
STEP = 8
EARLY = 0
CORE = 9
DEPTH = 32
FIELD_ROWS = 40

F32 = jnp.float32
BF16 = jnp.bfloat16
I32 = jnp.int32


def vmem_spec():
    return pl.BlockSpec(memory_space=pltpu.VMEM)


def smem_spec():
    return pl.BlockSpec(memory_space=pltpu.SMEM)


def hbm_spec():
    return pl.BlockSpec(memory_space=pltpu.HBM)


def any_spec():
    return pl.BlockSpec(memory_space=pl.ANY)


SPECS = {"s": smem_spec, "v": vmem_spec, "h": hbm_spec, "a": any_spec}


def in_hbm(array):
    return pltpu.with_memory_space_constraint(array, pltpu.HBM)


def kernel_call(kernel, ins, outs, scratch, nanoseconds, name, aliases=None):
    return pl.pallas_call(
        kernel,
        out_shape=[
            pltpu.SMEM(shape, dtype) if memory == "s" else jax.ShapeDtypeStruct(shape, dtype)
            for memory, shape, dtype in outs
        ],
        in_specs=[SPECS[memory]() for memory, _ in ins],
        out_specs=[SPECS[memory]() for memory, _, _ in outs],
        scratch_shapes=scratch,
        input_output_aliases=aliases or {},
        compiler_params=pltpu.CompilerParams(vmem_limit_bytes=32 * 1024 * 1024),
        cost_estimate=pl.CostEstimate(flops=0, bytes_accessed=3000 * nanoseconds, transcendentals=0),
        name=name,
    )(*[array for _, array in ins])


def is_power(count):
    return count & (count - 1) == 0


def partner_tile(index, step, count):
    return index ^ step if is_power(count) else (index + step) % count


def source_tile(index, step, count):
    return index ^ step if is_power(count) else lax.rem(index + count - step, count)


def rounded(value):
    return value.astype(BF16).astype(F32)


def split2(value):
    hi = rounded(value)
    return hi, rounded(value - hi)


def split3(value):
    hi = rounded(value)
    mid = rounded(value - hi)
    return hi, mid, rounded(value - hi - mid)


def sum_rows(tile):
    tile = tile + pltpu.roll(tile, 4, 0)
    tile = tile + pltpu.roll(tile, 2, 0)
    return tile + pltpu.roll(tile, 1, 0)


class Plan:
    def __init__(self, slots, width):
        self.slots, self.width = slots, width
        self.entry_bits = (width - 1).bit_length()
        self.cand_bits = slots.bit_length()
        self.length = slots * width + STEP
        self.codes = (slots + 1) << self.entry_bits
        self.counts = 3 * self.length
        self.size = 3 * self.length + 8
        self.stored = slots * width + 4 * STEP
        self.dummy = self.word(slots, 0, slots)

    def word(self, slot, entry, cand):
        return (((slot << self.entry_bits) + entry) << self.cand_bits) + cand

    def code(self, word):
        return word >> self.cand_bits

    def slot(self, word):
        return word >> (self.cand_bits + self.entry_bits)

    def cand(self, word):
        return word & ((1 << self.cand_bits) - 1)

    def stored_base(self, ref, which):
        base = 0
        for k in range(which):
            base = base + lax.div(ref[self.counts + k] + STEP - 1, STEP) * STEP
        return base


def in_groups(plan, plan_ref, which, groups, work):
    loops, tails = groups
    start, count = 0, plan_ref[plan.counts + which]
    for size, left in loops:

        def step(g, first, size=size):
            work(first, size)
            return first + size

        number = lax.div(jnp.maximum(count - start - left + size - 1, 0), size)
        start = lax.fori_loop(0, number, step, start)
    rest = count - start
    for size, below in zip(tails, tails[1:] + (0,)):

        @pl.when((rest <= size) & (rest > below))
        def _(size=size):
            work(start, size)


def plan_kernel(plan, neighbours_ref, counts_ref, after_ref, plan_ref, weight_ref):
    slots = plan.slots
    entries = 1 << plan.entry_bits
    upper_first = lax.rem(lax.axis_index("slab"), 2) == 0
    low = jnp.where(upper_first, 2, 1)
    high = 3 - low

    def fill(i, totals):
        used = counts_ref[i]
        for k in range(plan.width):
            n = neighbours_ref[k, i]
            region = lax.div(n, slots)
            which = jnp.where(region == 1, 0, jnp.where(region == 0, low, high))
            word = plan.word(i, k, n - region * slots)
            kept = []
            for w in range(3):
                plan_ref[w * plan.length + totals[w]] = word
                kept.append(totals[w] + ((k < used) & (which == w)).astype(I32))
            totals = tuple(kept)
        weight_ref[pl.ds(i * entries, entries)] = jnp.zeros((entries, 8, LANES), F32)
        return totals

    totals = lax.fori_loop(0, slots, fill, (jnp.int32(0),) * 3, unroll=4)
    for w in range(3):
        for k in range(STEP):
            plan_ref[w * plan.length + totals[w] + k] = plan.dummy
        plan_ref[plan.counts + w] = totals[w]


def pack_kernel(tiles, cap, floats, dest_ref, particles_ref, *refs):
    cores, rests, (packed, staged, dest, sems) = refs[:tiles], refs[tiles:-4], refs[-4:]
    pieces = sems.shape[0] - 1
    bins = staged.shape[0] // pieces
    bring = [pltpu.make_async_copy(dest_ref, dest, sems.at[pieces])]
    for p in range(pieces):
        part = pl.ds(p * bins, bins)
        bring.append(pltpu.make_async_copy(particles_ref.at[part], staged.at[part], sems.at[p]))
    for copy in bring:
        copy.start()
    packed[...] = jnp.zeros_like(packed)
    me = lax.axis_index("tile")
    for copy in bring:
        copy.wait()

    def place(b, carry):
        target = dest[b]
        owner = lax.div(target, cap)
        step = owner ^ me if is_power(tiles) else lax.rem(owner + tiles - me, tiles)
        start = pl.multiple_of((step * cap + lax.rem(target, cap)) * floats, 8)
        packed[pl.ds(start, floats), :] = staged[b]
        return carry

    lax.fori_loop(0, staged.shape[0], place, 0, unroll=4)
    for k in range(tiles):
        for f in range(floats):
            value = packed[pl.ds(k * cap * floats + f, cap, stride=floats), :]
            if f < CORE:
                cores[k][f] = value
            else:
                if k % 2 == 0:
                    rests[k // 2][f - CORE] = value
                else:
                    cores[1][f + (k // 2) * (floats - CORE)] = value


def states_kernel(tiles, cap, steps, *refs):
    parts, (own_ref, moving_ref) = dict(zip(steps, refs)), refs[-2:]
    me = lax.axis_index("tile")
    for k in steps:
        rows = pl.ds(pl.multiple_of(source_tile(me, k, tiles) * cap, cap), cap)
        field = parts[k]
        for f in range(CORE):
            own_ref[f, rows, :] = field[f]
        mass = field[6]
        present = mass > 0
        for f in range(3):
            moving_ref[f, rows, :] = field[f] - CENTRE
        moving_ref[3, rows, :] = jnp.where(present, field[8], 1.0)
        scaled = jnp.where(present, mass * MASS_UNIT, 1.0)
        root = jnp.exp(jnp.log(scaled) * (-1.0 / 3.0))
        for _ in range(2):
            root = root * (4.0 - scaled * (root * root * root)) * (1.0 / 3.0)
        moving_ref[4, rows, :] = jnp.where(present, root, 0.0)
        for f in range(EARLY):
            moving_ref[5 + f, rows, :] = field[3 + f]


def near_states_kernel(tiles, cap, floats, *refs):
    nearest, rests, refs = refs[0], refs[1 : 1 + tiles // 2], refs[1 + tiles // 2 :]
    bundles, (own_ref, moving_ref) = refs[-2 - tiles // 2 : -2], refs[-2:]
    states_kernel(tiles, cap, [1], nearest, own_ref, moving_ref)
    extra = floats - CORE
    for q in range(tiles // 2):
        bundles[q][0:extra] = rests[q][...]
        bundles[q][extra : 2 * extra] = nearest[CORE + q * extra : CORE + (q + 1) * extra]


def slot_major(rows):
    slots, lanes = rows[0].shape
    return jnp.swapaxes(jnp.stack(rows, axis=0), 0, 1).reshape(slots * len(rows), lanes)


def store_far(far_ref, moving_ref, slots):
    place = [moving_ref[f] for f in range(3)]
    smooth, stretch = moving_ref[3], moving_ref[4]
    present = stretch > 0
    stretch = jnp.where(present, stretch, 1.0)
    square = stretch * stretch
    norm = 0.0
    rows = [None] * DEPTH
    for f in range(3):
        hi, mid, lo = split3(-2.0 * square * place[f])
        norm = norm + place[f] * place[f]
        rows[f : 15 : 3] = [hi, hi, hi, mid, lo]
    rows[15:18] = split3(jnp.where(present, square * norm, AWAY))
    s1, s2, s3 = split3(square)
    rows[18:24] = [s1, s1, s1, s2, s2, s3]
    rows[24:27] = split3(0.25 * stretch * smooth)
    u1, u2 = split2(0.25 * stretch)
    rows[27:32] = [u1, u1, u2, u2, jnp.zeros_like(u1)]
    far_ref[0 : slots * DEPTH, :] = slot_major(rows)


def store_far_dummy(far_ref, index):
    row = lax.broadcasted_iota(I32, (DEPTH, LANES), 0)
    far_ref[index * DEPTH : (index + 1) * DEPTH, :] = jnp.where(row == 15, AWAY, jnp.where(row == 24, 1.0, 0.0))


def store_near(near_ref, moving_ref, slots):
    row = lax.broadcasted_iota(I32, (DEPTH, LANES), 0)
    start = 2 * slots * DEPTH
    near_ref[start : start + DEPTH, :] = jnp.where((row >= 15) & (row < 18), 1.0, 0.0)
    near_ref[start + DEPTH : start + 2 * DEPTH, :] = jnp.where((row >= 24) & (row < 27), 1.0, 0.0)
    place = [moving_ref[f] for f in range(3)]
    zeros, ones = jnp.zeros_like(place[0]), jnp.ones_like(place[0])
    norm = 0.0
    rows = [zeros] * (2 * DEPTH)
    for f in range(3):
        hi, mid, lo = split3(place[f])
        norm = norm + place[f] * place[f]
        rows[f : 15 : 3] = [hi, mid, lo, hi, hi]
    rows[15:18] = [ones] * 3
    n1, n2, n3 = split3(norm)
    rows[18:24] = [n1, n2, n3, n1, n2, n1]
    h1, h2 = split2(moving_ref[3])
    rows[DEPTH + 24 : DEPTH + 31] = [ones] * 3 + [h1, h2, h1, h2]
    near_ref[0:start, :] = slot_major(rows)


def pair_loop(plan, plan_ref, which, groups, near_ref, far_ref, weight_ref, slope_ref):
    base = which * plan.length
    stored = plan.stored_base(plan_ref, which)

    def work(start, size):
        for u in range(size):
            word = plan_ref[base + start + u]
            far = far_ref[pl.ds(pl.multiple_of(plan.cand(word) * DEPTH, DEPTH), DEPTH), :]
            near = near_ref[pl.ds(pl.multiple_of(plan.slot(word) * (2 * DEPTH), DEPTH), 2 * DEPTH), :]
            near = jnp.concatenate([near[0:DEPTH], near[DEPTH : 2 * DEPTH]], axis=1)
            both = lax.dot_general(
                far.astype(BF16), near.astype(BF16), (((0,), (0,)), ((), ())), preferred_element_type=F32
            )
            squared = jnp.maximum(both[:, 0:LANES], 1e-20)
            inverse = pltpu.reciprocal(both[:, LANES : 2 * LANES], approx=True)
            remain = jnp.maximum(4.0 - squared * lax.rsqrt(squared) * inverse, 0.0)
            scaled = inverse * remain
            cubed = scaled * scaled * scaled
            if weight_ref is not None:
                weight = cubed * (remain * (5.0 - remain))
                weight_ref[plan.code(word)] = jnp.sum(weight.reshape(LANES // 8, 8, LANES), axis=0)
            if slope_ref is not None:
                slope_ref[stored + start + u] = cubed * (inverse * inverse)

    in_groups(plan, plan_ref, which, groups, work)


def local_kernel(plan, plan_ref, moving_ref, weight_in_ref, near_ref, weight_ref, slope_ref, far_ref):
    slots = plan.slots
    store_near(near_ref, moving_ref, slots)
    store_far(far_ref, moving_ref, slots)
    store_far_dummy(far_ref, slots)
    pair_loop(plan, plan_ref, 0, LARGE_GROUPS, near_ref, far_ref, weight_ref, slope_ref)


def first_kernel(plan, plan_ref, moving_ref, near_ref, weight_in_ref, slope_in_ref, weight_ref, slope_ref, far_ref):
    store_far(far_ref, moving_ref, plan.slots)
    store_far_dummy(far_ref, plan.slots)
    pair_loop(plan, plan_ref, 1, GROUPS, near_ref, far_ref, weight_ref, slope_ref)


def second_kernel(plan, plan_ref, own_ref, moving_ref, near_ref, weight_in_ref,
                  density_ref, thermal_ref, weight_ref, far_ref):
    store_far(far_ref, moving_ref, plan.slots)
    store_far_dummy(far_ref, plan.slots)
    pair_loop(plan, plan_ref, 2, WEIGHT_GROUPS, near_ref, far_ref, weight_ref, None)
    for i in range(plan.slots):
        first = i << plan.entry_bits
        tile = weight_ref[first]
        for k in range(1, plan.width):
            tile = tile + weight_ref[first + k]
        density_ref[i : i + 1, :] = sum_rows(tile)[0:1, :]
    density = WEIGHT_FACTOR * density_ref[...]
    density_ref[...] = density
    safe = jnp.where(own_ref[6] > 0, density, 1.0)
    thermal_ref[0] = (ADIABATIC - 1.0) * density * own_ref[7] / (safe * safe)
    for f in range(EARLY, 3):
        thermal_ref[1 + f - EARLY] = own_ref[3 + f]


def slope_kernel(plan, plan_ref, moving_ref, near_ref, thermal_ref, slope_in_ref, slope_ref, far_ref):
    store_far(far_ref, moving_ref, plan.slots)
    store_far_dummy(far_ref, plan.slots)
    pair_loop(plan, plan_ref, 2, GROUPS, near_ref, far_ref, None, slope_ref)


def store_fields(field_ref, moving_ref, thermal_ref, slots):
    def put(row, value):
        field_ref[pl.ds(row, slots, stride=FIELD_ROWS), :] = value

    stretch = moving_ref[4]
    square = stretch * stretch
    place = [moving_ref[f] for f in range(3)]
    speed = [moving_ref[5 + f] if f < EARLY else thermal_ref[1 + f - EARLY] for f in range(3)]
    dotted = place[0] * speed[0] + place[1] * speed[1] + place[2] * speed[2]
    plain = [square] + [square * value for value in place + speed + [dotted]]
    heavy = [thermal_ref[0] * value for value in plain[0:4]]
    for row, value in enumerate(plain):
        for part, piece in enumerate(split3(value)):
            put(8 * part + row, piece)
    for row, value in enumerate(heavy):
        for part, piece in enumerate(split3(value)):
            put(24 + 4 * part + row, piece)
        put(36 + row, jnp.zeros_like(value))


def store_field_dummy(field_ref, index):
    field_ref[index * FIELD_ROWS : (index + 1) * FIELD_ROWS, :] = jnp.zeros((FIELD_ROWS, LANES), F32)


def field_loop(plan, plan_ref, which, field_ref, slope_ref, sum_ref):
    base = which * plan.length
    stored = plan.stored_base(plan_ref, which)

    def work(start, size):
        for u in range(size):
            word = plan_ref[base + start + u]
            field = field_ref[pl.ds(pl.multiple_of(plan.cand(word) * FIELD_ROWS, 8), FIELD_ROWS), :].astype(BF16)
            slope = slope_ref[stored + start + u]
            hi = slope.astype(BF16)
            lo = (slope - hi.astype(F32)).astype(BF16)
            both = jnp.dot(
                jnp.concatenate([field, field], axis=1),
                jnp.concatenate([hi, lo], axis=0),
                preferred_element_type=F32,
            )
            code = plan.code(word)
            sum_ref[code, 0:8, :] = both[0:8] + both[8:16] + both[16:24]
            sum_ref[code, 8:16, :] = both[24:32] + both[32:40]

    in_groups(plan, plan_ref, which, GROUPS, work)


def local_field_kernel(plan, plan_ref, moving_ref, thermal_ref, slope_ref, sum_ref, field_ref):
    store_fields(field_ref, moving_ref, thermal_ref, plan.slots)
    store_field_dummy(field_ref, plan.slots)
    sum_ref[...] = jnp.zeros_like(sum_ref)
    field_loop(plan, plan_ref, 0, field_ref, slope_ref, sum_ref)


def first_field_kernel(plan, plan_ref, moving_ref, thermal_ref, slope_ref, sum_in_ref, sum_ref, field_ref):
    store_fields(field_ref, moving_ref, thermal_ref, plan.slots)
    store_field_dummy(field_ref, plan.slots)
    field_loop(plan, plan_ref, 1, field_ref, slope_ref, sum_ref)


def final_kernel(plan, tiles, cap, floats, plan_ref, own_ref, moving_ref, second_ref, density_ref, thermal_ref,
                 second_thermal_ref, slope_ref, sum_in_ref, *refs):
    bundles, (updated_ref, derived_ref, sum_ref, field_ref, total_ref) = refs[: tiles // 2], refs[tiles // 2 :]
    slots = plan.slots
    store_fields(field_ref, second_ref, second_thermal_ref, slots)
    store_field_dummy(field_ref, slots)
    me = lax.axis_index("tile")
    for k in range(tiles):
        base = pl.multiple_of(source_tile(me, k, tiles) * cap, cap)
        held = (own_ref[6, pl.ds(base, cap), :] > 0).astype(F32)
        for f in range(floats - CORE):
            value = bundles[k // 2][(k % 2) * (floats - CORE) + f]
            updated_ref[pl.ds(base * floats + CORE + f, cap, stride=floats), :] = value * held
    field_loop(plan, plan_ref, 2, field_ref, slope_ref, sum_ref)
    for i in range(slots):
        first = i << plan.entry_bits
        tile = sum_ref[first]
        for k in range(1, plan.width):
            tile = tile + sum_ref[first + k]
        total_ref[16 * i : 16 * (i + 1), :] = tile

    def summed(row):
        return SLOPE_FACTOR * total_ref[pl.ds(row, slots, stride=16), :]

    plain = [summed(row) for row in range(8)]
    heavy = [summed(8 + row) + summed(12 + row) for row in range(4)]
    place = [moving_ref[f] for f in range(3)]
    speed = [own_ref[3 + f] for f in range(3)]
    ratio, density = thermal_ref[0], density_ref[...]
    accel, heating = [], plain[7]
    for f in range(3):
        spread = place[f] * plain[0] - plain[1 + f]
        accel.append(-(ratio * spread + (place[f] * heavy[0] - heavy[1 + f])))
        heating = heating + place[f] * (speed[f] * plain[0] - plain[4 + f]) - speed[f] * plain[1 + f]
    heating = ratio * heating
    present = (own_ref[6] > 0).astype(F32)
    fresh = {}
    for f in range(3):
        fresh[3 + f] = speed[f] + TIMESTEP * accel[f]
        fresh[f] = own_ref[f] + TIMESTEP * fresh[3 + f]
    fresh[6] = own_ref[6]
    fresh[7] = own_ref[7] + TIMESTEP * heating
    fresh[8] = own_ref[8]
    for f in range(CORE):
        updated_ref[pl.ds(f, slots, stride=floats), :] = fresh[f] * present
    for f, value in enumerate([density] + accel + [heating]):
        derived_ref[f] = value * present


def body(tiles, slabs, particles, dest_slot, neighbours, counts):
    bins, floats, lanes = particles.shape
    slots, width = neighbours.shape
    cap = slots // tiles
    plan = Plan(slots, width)
    half, extra = tiles // 2, floats - CORE
    packed = kernel_call(
        lambda *refs: pack_kernel(tiles, cap, floats, *refs),
        [("h", in_hbm(dest_slot)), ("h", in_hbm(particles))],
        [("v", (CORE + (extra * half if k == 1 else 0), cap, lanes), F32) for k in range(tiles)]
        + [("v", (extra, cap, lanes), F32)] * half,
        [
            pltpu.VMEM((slots * floats, lanes), F32),
            pltpu.VMEM((bins, floats, lanes), F32),
            pltpu.SMEM((bins,), I32),
            pltpu.SemaphoreType.DMA((9 if bins % 8 == 0 else 2,)),
        ],
        1500,
        "pack",
    )
    packed, rests = packed[:tiles], packed[tiles:]

    def to_partner(array, step):
        return lax.ppermute(array, "tile", [(t, partner_tile(t, step, tiles)) for t in range(tiles)])

    near_out = ("v", ((slots + 1) * 2 * DEPTH, lanes), F32)
    weight_out = ("v", (plan.codes, 8, lanes), F32)
    lists, weights = kernel_call(
        lambda *refs: plan_kernel(plan, *refs),
        [("s", in_hbm(neighbours.T)), ("s", in_hbm(counts)), ("a", packed[0])],
        [("s", (plan.size,), I32), weight_out],
        [],
        2000,
        "plan",
    )
    parts = [packed[0]] + [to_partner(packed[k], k) for k in range(1, tiles)]
    state_outs = [("v", (CORE, slots, lanes), F32), ("v", (5 + EARLY, slots, lanes), F32)]
    far_steps = [k for k in range(tiles) if k != 1]
    own, moving = kernel_call(
        lambda *refs: states_kernel(tiles, cap, far_steps, *refs),
        [("v", parts[k]) for k in far_steps],
        state_outs,
        [],
        200,
        "far_states",
    )
    *bundles, own, moving = kernel_call(
        lambda *refs: near_states_kernel(tiles, cap, floats, *refs),
        [("v", parts[1])] + [("v", rest) for rest in rests] + [("v", own), ("v", moving), ("a", lists)],
        [("v", (2 * extra, cap, lanes), F32)] * half + state_outs,
        [],
        100,
        "near_states",
        {1 + half: half, 2 + half: half + 1},
    )
    first_pairs = [(s, s ^ 1) for s in range(slabs)]
    second_pairs = [(s, (((s + 1) ^ 1) - 1) % slabs) for s in range(slabs)]

    def both_sides(array):
        second = lax.ppermute(array, "slab", second_pairs)
        first = lax.ppermute(array, "slab", first_pairs)
        return first, second

    first, second = both_sides(moving)
    slope_out = ("v", (plan.stored, lanes, lanes), F32)
    sum_out = ("v", (plan.codes, 16, lanes), F32)
    far_table = [pltpu.VMEM(((slots + 1) * DEPTH, lanes), F32)]
    field_table = [pltpu.VMEM(((slots + 1) * FIELD_ROWS, lanes), F32)]
    near, weights, slopes = kernel_call(
        lambda *refs: local_kernel(plan, *refs),
        [("s", lists), ("v", moving), ("v", weights)],
        [near_out, weight_out, slope_out],
        far_table,
        3500,
        "local",
        {2: 1},
    )
    weights, slopes = kernel_call(
        lambda *refs: first_kernel(plan, *refs),
        [("s", lists), ("v", first), ("v", near), ("v", weights), ("v", slopes)],
        [weight_out, slope_out],
        far_table,
        1500,
        "first",
        {3: 0, 4: 1},
    )
    density, thermal, weights = kernel_call(
        lambda *refs: second_kernel(plan, *refs),
        [("s", lists), ("v", own), ("v", second), ("v", near), ("v", weights)],
        [("v", (slots, lanes), F32), ("v", (4 - EARLY, slots, lanes), F32), weight_out],
        far_table,
        2000,
        "second",
        {4: 2},
    )
    first_thermal, second_thermal = both_sides(thermal)
    (sums,) = kernel_call(
        lambda *refs: local_field_kernel(plan, *refs),
        [("s", lists), ("v", moving), ("v", thermal), ("v", slopes)],
        [sum_out],
        field_table,
        1700,
        "local_fields",
    )
    bundles = [bundles[0]] + [to_partner(bundles[q], 2 * q) for q in range(1, half)]
    (slopes,) = kernel_call(
        lambda *refs: slope_kernel(plan, *refs),
        [("s", lists), ("v", second), ("v", near), ("a", thermal), ("v", slopes)],
        [slope_out],
        far_table,
        1300,
        "slopes",
        {4: 0},
    )
    (sums,) = kernel_call(
        lambda *refs: first_field_kernel(plan, *refs),
        [("s", lists), ("v", first), ("v", first_thermal), ("v", slopes), ("v", sums)],
        [sum_out],
        field_table,
        1000,
        "first_fields",
        {4: 0},
    )
    updated, derived, _ = kernel_call(
        lambda *refs: final_kernel(plan, tiles, cap, floats, *refs),
        [("s", lists), ("v", own), ("v", moving), ("v", second), ("v", density), ("v", thermal),
         ("v", second_thermal), ("v", slopes), ("v", sums)]
        + [("v", bundle) for bundle in bundles],
        [("v", (slots * floats, lanes), F32), ("v", (5, slots, lanes), F32), sum_out],
        field_table + [pltpu.VMEM((slots * 16, lanes), F32)],
        2000,
        "final",
        {8: 2},
    )
    return updated.reshape(slots, floats, lanes), derived.transpose(1, 0, 2)


def solution(mesh):
    tiles, slabs = mesh.shape["tile"], mesh.shape["slab"]
    in_specs = (
        P(("slab", "tile"), None, None),
        P(("slab", "tile")),
        P(("slab", "tile"), None),
        P(("slab", "tile")),
    )
    out_specs = (P(("slab", "tile"), None, None), P(("slab", "tile"), None, None))
    return jax.shard_map(
        lambda *args: body(tiles, slabs, *args), mesh=mesh, in_specs=in_specs, out_specs=out_specs, check_vma=False
    )
```
